512 devices in a mesh: gx: 16 (over z), gy: 4 (over x), gz: 8 (over y, core).
Axes of the slice: x: 4, y: 4, z: 16, core: 2. Of those that a mesh axis runs over, the one named last changes fastest.
Arguments:
- species_field: float32 [11, 512, 16, 1024], P(None, 'gx', 'gy', 'gz'), may hold values from -24 to 24
- start_basis: float32 [512, 112], replicated, may hold values from -0.5 to 0.5
Outputs:
- subspace: float32 [512, 112], replicated
- core_field: float32 [112, 11, 16, 1024], P('gx', None, 'gy', 'gz')
The draws below stay inside these ranges and needn't reach their ends.
All inputs are finite; a program needn't handle non-finite values.
Results may differ from the reference program's by a relative error of at most 0.0003.
Values sent between devices are 32-bit elements; how exact they have to be, the bound alone decides.
A program may use at most 64 MiB of HBM per device.

```python
import jax
import jax.numpy as jnp
from jax import lax

S = 11
NX = 512
R = 112
ITERS = 8
NY = 16
NZ = 1024


def draw_species_field(key, part):
    key = jax.random.fold_in(key, 7)
    noise_key, scale_key = jax.random.split(key)
    noise = jax.random.truncated_normal(noise_key, -6.0, 6.0, (S, NX, NY, NZ), jnp.float32)
    top_scale = 4.0
    exponent = jax.random.uniform(scale_key, (S, NX, NY, NZ // 16), jnp.float32, 0.0, 1.0)
    scales = jnp.exp(exponent * jnp.log(top_scale))
    scales = jnp.repeat(scales, 16, axis=3)
    return (noise * scales).astype(jnp.float32)


def centred(own_key, shape, deviation, limit, kind=jnp.bfloat16):
    array = deviation * jax.random.normal(own_key, shape, jnp.float32)
    return jnp.clip(array, min=-limit, max=limit).astype(kind)


def setup_inputs(seed: int = 0) -> dict:
    key_list = jax.random.split(jax.random.key(seed), 3)
    return {
        "species_field": draw_species_field(jax.random.fold_in(key_list[2], 71), 0),
        "start_basis": centred(key_list[1], (NX, R), R ** -0.5, 0.5, jnp.float32),
    }


def reference(species_field, start_basis):
    highest = lax.Precision.HIGHEST
    gram_matrix = jnp.zeros((NX, NX), jnp.float32)
    for species_index in range(S):
        flat_rows = species_field[species_index].reshape(NX, NY * NZ)
        gram_matrix = gram_matrix + jnp.dot(flat_rows, flat_rows.T, precision=highest)
    gram_matrix = gram_matrix / float(S * NY * NZ)
    subspace = start_basis
    for turn_index in range(ITERS):
        image_cols = jnp.dot(gram_matrix, subspace, precision=highest)
        inner = jnp.dot(image_cols.T, image_cols, precision=highest)
        factor = jnp.linalg.cholesky(inner)
        subspace = lax.linalg.triangular_solve(factor, image_cols, left_side=False, lower=True, transpose_a=True)
    core_field = jnp.einsum('ir,sixy->rsxy', subspace, species_field, precision=highest)
    return (subspace, core_field)
```

```python
import functools

import jax
import jax.numpy as jnp
from jax import lax
from jax.experimental import pallas as pl
from jax.experimental.pallas import tpu as pltpu
from jax.sharding import PartitionSpec as P

ITERS = 8
MESH = pl.DeviceIdType.MESH
F32 = jnp.float32
BF16 = jnp.bfloat16

Z = 16
GROUPS = 44
SLOTS = 3
CHIPS = 16


def place():
    z = lax.axis_index("gx")
    x = lax.axis_index("gy")
    w = lax.axis_index("gz")
    core = lax.rem(w, 2)
    return z, x, lax.div(w, 2), core


def first_group(dest, core):
    return 3 * dest - lax.div(dest + 3 - 2 * core, 4)


def short(dest, core):
    return lax.rem(dest, 4) == 2 * core


def partner(me, step):
    half = lax.div(step + 1, 2)
    k = 8 + half * (2 * lax.rem(step, 2) - 1)
    return lax.rem(me + k, Z)


def wait_bytes(ref, sem):
    pltpu.make_async_copy(ref, ref, sem).wait()


def split(v):
    hi = v.astype(BF16)
    return hi, (v - hi.astype(F32)).astype(BF16)


def dot_t(a, b):
    return lax.dot_general(a, b, (((1,), (1,)), ((), ())), preferred_element_type=F32)


def gram_kernel(total, x_ref, xt_out, g_out, send, recv, hi_ref, lo_ref, part, sib, half, spread,
                unit_in, unit, chunk, mine, fin, ssem, rsem, lsem):
    z, x, y, core = place()
    q = x * 4 + y
    barrier = pltpu.get_barrier_semaphore()

    def greet(step, carry):
        pl.semaphore_signal(barrier, inc=1, device_id={"gx": partner(z, step)}, device_id_type=MESH)
        p = lax.rem(q + step + 1, CHIPS)
        pl.semaphore_signal(
            barrier, inc=1, device_id={"gy": lax.div(p, 4), "gz": lax.rem(p, 4) * 2 + core}, device_id_type=MESH
        )
        return carry

    lax.fori_loop(0, 15, greet, 0)
    sibling = {"gz": y * 2 + 1 - core}
    pl.semaphore_signal(barrier, inc=1, device_id=sibling, device_id_type=MESH)

    for g in range(GROUPS):
        s, yy = divmod(g, 4)
        send[g] = x_ref[s, pl.ds(yy, 32, stride=4), :]
    pl.semaphore_wait(barrier, 31)

    rows = pl.ds(pl.multiple_of(z * 32, 32), 32)

    def copy_to(slot, d):
        return pltpu.make_async_remote_copy(
            src_ref=send.at[first_group(d, core) + slot],
            dst_ref=recv.at[slot, rows],
            send_sem=ssem.at[slot],
            recv_sem=rsem.at[slot],
            device_id={"gx": d},
            device_id_type=MESH,
        )

    for slot in range(SLOTS):
        def push(step, carry, slot=slot):
            d = partner(z, step)
            if slot < 2:
                copy_to(slot, d).start()
            else:
                @pl.when(jnp.logical_not(short(d, core)))
                def _():
                    copy_to(slot, d).start()
            return carry

        lax.fori_loop(0, 15, push, 0)
    mine_first = first_group(z, core)
    recv[0, rows] = send[mine_first]
    recv[1, rows] = send[mine_first + 1]
    is_short = short(z, core)

    @pl.when(is_short)
    def _():
        recv[2] = jnp.zeros((512, 128), F32)

    @pl.when(jnp.logical_not(is_short))
    def _():
        recv[2, rows] = send[mine_first + 2]

    others = pl.ds(0, 480)

    def accumulate(lanes, first):
        for i in range(4):
            ri = slice(128 * i, 128 * i + 128)
            up = slice(0, 128 * i + 128)
            hi_i, lo_i = hi_ref[ri, lanes], lo_ref[ri, lanes]
            hi_u = hi_ref[up, lanes]
            block = dot_t(hi_i, hi_u) + dot_t(hi_i, lo_ref[up, lanes]) + dot_t(lo_i, hi_u)
            for j in range(i + 1):
                b = i * (i + 1) // 2 + j
                rb = slice(128 * b, 128 * b + 128)
                piece = block[:, 128 * j:128 * j + 128]
                part[rb] = piece if first else part[rb] + piece

    def take(slot):
        hi, lo = split(recv[slot])
        hi_ref[:, 128 * slot:128 * slot + 128] = hi
        lo_ref[:, 128 * slot:128 * slot + 128] = lo

    wait_bytes(recv.at[0, others], rsem.at[0])
    take(0)
    wait_bytes(recv.at[1, others], rsem.at[1])
    take(1)
    accumulate(slice(0, 256), True)

    @pl.when(jnp.logical_not(is_short))
    def _():
        wait_bytes(recv.at[2, others], rsem.at[2])

    take(2)
    accumulate(slice(256, 384), False)
    keep = pltpu.make_async_copy(recv, xt_out, lsem)
    keep.start()

    own_half = pl.ds(pl.multiple_of(core * 640, 8), 640)
    other_half = pl.ds(pl.multiple_of((1 - core) * 640, 8), 640)
    swap = pltpu.make_async_remote_copy(
        src_ref=part.at[other_half], dst_ref=sib, send_sem=ssem.at[3], recv_sem=rsem.at[3],
        device_id=sibling, device_id_type=MESH)
    swap.start()
    swap.wait_recv()
    half[...] = part[own_half] + sib[...]

    def spread_to(step, carry):
        p = lax.rem(q + step + 1, CHIPS)
        pltpu.make_async_remote_copy(
            src_ref=half.at[pl.ds(pl.multiple_of(40 * p, 8), 40)], dst_ref=spread.at[q],
            send_sem=ssem.at[4], recv_sem=rsem.at[4],
            device_id={"gy": lax.div(p, 4), "gz": lax.rem(p, 4) * 2 + core}, device_id_type=MESH).start()
        return carry

    lax.fori_loop(0, 15, spread_to, 0)
    spread[q] = half[pl.ds(pl.multiple_of(40 * q, 8), 40)]
    wait_bytes(spread.at[pl.ds(0, 15)], rsem.at[4])
    chunk[...] = jnp.sum(spread[...], axis=0)

    is_owner = jnp.logical_and(lax.rem(z, 3) == 0, z < 15)
    own_t = lax.div(z, 3)
    for t in range(5):
        @pl.when(z != 3 * t)
        def _(t=t):
            pltpu.make_async_remote_copy(
                src_ref=chunk.at[pl.ds(8 * t, 8)], dst_ref=unit_in.at[z],
                send_sem=ssem.at[5], recv_sem=rsem.at[5],
                device_id={"gx": 3 * t}, device_id_type=MESH).start()

    @pl.when(is_owner)
    def _():
        mine_rows = pl.ds(pl.multiple_of(8 * own_t, 8), 8)
        unit_in[z] = chunk[mine_rows]
        wait_bytes(unit_in.at[pl.ds(0, 15)], rsem.at[5])
        unit[...] = jnp.sum(unit_in[...], axis=0) * (1.0 / total)

        def give(step, carry):
            pltpu.make_async_remote_copy(
                src_ref=unit, dst_ref=mine.at[mine_rows],
                send_sem=ssem.at[6], recv_sem=rsem.at[6],
                device_id={"gx": partner(z, step)}, device_id_type=MESH).start()
            return carry

        lax.fori_loop(0, 15, give, 0)
        mine[mine_rows] = unit[...]
        wait_bytes(mine.at[pl.ds(0, 32)], rsem.at[6])
        wait_bytes(unit_in.at[pl.ds(0, 15)], ssem.at[6])
        wait_bytes(chunk.at[pl.ds(0, 32)], ssem.at[5])

    @pl.when(jnp.logical_not(is_owner))
    def _():
        wait_bytes(mine, rsem.at[6])
        wait_bytes(chunk, ssem.at[5])

    def back_to(step, carry):
        p = lax.rem(q + step + 1, CHIPS)
        pltpu.make_async_remote_copy(
            src_ref=mine, dst_ref=fin.at[pl.ds(pl.multiple_of(core * 640 + 40 * q, 8), 40)],
            send_sem=ssem.at[7], recv_sem=rsem.at[7],
            device_id={"gy": lax.div(p, 4), "gz": lax.rem(p, 4) * 2 + core}, device_id_type=MESH).start()
        return carry

    lax.fori_loop(0, 15, back_to, 0)
    fin[pl.ds(pl.multiple_of(core * 640 + 40 * q, 8), 40)] = mine[...]
    wait_bytes(fin.at[pl.ds(0, 600)], rsem.at[7])
    swap_back = pltpu.make_async_remote_copy(
        src_ref=fin.at[own_half], dst_ref=fin.at[own_half], send_sem=ssem.at[8], recv_sem=rsem.at[8],
        device_id=sibling, device_id_type=MESH)
    swap_back.start()
    swap_back.wait_recv()

    for i in range(4):
        for j in range(i + 1):
            b = i * (i + 1) // 2 + j
            block = fin[128 * b:128 * b + 128]
            g_out[128 * i:128 * i + 128, 128 * j:128 * j + 128] = block
            if j < i:
                g_out[128 * j:128 * j + 128, 128 * i:128 * i + 128] = block.T

    wait_bytes(send.at[pl.ds(0, 15)], ssem.at[0])
    wait_bytes(send.at[pl.ds(0, 15)], ssem.at[1])

    @pl.when(is_short)
    def _():
        wait_bytes(send.at[pl.ds(0, 12)], ssem.at[2])

    @pl.when(jnp.logical_not(is_short))
    def _():
        wait_bytes(send.at[pl.ds(0, 11)], ssem.at[2])

    swap.wait_send()
    wait_bytes(half.at[pl.ds(0, 600)], ssem.at[4])
    wait_bytes(half.at[pl.ds(0, 600)], ssem.at[7])
    swap_back.wait_send()
    keep.wait()


def gram(x, total):
    vm = pl.BlockSpec(memory_space=pltpu.VMEM)
    return pl.pallas_call(
        functools.partial(gram_kernel, total),
        out_shape=(jax.ShapeDtypeStruct((SLOTS, 512, 128), F32), jax.ShapeDtypeStruct((512, 512), F32)),
        in_specs=[vm],
        out_specs=(pl.BlockSpec(memory_space=pl.ANY), vm),
        scratch_shapes=[
            pltpu.VMEM((GROUPS, 32, 128), F32),
            pltpu.VMEM((SLOTS, 512, 128), F32),
            pltpu.VMEM((512, 384), BF16),
            pltpu.VMEM((512, 384), BF16),
            pltpu.VMEM((1280, 128), F32),
            pltpu.VMEM((640, 128), F32),
            pltpu.VMEM((640, 128), F32),
            pltpu.VMEM((CHIPS, 40, 128), F32),
            pltpu.VMEM((Z, 8, 128), F32),
            pltpu.VMEM((8, 128), F32),
            pltpu.VMEM((40, 128), F32),
            pltpu.VMEM((40, 128), F32),
            pltpu.VMEM((1280, 128), F32),
            pltpu.SemaphoreType.DMA((9,)),
            pltpu.SemaphoreType.DMA((9,)),
            pltpu.SemaphoreType.DMA,
        ],
        compiler_params=pltpu.CompilerParams(
            collective_id=0, has_side_effects=True, vmem_limit_bytes=32 * 1024 * 1024),
    )(x)


def return_kernel(y_ref, out_ref, got, ssem, rsem):
    z, x, y, core = place()
    barrier = pltpu.get_barrier_semaphore()

    def greet(step, carry):
        pl.semaphore_signal(barrier, inc=1, device_id={"gx": partner(z, step)}, device_id_type=MESH)
        return carry

    lax.fori_loop(0, 15, greet, 0)
    first = first_group(z, core)
    is_short = short(z, core)
    pl.semaphore_wait(barrier, 15)

    def push(n):
        def one(step, carry):
            d = partner(z, step)
            pltpu.make_async_remote_copy(
                src_ref=y_ref.at[d, pl.ds(0, n)], dst_ref=got.at[pl.ds(first, n)],
                send_sem=ssem, recv_sem=rsem, device_id={"gx": d}, device_id_type=MESH).start()
            return carry

        lax.fori_loop(0, 15, one, 0)
        got[pl.ds(first, n)] = y_ref[z, pl.ds(0, n)]
        wait_bytes(got.at[pl.ds(0, GROUPS - n)], rsem)
        wait_bytes(y_ref.at[pl.ds(0, 15), pl.ds(0, n)], ssem)

    @pl.when(is_short)
    def _():
        push(2)

    @pl.when(jnp.logical_not(is_short))
    def _():
        push(3)

    for e in range(7):
        for s in range(11):
            out_ref[e, s] = got[4 * s:4 * s + 4, e, :]


def give_back(y):
    vm = pl.BlockSpec(memory_space=pltpu.VMEM)
    return pl.pallas_call(
        return_kernel,
        out_shape=jax.ShapeDtypeStruct((7, 11, 4, 128), F32),
        in_specs=[vm],
        out_specs=vm,
        scratch_shapes=[
            pltpu.VMEM((GROUPS, 7, 128), F32),
            pltpu.SemaphoreType.DMA,
            pltpu.SemaphoreType.DMA,
        ],
        compiler_params=pltpu.CompilerParams(collective_id=1, has_side_effects=True),
    )(y)


def per_device(species_field, start_basis):
    highest = lax.Precision.HIGHEST
    total = float(11 * 16 * 1024)
    xt, gram_matrix = gram(species_field.reshape(11, 128, 128), total)
    subspace = start_basis
    for turn_index in range(ITERS):
        image_cols = jnp.dot(gram_matrix, subspace, precision=highest)
        inner = jnp.dot(image_cols.T, image_cols, precision=highest)
        factor = jnp.linalg.cholesky(inner)
        subspace = lax.linalg.triangular_solve(
            factor, image_cols, left_side=False, lower=True, transpose_a=True
        )
    core = jnp.einsum("ir,gil->rgl", subspace, xt, precision=highest)
    core = core.reshape(16, 7, SLOTS, 128).transpose(0, 2, 1, 3)
    return (subspace, give_back(core))


def solution(mesh):
    placed = (P(None, "gx", "gy", "gz"), P())
    return jax.shard_map(
        per_device,
        mesh=mesh,
        in_specs=placed,
        out_specs=(P(), P("gx", None, "gy", "gz")),
        check_vma=False,
    )
```

```python
import functools

import jax
import jax.numpy as jnp
from jax import lax
from jax.experimental import pallas as pl
from jax.experimental.pallas import tpu as pltpu
from jax.sharding import PartitionSpec as P

ITERS = 8
MESH = pl.DeviceIdType.MESH
F32 = jnp.float32
BF16 = jnp.bfloat16

Z = 16
GROUPS = 44
SLOTS = 3
CHIPS = 16


def place():
    z = lax.axis_index("gx")
    x = lax.axis_index("gy")
    w = lax.axis_index("gz")
    core = lax.rem(w, 2)
    return z, x, lax.div(w, 2), core


def first_group(dest, core):
    return 3 * dest - lax.div(dest + 3 - 2 * core, 4)


def short(dest, core):
    return lax.rem(dest, 4) == 2 * core


def partner(me, step):
    half = lax.div(step + 1, 2)
    k = 8 + half * (2 * lax.rem(step, 2) - 1)
    return lax.rem(me + k, Z)


def wait_bytes(ref, sem):
    pltpu.make_async_copy(ref, ref, sem).wait()


def split(v):
    hi = v.astype(BF16)
    return hi, (v - hi.astype(F32)).astype(BF16)


def dot_t(a, b):
    return lax.dot_general(a, b, (((1,), (1,)), ((), ())), preferred_element_type=F32)


def gram_kernel(total, x_ref, xt_out, g_out, send, recv, hi_ref, lo_ref, part, sib, half, spread,
                unit_in, unit, chunk, mine, fin, ssem, rsem, lsem):
    z, x, y, core = place()
    q = x * 4 + y
    barrier = pltpu.get_barrier_semaphore()

    def greet(step, carry):
        pl.semaphore_signal(barrier, inc=1, device_id={"gx": partner(z, step)}, device_id_type=MESH)
        p = lax.rem(q + step + 1, CHIPS)
        pl.semaphore_signal(
            barrier, inc=1, device_id={"gy": lax.div(p, 4), "gz": lax.rem(p, 4) * 2 + core}, device_id_type=MESH
        )
        return carry

    lax.fori_loop(0, 15, greet, 0)
    sibling = {"gz": y * 2 + 1 - core}
    pl.semaphore_signal(barrier, inc=1, device_id=sibling, device_id_type=MESH)

    for g in range(GROUPS):
        s, yy = divmod(g, 4)
        send[g] = x_ref[s, pl.ds(yy, 32, stride=4), :]
    pl.semaphore_wait(barrier, 31)

    rows = pl.ds(pl.multiple_of(z * 32, 32), 32)

    def copy_to(slot, d):
        return pltpu.make_async_remote_copy(
            src_ref=send.at[first_group(d, core) + slot],
            dst_ref=recv.at[slot, rows],
            send_sem=ssem.at[slot],
            recv_sem=rsem.at[slot],
            device_id={"gx": d},
            device_id_type=MESH,
        )

    for slot in range(SLOTS):
        def push(step, carry, slot=slot):
            d = partner(z, step)
            if slot < 2:
                copy_to(slot, d).start()
            else:
                @pl.when(jnp.logical_not(short(d, core)))
                def _():
                    copy_to(slot, d).start()
            return carry

        lax.fori_loop(0, 15, push, 0)
    mine_first = first_group(z, core)
    recv[0, rows] = send[mine_first]
    recv[1, rows] = send[mine_first + 1]
    is_short = short(z, core)

    @pl.when(is_short)
    def _():
        recv[2] = jnp.zeros((512, 128), F32)

    @pl.when(jnp.logical_not(is_short))
    def _():
        recv[2, rows] = send[mine_first + 2]

    others = pl.ds(0, 480)

    def accumulate(lanes, first):
        for i in range(4):
            ri = slice(128 * i, 128 * i + 128)
            up = slice(0, 128 * i + 128)
            hi_i, lo_i = hi_ref[ri, lanes], lo_ref[ri, lanes]
            hi_u = hi_ref[up, lanes]
            block = dot_t(hi_i, hi_u) + dot_t(hi_i, lo_ref[up, lanes]) + dot_t(lo_i, hi_u)
            for j in range(i + 1):
                b = i * (i + 1) // 2 + j
                rb = slice(128 * b, 128 * b + 128)
                piece = block[:, 128 * j:128 * j + 128]
                part[rb] = piece if first else part[rb] + piece

    def take(slot):
        hi, lo = split(recv[slot])
        hi_ref[:, 128 * slot:128 * slot + 128] = hi
        lo_ref[:, 128 * slot:128 * slot + 128] = lo

    wait_bytes(recv.at[0, others], rsem.at[0])
    take(0)
    wait_bytes(recv.at[1, others], rsem.at[1])
    take(1)
    accumulate(slice(0, 256), True)

    @pl.when(jnp.logical_not(is_short))
    def _():
        wait_bytes(recv.at[2, others], rsem.at[2])

    take(2)
    accumulate(slice(256, 384), False)
    keep = pltpu.make_async_copy(recv, xt_out, lsem)
    keep.start()

    own_half = pl.ds(pl.multiple_of(core * 640, 8), 640)
    other_half = pl.ds(pl.multiple_of((1 - core) * 640, 8), 640)
    swap = pltpu.make_async_remote_copy(
        src_ref=part.at[other_half], dst_ref=sib, send_sem=ssem.at[3], recv_sem=rsem.at[3],
        device_id=sibling, device_id_type=MESH)
    swap.start()
    swap.wait_recv()
    half[...] = part[own_half] + sib[...]

    def spread_to(step, carry):
        p = lax.rem(q + step + 1, CHIPS)
        pltpu.make_async_remote_copy(
            src_ref=half.at[pl.ds(pl.multiple_of(40 * p, 8), 40)], dst_ref=spread.at[q],
            send_sem=ssem.at[4], recv_sem=rsem.at[4],
            device_id={"gy": lax.div(p, 4), "gz": lax.rem(p, 4) * 2 + core}, device_id_type=MESH).start()
        return carry

    lax.fori_loop(0, 15, spread_to, 0)
    spread[q] = half[pl.ds(pl.multiple_of(40 * q, 8), 40)]
    wait_bytes(spread.at[pl.ds(0, 15)], rsem.at[4])
    chunk[...] = jnp.sum(spread[...], axis=0)

    is_owner = jnp.logical_and(lax.rem(z, 3) == 0, z < 15)
    own_t = lax.div(z, 3)
    for t in range(5):
        @pl.when(z != 3 * t)
        def _(t=t):
            pltpu.make_async_remote_copy(
                src_ref=chunk.at[pl.ds(8 * t, 8)], dst_ref=unit_in.at[z],
                send_sem=ssem.at[5], recv_sem=rsem.at[5],
                device_id={"gx": 3 * t}, device_id_type=MESH).start()

    @pl.when(is_owner)
    def _():
        mine_rows = pl.ds(pl.multiple_of(8 * own_t, 8), 8)
        unit_in[z] = chunk[mine_rows]
        wait_bytes(unit_in.at[pl.ds(0, 15)], rsem.at[5])
        unit[...] = jnp.sum(unit_in[...], axis=0) * (1.0 / total)

        def give(step, carry):
            pltpu.make_async_remote_copy(
                src_ref=unit, dst_ref=mine.at[mine_rows],
                send_sem=ssem.at[6], recv_sem=rsem.at[6],
                device_id={"gx": partner(z, step)}, device_id_type=MESH).start()
            return carry

        lax.fori_loop(0, 15, give, 0)
        mine[mine_rows] = unit[...]
        wait_bytes(mine.at[pl.ds(0, 32)], rsem.at[6])
        wait_bytes(unit_in.at[pl.ds(0, 15)], ssem.at[6])
        wait_bytes(chunk.at[pl.ds(0, 32)], ssem.at[5])

    @pl.when(jnp.logical_not(is_owner))
    def _():
        wait_bytes(mine, rsem.at[6])
        wait_bytes(chunk, ssem.at[5])

    def back_to(step, carry):
        p = lax.rem(q + step + 1, CHIPS)
        pltpu.make_async_remote_copy(
            src_ref=mine, dst_ref=fin.at[pl.ds(pl.multiple_of(core * 640 + 40 * q, 8), 40)],
            send_sem=ssem.at[7], recv_sem=rsem.at[7],
            device_id={"gy": lax.div(p, 4), "gz": lax.rem(p, 4) * 2 + core}, device_id_type=MESH).start()
        return carry

    lax.fori_loop(0, 15, back_to, 0)
    fin[pl.ds(pl.multiple_of(core * 640 + 40 * q, 8), 40)] = mine[...]
    wait_bytes(fin.at[pl.ds(0, 600)], rsem.at[7])
    swap_back = pltpu.make_async_remote_copy(
        src_ref=fin.at[own_half], dst_ref=fin.at[own_half], send_sem=ssem.at[8], recv_sem=rsem.at[8],
        device_id=sibling, device_id_type=MESH)
    swap_back.start()
    swap_back.wait_recv()

    for i in range(4):
        for j in range(i + 1):
            b = i * (i + 1) // 2 + j
            block = fin[128 * b:128 * b + 128]
            g_out[128 * i:128 * i + 128, 128 * j:128 * j + 128] = block
            if j < i:
                g_out[128 * j:128 * j + 128, 128 * i:128 * i + 128] = block.T

    wait_bytes(send.at[pl.ds(0, 15)], ssem.at[0])
    wait_bytes(send.at[pl.ds(0, 15)], ssem.at[1])

    @pl.when(is_short)
    def _():
        wait_bytes(send.at[pl.ds(0, 12)], ssem.at[2])

    @pl.when(jnp.logical_not(is_short))
    def _():
        wait_bytes(send.at[pl.ds(0, 11)], ssem.at[2])

    swap.wait_send()
    wait_bytes(half.at[pl.ds(0, 600)], ssem.at[4])
    wait_bytes(half.at[pl.ds(0, 600)], ssem.at[7])
    swap_back.wait_send()
    keep.wait()


def gram(x, total):
    vm = pl.BlockSpec(memory_space=pltpu.VMEM)
    return pl.pallas_call(
        functools.partial(gram_kernel, total),
        out_shape=(jax.ShapeDtypeStruct((SLOTS, 512, 128), F32), jax.ShapeDtypeStruct((512, 512), F32)),
        in_specs=[vm],
        out_specs=(pl.BlockSpec(memory_space=pl.ANY), vm),
        scratch_shapes=[
            pltpu.VMEM((GROUPS, 32, 128), F32),
            pltpu.VMEM((SLOTS, 512, 128), F32),
            pltpu.VMEM((512, 384), BF16),
            pltpu.VMEM((512, 384), BF16),
            pltpu.VMEM((1280, 128), F32),
            pltpu.VMEM((640, 128), F32),
            pltpu.VMEM((640, 128), F32),
            pltpu.VMEM((CHIPS, 40, 128), F32),
            pltpu.VMEM((Z, 8, 128), F32),
            pltpu.VMEM((8, 128), F32),
            pltpu.VMEM((40, 128), F32),
            pltpu.VMEM((40, 128), F32),
            pltpu.VMEM((1280, 128), F32),
            pltpu.SemaphoreType.DMA((9,)),
            pltpu.SemaphoreType.DMA((9,)),
            pltpu.SemaphoreType.DMA,
        ],
        compiler_params=pltpu.CompilerParams(
            collective_id=0, has_side_effects=True, vmem_limit_bytes=32 * 1024 * 1024),
    )(x)


def return_kernel(y_ref, out_ref, got, ssem, rsem):
    z, x, y, core = place()
    barrier = pltpu.get_barrier_semaphore()

    def greet(step, carry):
        pl.semaphore_signal(barrier, inc=1, device_id={"gx": partner(z, step)}, device_id_type=MESH)
        return carry

    lax.fori_loop(0, 15, greet, 0)
    first = first_group(z, core)
    is_short = short(z, core)
    pl.semaphore_wait(barrier, 15)

    def push(n):
        def one(step, carry):
            d = partner(z, step)
            pltpu.make_async_remote_copy(
                src_ref=y_ref.at[d, pl.ds(0, n)], dst_ref=got.at[pl.ds(first, n)],
                send_sem=ssem, recv_sem=rsem, device_id={"gx": d}, device_id_type=MESH).start()
            return carry

        lax.fori_loop(0, 15, one, 0)
        got[pl.ds(first, n)] = y_ref[z, pl.ds(0, n)]
        wait_bytes(got.at[pl.ds(0, GROUPS - n)], rsem)
        wait_bytes(y_ref.at[pl.ds(0, 15), pl.ds(0, n)], ssem)

    @pl.when(is_short)
    def _():
        push(2)

    @pl.when(jnp.logical_not(is_short))
    def _():
        push(3)

    for e in range(7):
        for s in range(11):
            out_ref[e, s] = got[4 * s:4 * s + 4, e, :]


def give_back(y):
    vm = pl.BlockSpec(memory_space=pltpu.VMEM)
    return pl.pallas_call(
        return_kernel,
        out_shape=jax.ShapeDtypeStruct((7, 11, 4, 128), F32),
        in_specs=[vm],
        out_specs=vm,
        scratch_shapes=[
            pltpu.VMEM((GROUPS, 7, 128), F32),
            pltpu.SemaphoreType.DMA,
            pltpu.SemaphoreType.DMA,
        ],
        compiler_params=pltpu.CompilerParams(collective_id=1, has_side_effects=True),
    )(y)


RANK = 112
TILES = RANK // 8


def spread_out(v):
    return jnp.broadcast_to(v, (8, 128))


def inverse_factor(a):
    sub = lax.broadcasted_iota(jnp.int32, (8, 128), 0)
    lane = lax.broadcasted_iota(jnp.int32, (8, 128), 1)
    left = [a[8 * t:8 * t + 8, :] for t in range(TILES)]
    right = [(lane == sub + 8 * t).astype(F32) for t in range(TILES)]
    result = []
    for t0 in range(TILES):
        k0 = 8 * t0
        later = range(t0 + 1, TILES)
        row = [spread_out(left[t0][i:i + 1, :]) for i in range(8)]
        row_inv = [spread_out(right[t0][i:i + 1, :]) for i in range(8)]
        s = [[spread_out(row[i][:, k0 + j:k0 + j + 1]) for j in range(i + 1)] for i in range(8)]
        col = {t: [spread_out(left[t][:, k0 + j:k0 + j + 1]) for j in range(8)] for t in later}
        for j in range(8):
            inv = 1.0 / s[j][j]
            m = [None] * 8
            for i in range(j + 1, 8):
                m[i] = s[i][j] * inv
            for i in range(j + 1, 8):
                for n in range(j + 1, i + 1):
                    s[i][n] = s[i][n] - m[i] * s[n][j]
            for i in range(j + 1, 8):
                row[i] = row[i] - m[i] * row[j]
                row_inv[i] = row_inv[i] - m[i] * row_inv[j]
            for t in later:
                x = col[t][j] * inv
                for n in range(j + 1, 8):
                    col[t][n] = col[t][n] - x * s[n][j]
                left[t] = left[t] - x * row[j]
                right[t] = right[t] - x * row_inv[j]
        tile = None
        for i in range(8):
            v = row_inv[i] * lax.rsqrt(s[i][i])
            tile = v if tile is None else jnp.where(sub == i, v, tile)
        result.append(tile)
    return jnp.concatenate(result, axis=0)


def dot(a, b, dims):
    return lax.dot_general(a, b, (dims, ((), ())), precision=lax.Precision.HIGHEST, preferred_element_type=F32)


PLAIN = ((1,), (0,))
BOTH_LAST = ((1,), (1,))


def turns_kernel(g_ref, s_ref, xt_ref, st_ref, core_ref, image):
    image[...] = dot(s_ref[...].T, g_ref[...], PLAIN)

    def factor(z):
        padded = jnp.concatenate([z, jnp.zeros((16, 512), F32)], axis=0)
        return inverse_factor(dot(z, padded, BOTH_LAST))[:, :RANK]

    def turn(index, carry):
        z = image[...]
        y = dot(z, g_ref[...], PLAIN)
        image[...] = dot(factor(z), y, PLAIN)
        return carry

    lax.fori_loop(0, ITERS - 1, turn, 0)
    z = image[...]
    basis = dot(factor(z), z, PLAIN)
    st_ref[...] = basis.T
    for slot in range(SLOTS):
        core = dot(basis, xt_ref[slot], PLAIN)
        for d in range(Z):
            core_ref[d, slot] = core[7 * d:7 * d + 7, :]


def turns(g, s, xt):
    vm = pl.BlockSpec(memory_space=pltpu.VMEM)
    return pl.pallas_call(
        turns_kernel,
        out_shape=(jax.ShapeDtypeStruct((512, RANK), F32), jax.ShapeDtypeStruct((Z, SLOTS, 7, 128), F32)),
        in_specs=[vm, vm, vm],
        out_specs=(vm, vm),
        scratch_shapes=[pltpu.VMEM((RANK, 512), F32)],
        compiler_params=pltpu.CompilerParams(vmem_limit_bytes=32 * 1024 * 1024),
    )(g, s, xt)


def per_device(species_field, start_basis):
    total = float(11 * 16 * 1024)
    xt, gram_matrix = gram(species_field.reshape(11, 128, 128), total)
    subspace, core = turns(gram_matrix, start_basis, xt)
    return (subspace, give_back(core))


def solution(mesh):
    placed = (P(None, "gx", "gy", "gz"), P())
    return jax.shard_map(
        per_device,
        mesh=mesh,
        in_specs=placed,
        out_specs=(P(), P("gx", None, "gy", "gz")),
        check_vma=False,
    )
```

```python
import functools

import jax
import jax.numpy as jnp
from jax import lax
from jax.experimental import pallas as pl
from jax.experimental.pallas import tpu as pltpu
from jax.sharding import PartitionSpec as P

ITERS = 8
MESH = pl.DeviceIdType.MESH
F32 = jnp.float32
BF16 = jnp.bfloat16

Z = 16
GROUPS = 44
SLOTS = 3
CHIPS = 16


def place():
    z = lax.axis_index("gx")
    x = lax.axis_index("gy")
    w = lax.axis_index("gz")
    core = lax.rem(w, 2)
    return z, x, lax.div(w, 2), core


def first_group(dest, core):
    return 3 * dest - lax.div(dest + 3 - 2 * core, 4)


def short(dest, core):
    return lax.rem(dest, 4) == 2 * core


def partner(me, step):
    half = lax.div(step + 1, 2)
    k = 8 + half * (2 * lax.rem(step, 2) - 1)
    return lax.rem(me + k, Z)


def wait_bytes(ref, sem):
    pltpu.make_async_copy(ref, ref, sem).wait()


def split(v):
    hi = v.astype(BF16)
    return hi, (v - hi.astype(F32)).astype(BF16)


def dot_t(a, b):
    return lax.dot_general(a, b, (((1,), (1,)), ((), ())), preferred_element_type=F32)


def gram_kernel(total, x_ref, xt_out, g_out, send, recv, hi_ref, lo_ref, part, sib, half, spread,
                unit_in, unit, chunk, mine, fin, ssem, rsem, lsem):
    z, x, y, core = place()
    q = x * 4 + y
    barrier = pltpu.get_barrier_semaphore()

    def greet(step, carry):
        pl.semaphore_signal(barrier, inc=1, device_id={"gx": partner(z, step)}, device_id_type=MESH)
        p = lax.rem(q + step + 1, CHIPS)
        pl.semaphore_signal(
            barrier, inc=1, device_id={"gy": lax.div(p, 4), "gz": lax.rem(p, 4) * 2 + core}, device_id_type=MESH
        )
        return carry

    lax.fori_loop(0, 15, greet, 0)
    sibling = {"gz": y * 2 + 1 - core}
    pl.semaphore_signal(barrier, inc=1, device_id=sibling, device_id_type=MESH)

    for g in range(GROUPS):
        s, yy = divmod(g, 4)
        send[g] = x_ref[s, pl.ds(yy, 32, stride=4), :]
    pl.semaphore_wait(barrier, 31)

    rows = pl.ds(pl.multiple_of(z * 32, 32), 32)

    def copy_to(slot, d):
        return pltpu.make_async_remote_copy(
            src_ref=send.at[first_group(d, core) + slot],
            dst_ref=recv.at[slot, rows],
            send_sem=ssem.at[slot],
            recv_sem=rsem.at[slot],
            device_id={"gx": d},
            device_id_type=MESH,
        )

    for slot in range(SLOTS):
        def push(step, carry, slot=slot):
            d = partner(z, step)
            if slot < 2:
                copy_to(slot, d).start()
            else:
                @pl.when(jnp.logical_not(short(d, core)))
                def _():
                    copy_to(slot, d).start()
            return carry

        lax.fori_loop(0, 15, push, 0)
    mine_first = first_group(z, core)
    recv[0, rows] = send[mine_first]
    recv[1, rows] = send[mine_first + 1]
    is_short = short(z, core)

    @pl.when(is_short)
    def _():
        recv[2] = jnp.zeros((512, 128), F32)

    @pl.when(jnp.logical_not(is_short))
    def _():
        recv[2, rows] = send[mine_first + 2]

    others = pl.ds(0, 480)

    def accumulate(lanes, first):
        for i in range(4):
            ri = slice(128 * i, 128 * i + 128)
            up = slice(0, 128 * i + 128)
            hi_i, lo_i = hi_ref[ri, lanes], lo_ref[ri, lanes]
            hi_u = hi_ref[up, lanes]
            block = dot_t(hi_i, hi_u) + dot_t(hi_i, lo_ref[up, lanes]) + dot_t(lo_i, hi_u)
            for j in range(i + 1):
                b = i * (i + 1) // 2 + j
                rb = slice(128 * b, 128 * b + 128)
                piece = block[:, 128 * j:128 * j + 128]
                part[rb] = piece if first else part[rb] + piece

    def take(slot):
        hi, lo = split(recv[slot])
        hi_ref[:, 128 * slot:128 * slot + 128] = hi
        lo_ref[:, 128 * slot:128 * slot + 128] = lo

    wait_bytes(recv.at[0, others], rsem.at[0])
    take(0)
    wait_bytes(recv.at[1, others], rsem.at[1])
    take(1)
    accumulate(slice(0, 256), True)

    @pl.when(jnp.logical_not(is_short))
    def _():
        wait_bytes(recv.at[2, others], rsem.at[2])

    take(2)
    accumulate(slice(256, 384), False)
    keep = pltpu.make_async_copy(recv, xt_out, lsem)
    keep.start()

    own_half = pl.ds(pl.multiple_of(core * 640, 8), 640)
    other_half = pl.ds(pl.multiple_of((1 - core) * 640, 8), 640)
    swap = pltpu.make_async_remote_copy(
        src_ref=part.at[other_half], dst_ref=sib, send_sem=ssem.at[3], recv_sem=rsem.at[3],
        device_id=sibling, device_id_type=MESH)
    swap.start()
    swap.wait_recv()
    half[...] = part[own_half] + sib[...]

    def spread_to(step, carry):
        p = lax.rem(q + step + 1, CHIPS)
        pltpu.make_async_remote_copy(
            src_ref=half.at[pl.ds(pl.multiple_of(40 * p, 8), 40)], dst_ref=spread.at[q],
            send_sem=ssem.at[4], recv_sem=rsem.at[4],
            device_id={"gy": lax.div(p, 4), "gz": lax.rem(p, 4) * 2 + core}, device_id_type=MESH).start()
        return carry

    lax.fori_loop(0, 15, spread_to, 0)
    spread[q] = half[pl.ds(pl.multiple_of(40 * q, 8), 40)]
    wait_bytes(spread.at[pl.ds(0, 15)], rsem.at[4])
    chunk[...] = jnp.sum(spread[...], axis=0)

    is_owner = jnp.logical_and(lax.rem(z, 3) == 0, z < 15)
    own_t = lax.div(z, 3)
    for t in range(5):
        @pl.when(z != 3 * t)
        def _(t=t):
            pltpu.make_async_remote_copy(
                src_ref=chunk.at[pl.ds(8 * t, 8)], dst_ref=unit_in.at[z],
                send_sem=ssem.at[5], recv_sem=rsem.at[5],
                device_id={"gx": 3 * t}, device_id_type=MESH).start()

    @pl.when(is_owner)
    def _():
        mine_rows = pl.ds(pl.multiple_of(8 * own_t, 8), 8)
        unit_in[z] = chunk[mine_rows]
        wait_bytes(unit_in.at[pl.ds(0, 15)], rsem.at[5])
        unit[...] = jnp.sum(unit_in[...], axis=0) * (1.0 / total)

        def give(step, carry):
            pltpu.make_async_remote_copy(
                src_ref=unit, dst_ref=mine.at[mine_rows],
                send_sem=ssem.at[6], recv_sem=rsem.at[6],
                device_id={"gx": partner(z, step)}, device_id_type=MESH).start()
            return carry

        lax.fori_loop(0, 15, give, 0)
        mine[mine_rows] = unit[...]
        wait_bytes(mine.at[pl.ds(0, 32)], rsem.at[6])
        wait_bytes(unit_in.at[pl.ds(0, 15)], ssem.at[6])
        wait_bytes(chunk.at[pl.ds(0, 32)], ssem.at[5])

    @pl.when(jnp.logical_not(is_owner))
    def _():
        wait_bytes(mine, rsem.at[6])
        wait_bytes(chunk, ssem.at[5])

    def back_to(step, carry):
        p = lax.rem(q + step + 1, CHIPS)
        pltpu.make_async_remote_copy(
            src_ref=mine, dst_ref=fin.at[pl.ds(pl.multiple_of(core * 640 + 40 * q, 8), 40)],
            send_sem=ssem.at[7], recv_sem=rsem.at[7],
            device_id={"gy": lax.div(p, 4), "gz": lax.rem(p, 4) * 2 + core}, device_id_type=MESH).start()
        return carry

    lax.fori_loop(0, 15, back_to, 0)
    fin[pl.ds(pl.multiple_of(core * 640 + 40 * q, 8), 40)] = mine[...]
    wait_bytes(fin.at[pl.ds(0, 600)], rsem.at[7])
    swap_back = pltpu.make_async_remote_copy(
        src_ref=fin.at[own_half], dst_ref=fin.at[own_half], send_sem=ssem.at[8], recv_sem=rsem.at[8],
        device_id=sibling, device_id_type=MESH)
    swap_back.start()
    swap_back.wait_recv()

    for i in range(4):
        for j in range(i + 1):
            b = i * (i + 1) // 2 + j
            block = fin[128 * b:128 * b + 128]
            g_out[128 * i:128 * i + 128, 128 * j:128 * j + 128] = block
            if j < i:
                g_out[128 * j:128 * j + 128, 128 * i:128 * i + 128] = block.T

    wait_bytes(send.at[pl.ds(0, 15)], ssem.at[0])
    wait_bytes(send.at[pl.ds(0, 15)], ssem.at[1])

    @pl.when(is_short)
    def _():
        wait_bytes(send.at[pl.ds(0, 12)], ssem.at[2])

    @pl.when(jnp.logical_not(is_short))
    def _():
        wait_bytes(send.at[pl.ds(0, 11)], ssem.at[2])

    swap.wait_send()
    wait_bytes(half.at[pl.ds(0, 600)], ssem.at[4])
    wait_bytes(half.at[pl.ds(0, 600)], ssem.at[7])
    swap_back.wait_send()
    keep.wait()


def gram(x, total):
    vm = pl.BlockSpec(memory_space=pltpu.VMEM)
    return pl.pallas_call(
        functools.partial(gram_kernel, total),
        out_shape=(jax.ShapeDtypeStruct((SLOTS, 512, 128), F32), jax.ShapeDtypeStruct((512, 512), F32)),
        in_specs=[vm],
        out_specs=(pl.BlockSpec(memory_space=pl.ANY), vm),
        scratch_shapes=[
            pltpu.VMEM((GROUPS, 32, 128), F32),
            pltpu.VMEM((SLOTS, 512, 128), F32),
            pltpu.VMEM((512, 384), BF16),
            pltpu.VMEM((512, 384), BF16),
            pltpu.VMEM((1280, 128), F32),
            pltpu.VMEM((640, 128), F32),
            pltpu.VMEM((640, 128), F32),
            pltpu.VMEM((CHIPS, 40, 128), F32),
            pltpu.VMEM((Z, 8, 128), F32),
            pltpu.VMEM((8, 128), F32),
            pltpu.VMEM((40, 128), F32),
            pltpu.VMEM((40, 128), F32),
            pltpu.VMEM((1280, 128), F32),
            pltpu.SemaphoreType.DMA((9,)),
            pltpu.SemaphoreType.DMA((9,)),
            pltpu.SemaphoreType.DMA,
        ],
        compiler_params=pltpu.CompilerParams(
            collective_id=0, has_side_effects=True, vmem_limit_bytes=32 * 1024 * 1024),
    )(x)


RANK = 112
TILES = RANK // 8
PIECES = [(p, q, half) for p, q in ((0, 0), (0, 1), (1, 0), (0, 2), (2, 0), (1, 1)) for half in range(2)]


def spread_out(v):
    return jnp.broadcast_to(v, (8, 128))


def column(tile, k):
    return spread_out(tile[:, k:k + 1])


def row_of(ref, index, i):
    return spread_out(ref[index, i:i + 1, :])


def inverse_factor(a, work, beside):
    sub = lax.broadcasted_iota(jnp.int32, (8, 128), 0)
    lane = lax.broadcasted_iota(jnp.int32, (8, 128), 1)
    left = [a[8 * t:8 * t + 8, :] for t in range(TILES)]
    right = [(lane == sub + 8 * t).astype(F32) for t in range(TILES)]
    result = []
    ahead = None
    for t0 in range(TILES):
        k0 = 8 * t0
        base = (t0 % 2) * 18
        work[base] = left[t0]
        work[base + 1] = right[t0]
        row = [row_of(work, base, i) for i in range(8)]
        row_inv = [row_of(work, base + 1, i) for i in range(8)]
        for j in range(8):
            work[base + 2 + j] = column(left[t0], k0 + j) if ahead is None else ahead[j]
        s = [[row_of(work, base + 2 + j, i) for j in range(i + 1)] for i in range(8)]
        near = range(t0 + 1, min(TILES, t0 + 3))
        far = range(min(TILES, t0 + 3), TILES)
        col = {t: [column(left[t], k0 + j) for j in range(8)] for t in near}
        ahead = [column(left[t0 + 1], k0 + 8 + j) for j in range(8)] if near else None
        beside(t0)
        factors, inverses = [], []
        for j in range(8):
            inv = 1.0 / s[j][j]
            m = [None] * 8
            for i in range(j + 1, 8):
                m[i] = s[i][j] * inv
            factors.append(m)
            inverses.append(inv)
            for i in range(j + 1, 8):
                for n in range(j + 1, i + 1):
                    s[i][n] = s[i][n] - m[i] * s[n][j]
            for i in range(j + 1, 8):
                row[i] = row[i] - m[i] * row[j]
                row_inv[i] = row_inv[i] - m[i] * row_inv[j]
            if near:
                work[base + 10 + j] = col[t0 + 1][j]
                next_row = [row_of(work, base + 10 + j, i) for i in range(8)]
            for t in near:
                x = col[t][j] * inv
                for n in range(j + 1, 8):
                    col[t][n] = col[t][n] - x * s[n][j]
                if t == t0 + 1:
                    ahead = [ahead[n] - x * next_row[n] for n in range(8)]
                left[t] = left[t] - x * row[j]
                right[t] = right[t] - x * row_inv[j]
        tile, pivots = row_inv[7], s[7][7]
        for i in range(7):
            tile = jnp.where(sub == i, row_inv[i], tile)
            pivots = jnp.where(sub == i, s[i][i], pivots)
        result.append(tile * lax.rsqrt(pivots))
        if far:
            back, back_inv = [None] * 8, [None] * 8
            for j in reversed(range(8)):
                u, v = row[j] * inverses[j], row_inv[j] * inverses[j]
                for i in range(j + 1, 8):
                    u = u - factors[j][i] * back[i]
                    v = v - factors[j][i] * back_inv[i]
                back[j], back_inv[j] = u, v
            for t in far:
                u, v = left[t], right[t]
                for j in range(8):
                    c = column(left[t], k0 + j)
                    u = u - c * back[j]
                    v = v - c * back_inv[j]
                left[t], right[t] = u, v
    return jnp.concatenate(result, axis=0)


def split3(v):
    hi = v.astype(BF16)
    rest = v - hi.astype(F32)
    mid = rest.astype(BF16)
    return hi, mid, (rest - mid.astype(F32)).astype(BF16)


def dot_p(a, b):
    return lax.dot_general(a, b, (((1,), (0,)), ((), ())), preferred_element_type=F32)


def full(a, b, mul):
    small = (mul(a[0], b[2]) + mul(a[2], b[0])) + mul(a[1], b[1])
    return mul(a[0], b[0]) + ((mul(a[0], b[1]) + mul(a[1], b[0])) + small)


def turns_kernel(g_ref, s_ref, xt_ref, st_ref, got, image, last, ahead, inverse, parts, work, core_ref, ssem, rsem):
    z, x, y, core = place()
    barrier = pltpu.get_barrier_semaphore()

    def greet(step, carry):
        pl.semaphore_signal(barrier, inc=1, device_id={"gx": partner(z, step)}, device_id_type=MESH)
        return carry

    lax.fori_loop(0, 15, greet, 0)

    for p, part in enumerate(split3(g_ref[...])):
        parts[p] = part
    image[...] = full(split3(s_ref[...]), (parts[0], parts[1], parts[2]), dot_p)
    zeros = jnp.zeros((16, 512), BF16)

    def turn(index, carry):
        now = image[...]
        last[...] = now
        now = split3(now)
        inner = full(now, tuple(jnp.concatenate([v, zeros], axis=0) for v in now), dot_t)

        def beside(t):
            if t < len(PIECES):
                p, q, half = PIECES[t]
                lanes = slice(256 * half, 256 * half + 256)
                piece = dot_p(now[p], parts[q, :, lanes])
                ahead[:, lanes] = piece if p + q == 0 else ahead[:, lanes] + piece

        w = inverse_factor(inner, work, beside)[:, :RANK]
        inverse[...] = w
        image[...] = full(split3(w), split3(ahead[...]), dot_p)
        return carry

    lax.fori_loop(0, ITERS, turn, 0)
    basis = full(split3(inverse[...]), split3(last[...]), dot_p)
    st_ref[...] = basis
    basis_hi, basis_lo = split(basis)
    for slot in range(SLOTS):
        field_hi, field_lo = split(xt_ref[slot])
        part = dot_p(basis_hi, field_hi) + (dot_p(basis_hi, field_lo) + dot_p(basis_lo, field_hi))
        for d in range(Z):
            core_ref[d, slot] = part[7 * d:7 * d + 7, :]

    first = first_group(z, core)
    is_short = short(z, core)
    pl.semaphore_wait(barrier, 15)

    def push(n):
        def one(step, carry):
            d = partner(z, step)
            pltpu.make_async_remote_copy(
                src_ref=core_ref.at[d, pl.ds(0, n)], dst_ref=got.at[pl.ds(first, n)],
                send_sem=ssem, recv_sem=rsem, device_id={"gx": d}, device_id_type=MESH).start()
            return carry

        lax.fori_loop(0, 15, one, 0)
        got[pl.ds(first, n)] = core_ref[z, pl.ds(0, n)]
        wait_bytes(got.at[pl.ds(0, GROUPS - n)], rsem)
        wait_bytes(core_ref.at[pl.ds(0, 15), pl.ds(0, n)], ssem)

    @pl.when(is_short)
    def _():
        push(2)

    @pl.when(jnp.logical_not(is_short))
    def _():
        push(3)


def turns(g, s, xt):
    vm = pl.BlockSpec(memory_space=pltpu.VMEM)
    return pl.pallas_call(
        turns_kernel,
        out_shape=(jax.ShapeDtypeStruct((RANK, 512), F32), jax.ShapeDtypeStruct((GROUPS, 7, 128), F32)),
        in_specs=[vm, vm, vm],
        out_specs=(vm, vm),
        scratch_shapes=[
            pltpu.VMEM((RANK, 512), F32),
            pltpu.VMEM((RANK, 512), F32),
            pltpu.VMEM((RANK, 512), F32),
            pltpu.VMEM((RANK, RANK), F32),
            pltpu.VMEM((3, 512, 512), BF16),
            pltpu.VMEM((36, 8, 128), F32),
            pltpu.VMEM((Z, SLOTS, 7, 128), F32),
            pltpu.SemaphoreType.DMA,
            pltpu.SemaphoreType.DMA,
        ],
        compiler_params=pltpu.CompilerParams(
            collective_id=1, has_side_effects=True, vmem_limit_bytes=32 * 1024 * 1024),
    )(g, s, xt)


def unpack_kernel(st_ref, got_ref, st_out, core_out):
    st_out[...] = st_ref[...]
    for e in range(7):
        for s in range(11):
            core_out[e, s] = got_ref[4 * s:4 * s + 4, e, :]


def unpack(st, got):
    vm = pl.BlockSpec(memory_space=pltpu.VMEM)
    return pl.pallas_call(
        unpack_kernel,
        out_shape=(jax.ShapeDtypeStruct((RANK, 512), F32), jax.ShapeDtypeStruct((7, 11, 4, 128), F32)),
        in_specs=[vm, vm],
        out_specs=(vm, vm),
    )(st, got)


def per_device(species_field, start_basis):
    total = float(11 * 16 * 1024)
    xt, gram_matrix = gram(species_field.reshape(11, 128, 128), total)
    st, core = unpack(*turns(gram_matrix, start_basis.T, xt))
    return (st.T, core)


def solution(mesh):
    placed = (P(None, "gx", "gy", "gz"), P())
    return jax.shard_map(
        per_device,
        mesh=mesh,
        in_specs=placed,
        out_specs=(P(), P("gx", None, "gy", "gz")),
        check_vma=False,
    )
```

```python
import functools

import jax
import jax.numpy as jnp
from jax import lax
from jax.experimental import pallas as pl
from jax.experimental.pallas import tpu as pltpu
from jax.sharding import PartitionSpec as P

ITERS = 8
MESH = pl.DeviceIdType.MESH
F32 = jnp.float32
BF16 = jnp.bfloat16

Z = 16
GROUPS = 44
SLOTS = 3
CHIPS = 16


def place():
    z = lax.axis_index("gx")
    x = lax.axis_index("gy")
    w = lax.axis_index("gz")
    core = lax.rem(w, 2)
    return z, x, lax.div(w, 2), core


def first_group(dest, core):
    return 3 * dest - lax.div(dest + 3 - 2 * core, 4)


def short(dest, core):
    return lax.rem(dest, 4) == 2 * core


def partner(me, step):
    half = lax.div(step + 1, 2)
    k = 8 + half * (2 * lax.rem(step, 2) - 1)
    return lax.rem(me + k, Z)


def wait_bytes(ref, sem):
    pltpu.make_async_copy(ref, ref, sem).wait()


def split(v):
    hi = v.astype(BF16)
    return hi, (v - hi.astype(F32)).astype(BF16)


def dot_t(a, b):
    return lax.dot_general(a, b, (((1,), (1,)), ((), ())), preferred_element_type=F32)


UNITS = 5


def gram_kernel(total, x_ref, xt_out, g_out, send, recv, hi_ref, lo_ref, part, sib, half, spread,
                unit_in, chunk, mine, fin, ssem, rsem, usem, lsem, token2, token3):
    z, x, y, core = place()
    q = x * 4 + y

    def along_z(k):
        return {"gx": lax.rem(z + k + Z, Z)}

    def chip(p):
        return {"gy": lax.div(p, 4), "gz": lax.rem(p, 4) * 2 + core}

    sibling = {"gz": y * 2 + 1 - core}
    close = [along_z(k) for k in (1, -1, 2, -2)] + [sibling]
    close += [{"gy": lax.rem(x + k, 4)} for k in (1, 2, 3)]
    close += [{"gz": lax.rem(y + k, 4) * 2 + core} for k in (1, 2, 3)]
    barrier = pltpu.get_barrier_semaphore()
    for device in close:
        pl.semaphore_signal(barrier, inc=1, device_id=device, device_id_type=MESH)
    for g in range(GROUPS):
        s, yy = divmod(g, 4)
        send[g] = x_ref[s, pl.ds(yy, 32, stride=4), :]
    pl.semaphore_wait(barrier, len(close))
    for device in close:
        pl.semaphore_signal(token2, inc=1, device_id=device, device_id_type=MESH)

    rows = pl.ds(pl.multiple_of(z * 32, 32), 32)

    def copy_to(slot, d):
        return pltpu.make_async_remote_copy(
            src_ref=send.at[first_group(d, core) + slot],
            dst_ref=recv.at[slot, rows],
            send_sem=ssem.at[slot],
            recv_sem=rsem.at[slot],
            device_id={"gx": d},
            device_id_type=MESH,
        )

    def push(slot, k):
        d = lax.rem(z + k + Z, Z)
        if slot < 2:
            copy_to(slot, d).start()
        else:
            @pl.when(jnp.logical_not(short(d, core)))
            def _():
                copy_to(slot, d).start()

    for slot in range(SLOTS):
        for k in (2, -2, 1, -1):
            push(slot, k)
    pl.semaphore_wait(token2, len(close))
    for k in range(1, 5):
        for sign in (1, -1):
            pl.semaphore_signal(token3, inc=1, device_id=along_z(sign * k), device_id_type=MESH)
    for slot in range(SLOTS):
        for k in (4, -4, 3, -3):
            push(slot, k)
    pl.semaphore_wait(token3, 8)
    for slot in range(SLOTS):
        for k in (8, 7, -7, 6, -6, 5, -5):
            push(slot, k)

    mine_first = first_group(z, core)
    recv[0, rows] = send[mine_first]
    recv[1, rows] = send[mine_first + 1]
    is_short = short(z, core)

    @pl.when(is_short)
    def _():
        recv[2] = jnp.zeros((512, 128), F32)

    @pl.when(jnp.logical_not(is_short))
    def _():
        recv[2, rows] = send[mine_first + 2]

    others = pl.ds(0, 480)

    def accumulate(lanes, first):
        for i in range(4):
            ri = slice(128 * i, 128 * i + 128)
            up = slice(0, 128 * i + 128)
            hi_i, lo_i = hi_ref[ri, lanes], lo_ref[ri, lanes]
            hi_u = hi_ref[up, lanes]
            block = dot_t(hi_i, hi_u) + dot_t(hi_i, lo_ref[up, lanes]) + dot_t(lo_i, hi_u)
            for j in range(i + 1):
                b = i * (i + 1) // 2 + j
                rb = slice(128 * b, 128 * b + 128)
                piece = block[:, 128 * j:128 * j + 128]
                part[rb] = piece if first else part[rb] + piece

    def take(slot):
        hi, lo = split(recv[slot])
        hi_ref[:, 128 * slot:128 * slot + 128] = hi
        lo_ref[:, 128 * slot:128 * slot + 128] = lo

    wait_bytes(recv.at[0, others], rsem.at[0])
    take(0)
    wait_bytes(recv.at[1, others], rsem.at[1])
    take(1)
    accumulate(slice(0, 256), True)

    @pl.when(jnp.logical_not(is_short))
    def _():
        wait_bytes(recv.at[2, others], rsem.at[2])

    take(2)
    accumulate(slice(256, 384), False)
    keep = pltpu.make_async_copy(recv, xt_out, lsem)
    keep.start()

    own_half = pl.ds(pl.multiple_of(core * 640, 8), 640)
    other_half = pl.ds(pl.multiple_of((1 - core) * 640, 8), 640)
    swap = pltpu.make_async_remote_copy(
        src_ref=part.at[other_half], dst_ref=sib, send_sem=ssem.at[3], recv_sem=rsem.at[3],
        device_id=sibling, device_id_type=MESH)
    swap.start()
    swap.wait_recv()
    half[...] = part[own_half] + sib[...]

    def spread_to(step, carry):
        p = lax.rem(q + step + 1, CHIPS)
        pltpu.make_async_remote_copy(
            src_ref=half.at[pl.ds(pl.multiple_of(40 * p, 8), 40)], dst_ref=spread.at[q],
            send_sem=ssem.at[4], recv_sem=rsem.at[4],
            device_id=chip(p), device_id_type=MESH).start()
        return carry

    lax.fori_loop(0, 15, spread_to, 0)
    spread[q] = half[pl.ds(pl.multiple_of(40 * q, 8), 40)]
    wait_bytes(spread.at[pl.ds(0, 15)], rsem.at[4])
    summed = jnp.sum(spread[...], axis=0)
    for t in range(UNITS):
        chunk[t] = summed[8 * t:8 * t + 8]

    is_owner = jnp.logical_and(lax.rem(z, 3) == 0, z < 15)
    own_t = lax.div(z, 3)
    for t in range(UNITS):
        @pl.when(z != 3 * t)
        def _(t=t):
            pltpu.make_async_remote_copy(
                src_ref=chunk.at[t], dst_ref=unit_in.at[z],
                send_sem=ssem.at[5], recv_sem=rsem.at[5],
                device_id={"gx": 3 * t}, device_id_type=MESH).start()

    @pl.when(is_owner)
    def _():
        unit_in[z] = chunk[own_t]
        wait_bytes(unit_in.at[pl.ds(0, 15)], rsem.at[5])
        mine[own_t] = jnp.sum(unit_in[...], axis=0) * (1.0 / total)

        def give(step, carry):
            pltpu.make_async_remote_copy(
                src_ref=mine.at[own_t], dst_ref=mine.at[own_t],
                send_sem=ssem.at[6], recv_sem=usem.at[own_t],
                device_id={"gx": partner(z, step)}, device_id_type=MESH).start()
            return carry

        lax.fori_loop(0, 15, give, 0)

    nearest = lax.div(z + 1, 3)

    def pass_on(i, carry):
        offset = lax.div(i + 1, 2) * (2 * lax.rem(i, 2) - 1)
        t = lax.rem(nearest + offset + UNITS, UNITS)

        @pl.when(jnp.logical_not(jnp.logical_and(is_owner, own_t == t)))
        def _():
            wait_bytes(mine.at[t], usem.at[t])

        def back_to(step, carry):
            p = lax.rem(q + step + 1, CHIPS)
            pltpu.make_async_remote_copy(
                src_ref=mine.at[t], dst_ref=fin.at[core, q, t],
                send_sem=ssem.at[7], recv_sem=rsem.at[6 + i],
                device_id=chip(p), device_id_type=MESH).start()
            return carry

        lax.fori_loop(0, 15, back_to, 0)
        fin[core, q, t] = mine[t]
        return carry

    lax.fori_loop(0, UNITS, pass_on, 0)

    def other_core(i, carry):
        offset = lax.div(i + 1, 2) * (2 * lax.rem(i, 2) - 1)
        t = lax.rem(nearest + offset + UNITS, UNITS)
        wait_bytes(fin.at[core, pl.ds(0, 15), t], rsem.at[6 + i])
        pltpu.make_async_remote_copy(
            src_ref=fin.at[core, :, t], dst_ref=fin.at[core, :, t],
            send_sem=ssem.at[8], recv_sem=rsem.at[11],
            device_id=sibling, device_id_type=MESH).start()
        return carry

    lax.fori_loop(0, UNITS, other_core, 0)
    wait_bytes(fin.at[1 - core], rsem.at[11])

    for i in range(4):
        for j in range(i + 1):
            b = i * (i + 1) // 2 + j
            tiles = []
            for r in range(16 * b, 16 * b + 16):
                h, rest = divmod(r, 80)
                tiles.append(fin[h, rest // UNITS, rest % UNITS])
            block = jnp.concatenate(tiles, axis=0)
            g_out[128 * i:128 * i + 128, 128 * j:128 * j + 128] = block
            if j < i:
                g_out[128 * j:128 * j + 128, 128 * i:128 * i + 128] = block.T

    wait_bytes(send.at[pl.ds(0, 15)], ssem.at[0])
    wait_bytes(send.at[pl.ds(0, 15)], ssem.at[1])

    @pl.when(is_short)
    def _():
        wait_bytes(send.at[pl.ds(0, 12)], ssem.at[2])

    @pl.when(jnp.logical_not(is_short))
    def _():
        wait_bytes(send.at[pl.ds(0, 11)], ssem.at[2])

    swap.wait_send()
    wait_bytes(half.at[pl.ds(0, 600)], ssem.at[4])

    @pl.when(is_owner)
    def _():
        wait_bytes(chunk.at[pl.ds(0, 4)], ssem.at[5])
        wait_bytes(unit_in.at[pl.ds(0, 15)], ssem.at[6])

    @pl.when(jnp.logical_not(is_owner))
    def _():
        wait_bytes(chunk, ssem.at[5])

    wait_bytes(fin.at[core, pl.ds(0, 15)], ssem.at[7])
    wait_bytes(fin.at[core], ssem.at[8])
    keep.wait()


def gram(x, total):
    vm = pl.BlockSpec(memory_space=pltpu.VMEM)
    return pl.pallas_call(
        functools.partial(gram_kernel, total),
        out_shape=(jax.ShapeDtypeStruct((SLOTS, 512, 128), F32), jax.ShapeDtypeStruct((512, 512), F32)),
        in_specs=[vm],
        out_specs=(pl.BlockSpec(memory_space=pl.ANY), vm),
        scratch_shapes=[
            pltpu.VMEM((GROUPS, 32, 128), F32),
            pltpu.VMEM((SLOTS, 512, 128), F32),
            pltpu.VMEM((512, 384), BF16),
            pltpu.VMEM((512, 384), BF16),
            pltpu.VMEM((1280, 128), F32),
            pltpu.VMEM((640, 128), F32),
            pltpu.VMEM((640, 128), F32),
            pltpu.VMEM((CHIPS, 40, 128), F32),
            pltpu.VMEM((Z, 8, 128), F32),
            pltpu.VMEM((UNITS, 8, 128), F32),
            pltpu.VMEM((UNITS, 8, 128), F32),
            pltpu.VMEM((2, CHIPS, UNITS, 8, 128), F32),
            pltpu.SemaphoreType.DMA((9,)),
            pltpu.SemaphoreType.DMA((12,)),
            pltpu.SemaphoreType.DMA((UNITS,)),
            pltpu.SemaphoreType.DMA,
            pltpu.SemaphoreType.REGULAR,
            pltpu.SemaphoreType.REGULAR,
        ],
        compiler_params=pltpu.CompilerParams(
            collective_id=0, has_side_effects=True, vmem_limit_bytes=32 * 1024 * 1024),
    )(x)


RANK = 112
TILES = RANK // 8
PIECES = [(p, q, half) for p, q in ((0, 0), (0, 1), (1, 0), (0, 2), (2, 0), (1, 1)) for half in range(2)]


def spread_out(v):
    return jnp.broadcast_to(v, (8, 128))


def column(tile, k):
    return spread_out(tile[:, k:k + 1])


def row_of(ref, index, i):
    return spread_out(ref[index, i:i + 1, :])


def inverse_factor(a, work, beside):
    sub = lax.broadcasted_iota(jnp.int32, (8, 128), 0)
    lane = lax.broadcasted_iota(jnp.int32, (8, 128), 1)
    left = [a[8 * t:8 * t + 8, :] for t in range(TILES)]
    right = [(lane == sub + 8 * t).astype(F32) for t in range(TILES)]
    result = []
    ahead = None
    for t0 in range(TILES):
        k0 = 8 * t0
        base = (t0 % 2) * 18
        work[base] = left[t0]
        work[base + 1] = right[t0]
        row = [row_of(work, base, i) for i in range(8)]
        row_inv = [row_of(work, base + 1, i) for i in range(8)]
        for j in range(8):
            work[base + 2 + j] = column(left[t0], k0 + j) if ahead is None else ahead[j]
        s = [[row_of(work, base + 2 + j, i) for j in range(i + 1)] for i in range(8)]
        near = range(t0 + 1, min(TILES, t0 + 3))
        far = range(min(TILES, t0 + 3), TILES)
        col = {t: [column(left[t], k0 + j) for j in range(8)] for t in near}
        ahead = [column(left[t0 + 1], k0 + 8 + j) for j in range(8)] if near else None
        beside(t0)
        factors, inverses = [], []
        for j in range(8):
            inv = 1.0 / s[j][j]
            m = [None] * 8
            for i in range(j + 1, 8):
                m[i] = s[i][j] * inv
            factors.append(m)
            inverses.append(inv)
            for i in range(j + 1, 8):
                for n in range(j + 1, i + 1):
                    s[i][n] = s[i][n] - m[i] * s[n][j]
            for i in range(j + 1, 8):
                row[i] = row[i] - m[i] * row[j]
                row_inv[i] = row_inv[i] - m[i] * row_inv[j]
            if near:
                work[base + 10 + j] = col[t0 + 1][j]
                next_row = [row_of(work, base + 10 + j, i) for i in range(8)]
            for t in near:
                x = col[t][j] * inv
                for n in range(j + 1, 8):
                    col[t][n] = col[t][n] - x * s[n][j]
                if t == t0 + 1:
                    ahead = [ahead[n] - x * next_row[n] for n in range(8)]
                left[t] = left[t] - x * row[j]
                right[t] = right[t] - x * row_inv[j]
        tile, pivots = row_inv[7], s[7][7]
        for i in range(7):
            tile = jnp.where(sub == i, row_inv[i], tile)
            pivots = jnp.where(sub == i, s[i][i], pivots)
        result.append(tile * lax.rsqrt(pivots))
        if far:
            back, back_inv = [None] * 8, [None] * 8
            for j in reversed(range(8)):
                u, v = row[j] * inverses[j], row_inv[j] * inverses[j]
                for i in range(j + 1, 8):
                    u = u - factors[j][i] * back[i]
                    v = v - factors[j][i] * back_inv[i]
                back[j], back_inv[j] = u, v
            for t in far:
                u, v = left[t], right[t]
                for j in range(8):
                    c = column(left[t], k0 + j)
                    u = u - c * back[j]
                    v = v - c * back_inv[j]
                left[t], right[t] = u, v
    return jnp.concatenate(result, axis=0)


def split3(v):
    hi = v.astype(BF16)
    rest = v - hi.astype(F32)
    mid = rest.astype(BF16)
    return hi, mid, (rest - mid.astype(F32)).astype(BF16)


def dot_p(a, b):
    return lax.dot_general(a, b, (((1,), (0,)), ((), ())), preferred_element_type=F32)


def full(a, b, mul):
    small = (mul(a[0], b[2]) + mul(a[2], b[0])) + mul(a[1], b[1])
    return mul(a[0], b[0]) + ((mul(a[0], b[1]) + mul(a[1], b[0])) + small)


def turns_kernel(g_ref, s_ref, xt_ref, st_ref, got, image, last, ahead, inverse, parts, work, core_ref, ssem, rsem):
    z, x, y, core = place()
    barrier = pltpu.get_barrier_semaphore()

    def greet(step, carry):
        pl.semaphore_signal(barrier, inc=1, device_id={"gx": partner(z, step)}, device_id_type=MESH)
        return carry

    lax.fori_loop(0, 15, greet, 0)

    for p, part in enumerate(split3(g_ref[...])):
        parts[p] = part
    image[...] = full(split3(s_ref[...]), (parts[0], parts[1], parts[2]), dot_p)
    zeros = jnp.zeros((16, 512), BF16)

    def turn(index, carry):
        now = image[...]
        last[...] = now
        now = split3(now)
        inner = full(now, tuple(jnp.concatenate([v, zeros], axis=0) for v in now), dot_t)

        def beside(t):
            if t < len(PIECES):
                p, q, half = PIECES[t]
                lanes = slice(256 * half, 256 * half + 256)
                piece = dot_p(now[p], parts[q, :, lanes])
                ahead[:, lanes] = piece if p + q == 0 else ahead[:, lanes] + piece

        w = inverse_factor(inner, work, beside)[:, :RANK]
        inverse[...] = w
        image[...] = full(split3(w), split3(ahead[...]), dot_p)
        return carry

    lax.fori_loop(0, ITERS, turn, 0)
    basis = full(split3(inverse[...]), split3(last[...]), dot_p)
    st_ref[...] = basis
    basis_hi, basis_lo = split(basis)
    for slot in range(SLOTS):
        field_hi, field_lo = split(xt_ref[slot])
        part = dot_p(basis_hi, field_hi) + (dot_p(basis_hi, field_lo) + dot_p(basis_lo, field_hi))
        for d in range(Z):
            core_ref[d, slot] = part[7 * d:7 * d + 7, :]

    first = first_group(z, core)
    is_short = short(z, core)
    pl.semaphore_wait(barrier, 15)

    def push(n):
        def one(step, carry):
            d = partner(z, step)
            pltpu.make_async_remote_copy(
                src_ref=core_ref.at[d, pl.ds(0, n)], dst_ref=got.at[pl.ds(first, n)],
                send_sem=ssem, recv_sem=rsem, device_id={"gx": d}, device_id_type=MESH).start()
            return carry

        lax.fori_loop(0, 15, one, 0)
        got[pl.ds(first, n)] = core_ref[z, pl.ds(0, n)]
        wait_bytes(got.at[pl.ds(0, GROUPS - n)], rsem)
        wait_bytes(core_ref.at[pl.ds(0, 15), pl.ds(0, n)], ssem)

    @pl.when(is_short)
    def _():
        push(2)

    @pl.when(jnp.logical_not(is_short))
    def _():
        push(3)


def turns(g, s, xt):
    vm = pl.BlockSpec(memory_space=pltpu.VMEM)
    return pl.pallas_call(
        turns_kernel,
        out_shape=(jax.ShapeDtypeStruct((RANK, 512), F32), jax.ShapeDtypeStruct((GROUPS, 7, 128), F32)),
        in_specs=[vm, vm, vm],
        out_specs=(vm, vm),
        scratch_shapes=[
            pltpu.VMEM((RANK, 512), F32),
            pltpu.VMEM((RANK, 512), F32),
            pltpu.VMEM((RANK, 512), F32),
            pltpu.VMEM((RANK, RANK), F32),
            pltpu.VMEM((3, 512, 512), BF16),
            pltpu.VMEM((36, 8, 128), F32),
            pltpu.VMEM((Z, SLOTS, 7, 128), F32),
            pltpu.SemaphoreType.DMA,
            pltpu.SemaphoreType.DMA,
        ],
        compiler_params=pltpu.CompilerParams(
            collective_id=1, has_side_effects=True, vmem_limit_bytes=32 * 1024 * 1024),
    )(g, s, xt)


def unpack_kernel(st_ref, got_ref, st_out, core_out):
    st_out[...] = st_ref[...]
    for e in range(7):
        for s in range(11):
            core_out[e, s] = got_ref[4 * s:4 * s + 4, e, :]


def unpack(st, got):
    vm = pl.BlockSpec(memory_space=pltpu.VMEM)
    return pl.pallas_call(
        unpack_kernel,
        out_shape=(jax.ShapeDtypeStruct((RANK, 512), F32), jax.ShapeDtypeStruct((7, 11, 4, 128), F32)),
        in_specs=[vm, vm],
        out_specs=(vm, vm),
        compiler_params=pltpu.CompilerParams(vmem_limit_bytes=4 * 1024 * 1024),
    )(st, got)


def per_device(species_field, start_basis):
    total = float(11 * 16 * 1024)
    xt, gram_matrix = gram(species_field.reshape(11, 128, 128), total)
    st, core = unpack(*turns(gram_matrix, start_basis.T, xt))
    return (st.T, core)


def solution(mesh):
    placed = (P(None, "gx", "gy", "gz"), P())
    return jax.shard_map(
        per_device,
        mesh=mesh,
        in_specs=placed,
        out_specs=(P(), P("gx", None, "gy", "gz")),
        check_vma=False,
    )
```

```python
import functools

import jax
import jax.numpy as jnp
from jax import lax
from jax.experimental import pallas as pl
from jax.experimental.pallas import tpu as pltpu
from jax.sharding import PartitionSpec as P

ITERS = 8
MESH = pl.DeviceIdType.MESH
F32 = jnp.float32
BF16 = jnp.bfloat16

Z = 16
GROUPS = 44
SLOTS = 3
CHIPS = 16


def place():
    z = lax.axis_index("gx")
    x = lax.axis_index("gy")
    w = lax.axis_index("gz")
    core = lax.rem(w, 2)
    return z, x, lax.div(w, 2), core


def first_group(dest, core):
    return 3 * dest - lax.div(dest + 3 - 2 * core, 4)


def short(dest, core):
    return lax.rem(dest, 4) == 2 * core


def partner(me, step):
    half = lax.div(step + 1, 2)
    k = 8 + half * (2 * lax.rem(step, 2) - 1)
    return lax.rem(me + k, Z)


def wait_bytes(ref, sem):
    pltpu.make_async_copy(ref, ref, sem).wait()


def split(v):
    hi = v.astype(BF16)
    return hi, (v - hi.astype(F32)).astype(BF16)


def dot_t(a, b):
    return lax.dot_general(a, b, (((1,), (1,)), ((), ())), preferred_element_type=F32)


UNITS = 5


def gram_kernel(total, x_ref, xt_out, g_out, send, recv, hi_ref, lo_ref, part, sib, half, spread,
                unit_in, chunk, mine, fin, ssem, rsem, usem, lsem, token2, token3):
    z, x, y, core = place()
    q = x * 4 + y

    def along_z(k):
        return {"gx": lax.rem(z + k + Z, Z)}

    def chip(p):
        return {"gy": lax.div(p, 4), "gz": lax.rem(p, 4) * 2 + core}

    sibling = {"gz": y * 2 + 1 - core}
    close = [along_z(k) for k in (1, -1, 2, -2)] + [sibling]
    close += [{"gy": lax.rem(x + k, 4)} for k in (1, 2, 3)]
    close += [{"gz": lax.rem(y + k, 4) * 2 + core} for k in (1, 2, 3)]
    barrier = pltpu.get_barrier_semaphore()
    for device in close:
        pl.semaphore_signal(barrier, inc=1, device_id=device, device_id_type=MESH)
    for g in range(GROUPS):
        s, yy = divmod(g, 4)
        send[g] = x_ref[s, pl.ds(yy, 32, stride=4), :]
    pl.semaphore_wait(barrier, len(close))
    for device in close:
        pl.semaphore_signal(token2, inc=1, device_id=device, device_id_type=MESH)

    rows = pl.ds(pl.multiple_of(z * 32, 32), 32)

    def copy_to(slot, d):
        return pltpu.make_async_remote_copy(
            src_ref=send.at[first_group(d, core) + slot],
            dst_ref=recv.at[slot, rows],
            send_sem=ssem.at[slot],
            recv_sem=rsem.at[slot],
            device_id={"gx": d},
            device_id_type=MESH,
        )

    def push(slot, k):
        d = lax.rem(z + k + Z, Z)
        if slot < 2:
            copy_to(slot, d).start()
        else:
            @pl.when(jnp.logical_not(short(d, core)))
            def _():
                copy_to(slot, d).start()

    for slot in range(SLOTS):
        for k in (2, -2, 1, -1):
            push(slot, k)
    pl.semaphore_wait(token2, len(close))
    for k in range(1, 5):
        for sign in (1, -1):
            pl.semaphore_signal(token3, inc=1, device_id=along_z(sign * k), device_id_type=MESH)
    for slot in range(SLOTS):
        for k in (4, -4, 3, -3):
            push(slot, k)
    pl.semaphore_wait(token3, 8)
    for slot in range(SLOTS):
        for k in (8, 7, -7, 6, -6, 5, -5):
            push(slot, k)

    mine_first = first_group(z, core)
    recv[0, rows] = send[mine_first]
    recv[1, rows] = send[mine_first + 1]
    is_short = short(z, core)

    @pl.when(is_short)
    def _():
        recv[2] = jnp.zeros((512, 128), F32)

    @pl.when(jnp.logical_not(is_short))
    def _():
        recv[2, rows] = send[mine_first + 2]

    others = pl.ds(0, 480)

    def accumulate(lanes, first):
        for i in range(4):
            ri = slice(128 * i, 128 * i + 128)
            up = slice(0, 128 * i + 128)
            hi_i, lo_i = hi_ref[ri, lanes], lo_ref[ri, lanes]
            hi_u = hi_ref[up, lanes]
            block = dot_t(hi_i, hi_u) + dot_t(hi_i, lo_ref[up, lanes]) + dot_t(lo_i, hi_u)
            for j in range(i + 1):
                b = i * (i + 1) // 2 + j
                rb = slice(128 * b, 128 * b + 128)
                piece = block[:, 128 * j:128 * j + 128]
                part[rb] = piece if first else part[rb] + piece

    def take(slot):
        hi, lo = split(recv[slot])
        hi_ref[:, 128 * slot:128 * slot + 128] = hi
        lo_ref[:, 128 * slot:128 * slot + 128] = lo

    wait_bytes(recv.at[0, others], rsem.at[0])
    take(0)
    wait_bytes(recv.at[1, others], rsem.at[1])
    take(1)
    accumulate(slice(0, 256), True)

    @pl.when(jnp.logical_not(is_short))
    def _():
        wait_bytes(recv.at[2, others], rsem.at[2])

    take(2)
    accumulate(slice(256, 384), False)
    keep = pltpu.make_async_copy(recv, xt_out, lsem)
    keep.start()

    own_half = pl.ds(pl.multiple_of(core * 640, 8), 640)
    other_half = pl.ds(pl.multiple_of((1 - core) * 640, 8), 640)
    swap = pltpu.make_async_remote_copy(
        src_ref=part.at[other_half], dst_ref=sib, send_sem=ssem.at[3], recv_sem=rsem.at[3],
        device_id=sibling, device_id_type=MESH)
    swap.start()
    swap.wait_recv()
    half[...] = part[own_half] + sib[...]

    def spread_to(step, carry):
        p = lax.rem(q + step + 1, CHIPS)
        pltpu.make_async_remote_copy(
            src_ref=half.at[pl.ds(pl.multiple_of(40 * p, 8), 40)], dst_ref=spread.at[q],
            send_sem=ssem.at[4], recv_sem=rsem.at[4],
            device_id=chip(p), device_id_type=MESH).start()
        return carry

    lax.fori_loop(0, 15, spread_to, 0)
    spread[q] = half[pl.ds(pl.multiple_of(40 * q, 8), 40)]
    wait_bytes(spread.at[pl.ds(0, 15)], rsem.at[4])
    summed = jnp.sum(spread[...], axis=0)
    for t in range(UNITS):
        chunk[t] = summed[8 * t:8 * t + 8]

    is_owner = jnp.logical_and(lax.rem(z, 3) == 0, z < 15)
    own_t = lax.div(z, 3)
    for t in range(UNITS):
        @pl.when(z != 3 * t)
        def _(t=t):
            pltpu.make_async_remote_copy(
                src_ref=chunk.at[t], dst_ref=unit_in.at[z],
                send_sem=ssem.at[5], recv_sem=rsem.at[5],
                device_id={"gx": 3 * t}, device_id_type=MESH).start()

    @pl.when(is_owner)
    def _():
        unit_in[z] = chunk[own_t]
        wait_bytes(unit_in.at[pl.ds(0, 15)], rsem.at[5])
        mine[own_t] = jnp.sum(unit_in[...], axis=0) * (1.0 / total)

        def give(step, carry):
            pltpu.make_async_remote_copy(
                src_ref=mine.at[own_t], dst_ref=mine.at[own_t],
                send_sem=ssem.at[6], recv_sem=usem.at[own_t],
                device_id={"gx": partner(z, step)}, device_id_type=MESH).start()
            return carry

        lax.fori_loop(0, 15, give, 0)

    nearest = lax.div(z + 1, 3)

    def pass_on(i, carry):
        offset = lax.div(i + 1, 2) * (2 * lax.rem(i, 2) - 1)
        t = lax.rem(nearest + offset + UNITS, UNITS)

        @pl.when(jnp.logical_not(jnp.logical_and(is_owner, own_t == t)))
        def _():
            wait_bytes(mine.at[t], usem.at[t])

        def back_to(step, carry):
            p = lax.rem(q + step + 1, CHIPS)
            pltpu.make_async_remote_copy(
                src_ref=mine.at[t], dst_ref=fin.at[core, q, t],
                send_sem=ssem.at[7], recv_sem=rsem.at[6 + i],
                device_id=chip(p), device_id_type=MESH).start()
            return carry

        lax.fori_loop(0, 15, back_to, 0)
        fin[core, q, t] = mine[t]
        return carry

    lax.fori_loop(0, UNITS, pass_on, 0)

    def other_core(i, carry):
        offset = lax.div(i + 1, 2) * (2 * lax.rem(i, 2) - 1)
        t = lax.rem(nearest + offset + UNITS, UNITS)
        wait_bytes(fin.at[core, pl.ds(0, 15), t], rsem.at[6 + i])
        pltpu.make_async_remote_copy(
            src_ref=fin.at[core, :, t], dst_ref=fin.at[core, :, t],
            send_sem=ssem.at[8], recv_sem=rsem.at[11],
            device_id=sibling, device_id_type=MESH).start()
        return carry

    lax.fori_loop(0, UNITS, other_core, 0)
    wait_bytes(fin.at[1 - core], rsem.at[11])

    for i in range(4):
        for j in range(i + 1):
            b = i * (i + 1) // 2 + j
            tiles = []
            for r in range(16 * b, 16 * b + 16):
                h, rest = divmod(r, 80)
                tiles.append(fin[h, rest // UNITS, rest % UNITS])
            block = jnp.concatenate(tiles, axis=0)
            g_out[128 * i:128 * i + 128, 128 * j:128 * j + 128] = block
            if j < i:
                g_out[128 * j:128 * j + 128, 128 * i:128 * i + 128] = block.T

    wait_bytes(send.at[pl.ds(0, 15)], ssem.at[0])
    wait_bytes(send.at[pl.ds(0, 15)], ssem.at[1])

    @pl.when(is_short)
    def _():
        wait_bytes(send.at[pl.ds(0, 12)], ssem.at[2])

    @pl.when(jnp.logical_not(is_short))
    def _():
        wait_bytes(send.at[pl.ds(0, 11)], ssem.at[2])

    swap.wait_send()
    wait_bytes(half.at[pl.ds(0, 600)], ssem.at[4])

    @pl.when(is_owner)
    def _():
        wait_bytes(chunk.at[pl.ds(0, 4)], ssem.at[5])
        wait_bytes(unit_in.at[pl.ds(0, 15)], ssem.at[6])

    @pl.when(jnp.logical_not(is_owner))
    def _():
        wait_bytes(chunk, ssem.at[5])

    wait_bytes(fin.at[core, pl.ds(0, 15)], ssem.at[7])
    wait_bytes(fin.at[core], ssem.at[8])
    keep.wait()


def gram(x, total):
    vm = pl.BlockSpec(memory_space=pltpu.VMEM)
    return pl.pallas_call(
        functools.partial(gram_kernel, total),
        out_shape=(jax.ShapeDtypeStruct((SLOTS, 512, 128), F32), jax.ShapeDtypeStruct((512, 512), F32)),
        in_specs=[vm],
        out_specs=(pl.BlockSpec(memory_space=pl.ANY), vm),
        scratch_shapes=[
            pltpu.VMEM((GROUPS, 32, 128), F32),
            pltpu.VMEM((SLOTS, 512, 128), F32),
            pltpu.VMEM((512, 384), BF16),
            pltpu.VMEM((512, 384), BF16),
            pltpu.VMEM((1280, 128), F32),
            pltpu.VMEM((640, 128), F32),
            pltpu.VMEM((640, 128), F32),
            pltpu.VMEM((CHIPS, 40, 128), F32),
            pltpu.VMEM((Z, 8, 128), F32),
            pltpu.VMEM((UNITS, 8, 128), F32),
            pltpu.VMEM((UNITS, 8, 128), F32),
            pltpu.VMEM((2, CHIPS, UNITS, 8, 128), F32),
            pltpu.SemaphoreType.DMA((9,)),
            pltpu.SemaphoreType.DMA((12,)),
            pltpu.SemaphoreType.DMA((UNITS,)),
            pltpu.SemaphoreType.DMA,
            pltpu.SemaphoreType.REGULAR,
            pltpu.SemaphoreType.REGULAR,
        ],
        compiler_params=pltpu.CompilerParams(
            collective_id=0, has_side_effects=True, vmem_limit_bytes=32 * 1024 * 1024),
    )(x)


RANK = 112
TILES = RANK // 8
PIECES = [(p, q, half) for p, q in ((0, 0), (0, 1), (1, 0), (0, 2), (2, 0), (1, 1)) for half in range(2)]


def spread_out(v):
    return jnp.broadcast_to(v, (8, 128))


def column(tile, k):
    return spread_out(tile[:, k:k + 1])


def row_of(ref, index, i):
    return spread_out(ref[index, i:i + 1, :])


def inverse_factor(a, work, beside):
    sub = lax.broadcasted_iota(jnp.int32, (8, 128), 0)
    lane = lax.broadcasted_iota(jnp.int32, (8, 128), 1)
    left = [a[8 * t:8 * t + 8, :] for t in range(TILES)]
    right = [(lane == sub + 8 * t).astype(F32) for t in range(TILES)]
    result = []
    ahead = None
    for t0 in range(TILES):
        k0 = 8 * t0
        base = (t0 % 2) * 18
        work[base] = left[t0]
        work[base + 1] = right[t0]
        row = [row_of(work, base, i) for i in range(8)]
        row_inv = [row_of(work, base + 1, i) for i in range(8)]
        for j in range(8):
            work[base + 2 + j] = column(left[t0], k0 + j) if ahead is None else ahead[j]
        s = [[row_of(work, base + 2 + j, i) for j in range(i + 1)] for i in range(8)]
        near = range(t0 + 1, min(TILES, t0 + 3))
        far = range(min(TILES, t0 + 3), TILES)
        col = {t: [column(left[t], k0 + j) for j in range(8)] for t in near}
        ahead = [column(left[t0 + 1], k0 + 8 + j) for j in range(8)] if near else None
        beside(t0)
        factors, inverses = [], []
        for j in range(8):
            inv = 1.0 / s[j][j]
            m = [None] * 8
            for i in range(j + 1, 8):
                m[i] = s[i][j] * inv
            factors.append(m)
            inverses.append(inv)
            for i in range(j + 1, 8):
                for n in range(j + 1, i + 1):
                    s[i][n] = s[i][n] - m[i] * s[n][j]
            for i in range(j + 1, 8):
                row[i] = row[i] - m[i] * row[j]
                row_inv[i] = row_inv[i] - m[i] * row_inv[j]
            if near:
                work[base + 10 + j] = col[t0 + 1][j]
                next_row = [row_of(work, base + 10 + j, i) for i in range(8)]
            for t in near:
                x = col[t][j] * inv
                for n in range(j + 1, 8):
                    col[t][n] = col[t][n] - x * s[n][j]
                if t == t0 + 1:
                    ahead = [ahead[n] - x * next_row[n] for n in range(8)]
                left[t] = left[t] - x * row[j]
                right[t] = right[t] - x * row_inv[j]
        tile, pivots = row_inv[7], s[7][7]
        for i in range(7):
            tile = jnp.where(sub == i, row_inv[i], tile)
            pivots = jnp.where(sub == i, s[i][i], pivots)
        result.append(tile * lax.rsqrt(pivots))
        if far:
            back, back_inv = [None] * 8, [None] * 8
            for j in reversed(range(8)):
                u, v = row[j] * inverses[j], row_inv[j] * inverses[j]
                for i in range(j + 1, 8):
                    u = u - factors[j][i] * back[i]
                    v = v - factors[j][i] * back_inv[i]
                back[j], back_inv[j] = u, v
            for t in far:
                u, v = left[t], right[t]
                for j in range(8):
                    c = column(left[t], k0 + j)
                    u = u - c * back[j]
                    v = v - c * back_inv[j]
                left[t], right[t] = u, v
    return jnp.concatenate(result, axis=0)


def split3(v):
    hi = v.astype(BF16)
    rest = v - hi.astype(F32)
    mid = rest.astype(BF16)
    return hi, mid, (rest - mid.astype(F32)).astype(BF16)


def dot_p(a, b):
    return lax.dot_general(a, b, (((1,), (0,)), ((), ())), preferred_element_type=F32)


def full(a, b, mul):
    small = (mul(a[0], b[2]) + mul(a[2], b[0])) + mul(a[1], b[1])
    return mul(a[0], b[0]) + ((mul(a[0], b[1]) + mul(a[1], b[0])) + small)


def turns_kernel(g_ref, s_ref, xt_ref, st_ref, got, image, last, ahead, ahead_parts, inverse, parts, work, core_ref, ssem, rsem):
    z, x, y, core = place()
    barrier = pltpu.get_barrier_semaphore()

    def greet(step, carry):
        pl.semaphore_signal(barrier, inc=1, device_id={"gx": partner(z, step)}, device_id_type=MESH)
        return carry

    lax.fori_loop(0, 15, greet, 0)

    for p, part in enumerate(split3(g_ref[...])):
        parts[p] = part
    image[...] = full(split3(s_ref[...]), (parts[0], parts[1], parts[2]), dot_p)
    zeros = jnp.zeros((16, 512), BF16)
    for p in range(3):
        ahead_parts[p, RANK:] = zeros

    def turn(index, carry):
        now = image[...]
        last[...] = now
        hi, mid, lo = now = split3(now)
        pair = jnp.concatenate([hi, zeros, mid, zeros], axis=0)
        both = dot_t(pair, pair)
        small = dot_t(lo, jnp.concatenate([hi, zeros], axis=0)) + dot_t(hi, jnp.concatenate([lo, zeros], axis=0))
        cross = both[:RANK, 128:] + both[128:128 + RANK, :128]
        inner = both[:RANK, :128] + (cross + (small + both[128:128 + RANK, 128:]))

        def beside(t):
            if t < len(PIECES):
                p, q, half = PIECES[t]
                lanes = slice(256 * half, 256 * half + 256)
                piece = dot_p(now[p], parts[q, :, lanes])
                ahead[:, lanes] = piece if p + q == 0 else ahead[:, lanes] + piece
            elif t == len(PIECES):
                for p, part in enumerate(split3(ahead[...])):
                    ahead_parts[p, :RANK] = part

        w = inverse_factor(inner, work, beside)
        inverse[...] = w[:, :RANK]
        hi, mid, lo = split3(w)
        y_hi, y_mid, y_lo = ahead_parts[0], ahead_parts[1], ahead_parts[2]
        image[...] = dot_p(
            jnp.concatenate([hi, mid, hi, lo, hi, mid], axis=1),
            jnp.concatenate([y_hi, y_hi, y_mid, y_hi, y_lo, y_mid], axis=0),
        )
        return carry

    lax.fori_loop(0, ITERS, turn, 0)
    basis = full(split3(inverse[...]), split3(last[...]), dot_p)
    st_ref[...] = basis
    basis_hi, basis_lo = split(basis)
    for slot in range(SLOTS):
        field_hi, field_lo = split(xt_ref[slot])
        part = dot_p(basis_hi, field_hi) + (dot_p(basis_hi, field_lo) + dot_p(basis_lo, field_hi))
        for d in range(Z):
            core_ref[d, slot] = part[7 * d:7 * d + 7, :]

    first = first_group(z, core)
    is_short = short(z, core)
    pl.semaphore_wait(barrier, 15)

    def push(n):
        def one(step, carry):
            d = partner(z, step)
            pltpu.make_async_remote_copy(
                src_ref=core_ref.at[d, pl.ds(0, n)], dst_ref=got.at[pl.ds(first, n)],
                send_sem=ssem, recv_sem=rsem, device_id={"gx": d}, device_id_type=MESH).start()
            return carry

        lax.fori_loop(0, 15, one, 0)
        got[pl.ds(first, n)] = core_ref[z, pl.ds(0, n)]
        wait_bytes(got.at[pl.ds(0, GROUPS - n)], rsem)
        wait_bytes(core_ref.at[pl.ds(0, 15), pl.ds(0, n)], ssem)

    @pl.when(is_short)
    def _():
        push(2)

    @pl.when(jnp.logical_not(is_short))
    def _():
        push(3)


def turns(g, s, xt):
    vm = pl.BlockSpec(memory_space=pltpu.VMEM)
    return pl.pallas_call(
        turns_kernel,
        out_shape=(jax.ShapeDtypeStruct((RANK, 512), F32), jax.ShapeDtypeStruct((GROUPS, 7, 128), F32)),
        in_specs=[vm, vm, vm],
        out_specs=(vm, vm),
        scratch_shapes=[
            pltpu.VMEM((RANK, 512), F32),
            pltpu.VMEM((RANK, 512), F32),
            pltpu.VMEM((RANK, 512), F32),
            pltpu.VMEM((3, 128, 512), BF16),
            pltpu.VMEM((RANK, RANK), F32),
            pltpu.VMEM((3, 512, 512), BF16),
            pltpu.VMEM((36, 8, 128), F32),
            pltpu.VMEM((Z, SLOTS, 7, 128), F32),
            pltpu.SemaphoreType.DMA,
            pltpu.SemaphoreType.DMA,
        ],
        compiler_params=pltpu.CompilerParams(
            collective_id=1, has_side_effects=True, vmem_limit_bytes=32 * 1024 * 1024),
    )(g, s, xt)


def unpack_kernel(st_ref, got_ref, st_out, core_out):
    st_out[...] = st_ref[...]
    for e in range(7):
        for s in range(11):
            core_out[e, s] = got_ref[4 * s:4 * s + 4, e, :]


def unpack(st, got):
    vm = pl.BlockSpec(memory_space=pltpu.VMEM)
    return pl.pallas_call(
        unpack_kernel,
        out_shape=(jax.ShapeDtypeStruct((RANK, 512), F32), jax.ShapeDtypeStruct((7, 11, 4, 128), F32)),
        in_specs=[vm, vm],
        out_specs=(vm, vm),
        compiler_params=pltpu.CompilerParams(vmem_limit_bytes=4 * 1024 * 1024),
    )(st, got)


def per_device(species_field, start_basis):
    total = float(11 * 16 * 1024)
    xt, gram_matrix = gram(species_field.reshape(11, 128, 128), total)
    st, core = unpack(*turns(gram_matrix, start_basis.T, xt))
    return (st.T, core)


def solution(mesh):
    placed = (P(None, "gx", "gy", "gz"), P())
    return jax.shard_map(
        per_device,
        mesh=mesh,
        in_specs=placed,
        out_specs=(P(), P("gx", None, "gy", "gz")),
        check_vma=False,
    )
```

```python
import functools

import jax
import jax.numpy as jnp
from jax import lax
from jax.experimental import pallas as pl
from jax.experimental.pallas import tpu as pltpu
from jax.sharding import PartitionSpec as P

ITERS = 8
MESH = pl.DeviceIdType.MESH
F32 = jnp.float32
BF16 = jnp.bfloat16

Z = 16
GROUPS = 44
SLOTS = 3
CHIPS = 16


def place():
    z = lax.axis_index("gx")
    x = lax.axis_index("gy")
    w = lax.axis_index("gz")
    core = lax.rem(w, 2)
    return z, x, lax.div(w, 2), core


def first_group(dest, core):
    return 3 * dest - lax.div(dest + 3 - 2 * core, 4)


def short(dest, core):
    return lax.rem(dest, 4) == 2 * core


def partner(me, step):
    half = lax.div(step + 1, 2)
    k = 8 + half * (2 * lax.rem(step, 2) - 1)
    return lax.rem(me + k, Z)


def wait_bytes(ref, sem):
    pltpu.make_async_copy(ref, ref, sem).wait()


def split(v):
    hi = v.astype(BF16)
    return hi, (v - hi.astype(F32)).astype(BF16)


def dot_t(a, b):
    return lax.dot_general(a, b, (((1,), (1,)), ((), ())), preferred_element_type=F32)


UNITS = 5


def gram_kernel(total, x_ref, xt_out, g_out, send, recv, hi_ref, lo_ref, part, sib, half, spread,
                chunk, chunks, mine, fin, ssem, rsem, lsem, token2, token3):
    z, x, y, core = place()
    q = x * 4 + y

    def along_z(k):
        return {"gx": lax.rem(z + k + Z, Z)}

    def chip(p):
        return {"gy": lax.div(p, 4), "gz": lax.rem(p, 4) * 2 + core}

    sibling = {"gz": y * 2 + 1 - core}
    close = [along_z(k) for k in (1, -1, 2, -2)] + [sibling]
    close += [{"gy": lax.rem(x + k, 4)} for k in (1, 2, 3)]
    close += [{"gz": lax.rem(y + k, 4) * 2 + core} for k in (1, 2, 3)]
    barrier = pltpu.get_barrier_semaphore()
    for device in close:
        pl.semaphore_signal(barrier, inc=1, device_id=device, device_id_type=MESH)
    for g in range(GROUPS):
        s, yy = divmod(g, 4)
        send[g] = x_ref[s, pl.ds(yy, 32, stride=4), :]
    pl.semaphore_wait(barrier, len(close))
    for device in close:
        pl.semaphore_signal(token2, inc=1, device_id=device, device_id_type=MESH)

    rows = pl.ds(pl.multiple_of(z * 32, 32), 32)

    def copy_to(slot, d):
        return pltpu.make_async_remote_copy(
            src_ref=send.at[first_group(d, core) + slot],
            dst_ref=recv.at[slot, rows],
            send_sem=ssem.at[slot],
            recv_sem=rsem.at[slot],
            device_id={"gx": d},
            device_id_type=MESH,
        )

    def push(slot, k):
        d = lax.rem(z + k + Z, Z)
        if slot < 2:
            copy_to(slot, d).start()
        else:
            @pl.when(jnp.logical_not(short(d, core)))
            def _():
                copy_to(slot, d).start()

    for slot in range(SLOTS):
        for k in (2, -2, 1, -1):
            push(slot, k)
    pl.semaphore_wait(token2, len(close))
    for k in range(1, 5):
        for sign in (1, -1):
            pl.semaphore_signal(token3, inc=1, device_id=along_z(sign * k), device_id_type=MESH)
    for slot in range(SLOTS):
        for k in (4, -4, 3, -3):
            push(slot, k)
    pl.semaphore_wait(token3, 8)
    for slot in range(SLOTS):
        for k in (8, 7, -7, 6, -6, 5, -5):
            push(slot, k)

    mine_first = first_group(z, core)
    recv[0, rows] = send[mine_first]
    recv[1, rows] = send[mine_first + 1]
    is_short = short(z, core)

    @pl.when(is_short)
    def _():
        recv[2] = jnp.zeros((512, 128), F32)

    @pl.when(jnp.logical_not(is_short))
    def _():
        recv[2, rows] = send[mine_first + 2]

    others = pl.ds(0, 480)

    halves = (((0, 0, 1), (1, 0, 2), (2, 0, 2)), ((2, 2, 3), (3, 0, 4)))

    def accumulate(lanes, first, which):
        for i, j0, j1 in halves[which]:
            ri = slice(128 * i, 128 * i + 128)
            rj = slice(128 * j0, 128 * j1)
            hi_i, lo_i = hi_ref[ri, lanes], lo_ref[ri, lanes]
            hi_j = hi_ref[rj, lanes]
            block = dot_t(hi_i, hi_j) + dot_t(hi_i, lo_ref[rj, lanes]) + dot_t(lo_i, hi_j)
            for j in range(j0, j1):
                b = i * (i + 1) // 2 + j
                rb = slice(128 * b, 128 * b + 128)
                piece = block[:, 128 * (j - j0):128 * (j - j0) + 128]
                part[rb] = piece if first else part[rb] + piece

    def take(slot):
        hi, lo = split(recv[slot])
        hi_ref[:, 128 * slot:128 * slot + 128] = hi
        lo_ref[:, 128 * slot:128 * slot + 128] = lo

    wait_bytes(recv.at[0, others], rsem.at[0])
    take(0)
    wait_bytes(recv.at[1, others], rsem.at[1])
    take(1)
    accumulate(slice(0, 256), True, 0)
    accumulate(slice(0, 256), True, 1)

    @pl.when(jnp.logical_not(is_short))
    def _():
        wait_bytes(recv.at[2, others], rsem.at[2])

    take(2)

    own_half = pl.ds(pl.multiple_of(core * 640, 8), 640)
    other_half = pl.ds(pl.multiple_of((1 - core) * 640, 8), 640)
    swap = pltpu.make_async_remote_copy(
        src_ref=part.at[other_half], dst_ref=sib, send_sem=ssem.at[3], recv_sem=rsem.at[3],
        device_id=sibling, device_id_type=MESH)
    for c in range(2):
        @pl.when(core == c)
        def _(c=c):
            accumulate(slice(256, 384), False, 1 - c)
            swap.start()
            accumulate(slice(256, 384), False, c)

    keep = pltpu.make_async_copy(recv, xt_out, lsem)
    keep.start()
    swap.wait_recv()
    half[...] = (part[own_half] + sib[...]).reshape(CHIPS, UNITS, 8, 128)

    odd = lax.rem(z, 2)
    even_z, odd_z = {"gx": z - odd}, {"gx": z - odd + 1}
    source = q * 2 + odd

    def for_even(p):
        return pltpu.make_async_remote_copy(
            src_ref=half.at[p, pl.ds(0, 3)], dst_ref=spread.at[source], send_sem=ssem.at[4], recv_sem=rsem.at[4],
            device_id=even_z | chip(p), device_id_type=MESH)

    def for_odd(p):
        return pltpu.make_async_remote_copy(
            src_ref=half.at[p, pl.ds(3, 2)], dst_ref=spread.at[source, pl.ds(0, 2)],
            send_sem=ssem.at[5], recv_sem=rsem.at[5],
            device_id=odd_z | chip(p), device_id_type=MESH)

    def spread_to(step, carry):
        p = lax.rem(q + step + 1, CHIPS)
        for_even(p).start()
        for_odd(p).start()
        return carry

    lax.fori_loop(0, 15, spread_to, 0)

    def along(k):
        return {"gx": lax.rem(z + k + Z, Z)}

    def rest(n, first, cross, sum_sem):
        own = pl.ds(0, n)
        spread[source, 0:n] = half[q, first:first + n]
        cross(q).start()
        wait_bytes(spread.at[pl.ds(0, 31), own], sum_sem)
        chunk[0:n] = jnp.sum(spread[:, 0:n], axis=0)

        for k in (8, 6, -6, 4, -4, 2, -2):
            pltpu.make_async_remote_copy(
                src_ref=chunk.at[own], dst_ref=chunks.at[lax.div(z, 2), own],
                send_sem=ssem.at[6], recv_sem=rsem.at[6], device_id=along(k), device_id_type=MESH).start()
        chunks[lax.div(z, 2), 0:n] = chunk[0:n]
        wait_bytes(chunks.at[pl.ds(0, 7), own], rsem.at[6])
        mine[0:n] = jnp.sum(chunks[:, 0:n], axis=0) * (1.0 / total)

        def back(p, z_too, sem):
            return pltpu.make_async_remote_copy(
                src_ref=mine.at[own], dst_ref=fin.at[core, q, pl.ds(first, n)],
                send_sem=ssem.at[sem], recv_sem=rsem.at[sem], device_id=z_too | chip(p), device_id_type=MESH)

        other_z = odd_z if first == 0 else even_z

        def back_to(step, carry):
            p = lax.rem(q + step + 1, CHIPS)
            back(p, other_z, 8).start()
            back(p, {}, 7).start()
            return carry

        lax.fori_loop(0, 15, back_to, 0)
        back(q, other_z, 8).start()
        fin[core, q, first:first + n] = mine[0:n]

        def to_sibling(units):
            return pltpu.make_async_remote_copy(
                src_ref=fin.at[core, :, units], dst_ref=fin.at[core, :, units],
                send_sem=ssem.at[9], recv_sem=rsem.at[9], device_id=sibling, device_id_type=MESH)

        same, other = pl.ds(first, n), pl.ds(3 - first, 5 - n)
        wait_bytes(fin.at[core, pl.ds(0, 15), same], rsem.at[7])
        to_sibling(same).start()
        wait_bytes(fin.at[core, :, other], rsem.at[8])
        to_sibling(other).start()
        wait_bytes(fin.at[1 - core], rsem.at[9])

        wait_bytes(chunks.at[pl.ds(0, 7), own], ssem.at[6])
        wait_bytes(fin.at[core, pl.ds(0, 15), same], ssem.at[7])
        wait_bytes(fin.at[core, :, same], ssem.at[8])

    @pl.when(odd == 0)
    def _():
        rest(3, 0, for_odd, rsem.at[4])
        wait_bytes(half.at[pl.ds(0, 15), pl.ds(0, 3)], ssem.at[4])
        wait_bytes(half.at[:, pl.ds(0, 2)], ssem.at[5])

    @pl.when(odd == 1)
    def _():
        rest(2, 3, for_even, rsem.at[5])
        wait_bytes(half.at[:, pl.ds(0, 3)], ssem.at[4])
        wait_bytes(half.at[pl.ds(0, 15), pl.ds(0, 2)], ssem.at[5])

    for i in range(4):
        for j in range(i + 1):
            b = i * (i + 1) // 2 + j
            tiles = []
            for r in range(16 * b, 16 * b + 16):
                h, rest = divmod(r, 80)
                tiles.append(fin[h, rest // UNITS, rest % UNITS])
            block = jnp.concatenate(tiles, axis=0)
            g_out[128 * i:128 * i + 128, 128 * j:128 * j + 128] = block
            if j < i:
                g_out[128 * j:128 * j + 128, 128 * i:128 * i + 128] = block.T

    wait_bytes(send.at[pl.ds(0, 15)], ssem.at[0])
    wait_bytes(send.at[pl.ds(0, 15)], ssem.at[1])

    @pl.when(is_short)
    def _():
        wait_bytes(send.at[pl.ds(0, 12)], ssem.at[2])

    @pl.when(jnp.logical_not(is_short))
    def _():
        wait_bytes(send.at[pl.ds(0, 11)], ssem.at[2])

    swap.wait_send()
    wait_bytes(fin.at[core], ssem.at[9])
    keep.wait()


def gram(x, total):
    vm = pl.BlockSpec(memory_space=pltpu.VMEM)
    return pl.pallas_call(
        functools.partial(gram_kernel, total),
        out_shape=(jax.ShapeDtypeStruct((SLOTS, 512, 128), F32), jax.ShapeDtypeStruct((512, 512), F32)),
        in_specs=[vm],
        out_specs=(pl.BlockSpec(memory_space=pl.ANY), vm),
        scratch_shapes=[
            pltpu.VMEM((GROUPS, 32, 128), F32),
            pltpu.VMEM((SLOTS, 512, 128), F32),
            pltpu.VMEM((512, 384), BF16),
            pltpu.VMEM((512, 384), BF16),
            pltpu.VMEM((1280, 128), F32),
            pltpu.VMEM((640, 128), F32),
            pltpu.VMEM((CHIPS, UNITS, 8, 128), F32),
            pltpu.VMEM((2 * CHIPS, 3, 8, 128), F32),
            pltpu.VMEM((3, 8, 128), F32),
            pltpu.VMEM((Z // 2, 3, 8, 128), F32),
            pltpu.VMEM((3, 8, 128), F32),
            pltpu.VMEM((2, CHIPS, UNITS, 8, 128), F32),
            pltpu.SemaphoreType.DMA((10,)),
            pltpu.SemaphoreType.DMA((10,)),
            pltpu.SemaphoreType.DMA,
            pltpu.SemaphoreType.REGULAR,
            pltpu.SemaphoreType.REGULAR,
        ],
        compiler_params=pltpu.CompilerParams(
            collective_id=0, has_side_effects=True, vmem_limit_bytes=32 * 1024 * 1024),
    )(x)


RANK = 112
TILES = RANK // 8
PIECES = [(p, q, half) for p, q in ((0, 0), (0, 1), (1, 0), (0, 2), (2, 0), (1, 1)) for half in range(2)]


def spread_out(v):
    return jnp.broadcast_to(v, (8, 128))


def column(tile, k):
    return spread_out(tile[:, k:k + 1])


def row_of(ref, index, i):
    return spread_out(ref[index, i:i + 1, :])


def inverse_factor(a, work, beside):
    sub = lax.broadcasted_iota(jnp.int32, (8, 128), 0)
    lane = lax.broadcasted_iota(jnp.int32, (8, 128), 1)
    left = [a[8 * t:8 * t + 8, :] for t in range(TILES)]
    right = [(lane == sub + 8 * t).astype(F32) for t in range(TILES)]
    result = []
    ahead = None
    for t0 in range(TILES):
        k0 = 8 * t0
        base = (t0 % 2) * 18
        work[base] = left[t0]
        work[base + 1] = right[t0]
        row = [row_of(work, base, i) for i in range(8)]
        row_inv = [row_of(work, base + 1, i) for i in range(8)]
        for j in range(8):
            work[base + 2 + j] = column(left[t0], k0 + j) if ahead is None else ahead[j]
        s = [[row_of(work, base + 2 + j, i) for j in range(i + 1)] for i in range(8)]
        near = range(t0 + 1, min(TILES, t0 + 3))
        far = range(min(TILES, t0 + 3), TILES)
        col = {t: [column(left[t], k0 + j) for j in range(8)] for t in near}
        ahead = [column(left[t0 + 1], k0 + 8 + j) for j in range(8)] if near else None
        beside(t0)
        factors, inverses = [], []
        for j in range(8):
            inv = 1.0 / s[j][j]
            m = [None] * 8
            for i in range(j + 1, 8):
                m[i] = s[i][j] * inv
            factors.append(m)
            inverses.append(inv)
            for i in range(j + 1, 8):
                for n in range(j + 1, i + 1):
                    s[i][n] = s[i][n] - m[i] * s[n][j]
            for i in range(j + 1, 8):
                row[i] = row[i] - m[i] * row[j]
                row_inv[i] = row_inv[i] - m[i] * row_inv[j]
            if near:
                work[base + 10 + j] = col[t0 + 1][j]
                next_row = [row_of(work, base + 10 + j, i) for i in range(8)]
            for t in near:
                x = col[t][j] * inv
                for n in range(j + 1, 8):
                    col[t][n] = col[t][n] - x * s[n][j]
                if t == t0 + 1:
                    ahead = [ahead[n] - x * next_row[n] for n in range(8)]
                left[t] = left[t] - x * row[j]
                right[t] = right[t] - x * row_inv[j]
        tile, pivots = row_inv[7], s[7][7]
        for i in range(7):
            tile = jnp.where(sub == i, row_inv[i], tile)
            pivots = jnp.where(sub == i, s[i][i], pivots)
        result.append(tile * lax.rsqrt(pivots))
        if far:
            back, back_inv = [None] * 8, [None] * 8
            for j in reversed(range(8)):
                u, v = row[j] * inverses[j], row_inv[j] * inverses[j]
                for i in range(j + 1, 8):
                    u = u - factors[j][i] * back[i]
                    v = v - factors[j][i] * back_inv[i]
                back[j], back_inv[j] = u, v
            for t in far:
                u, v = left[t], right[t]
                for j in range(8):
                    c = column(left[t], k0 + j)
                    u = u - c * back[j]
                    v = v - c * back_inv[j]
                left[t], right[t] = u, v
    return jnp.concatenate(result, axis=0)


def split3(v):
    hi = v.astype(BF16)
    rest = v - hi.astype(F32)
    mid = rest.astype(BF16)
    return hi, mid, (rest - mid.astype(F32)).astype(BF16)


def dot_p(a, b):
    return lax.dot_general(a, b, (((1,), (0,)), ((), ())), preferred_element_type=F32)


def full(a, b, mul):
    small = (mul(a[0], b[2]) + mul(a[2], b[0])) + mul(a[1], b[1])
    return mul(a[0], b[0]) + ((mul(a[0], b[1]) + mul(a[1], b[0])) + small)


def turns_kernel(g_ref, s_ref, xt_ref, st_ref, got, image, last, ahead, ahead_parts, inverse, parts, work, core_ref, ssem, rsem):
    z, x, y, core = place()
    barrier = pltpu.get_barrier_semaphore()

    def greet(step, carry):
        pl.semaphore_signal(barrier, inc=1, device_id={"gx": partner(z, step)}, device_id_type=MESH)
        return carry

    lax.fori_loop(0, 15, greet, 0)

    for p, part in enumerate(split3(g_ref[...])):
        parts[p] = part
    image[...] = full(split3(s_ref[...]), (parts[0], parts[1], parts[2]), dot_p)
    zeros = jnp.zeros((16, 512), BF16)
    for p in range(3):
        ahead_parts[p, RANK:] = zeros

    def turn(index, carry):
        now = image[...]
        last[...] = now
        hi, mid, lo = now = split3(now)
        pair = jnp.concatenate([hi, zeros, mid, zeros], axis=0)
        both = dot_t(pair, pair)
        small = dot_t(lo, jnp.concatenate([hi, zeros], axis=0)) + dot_t(hi, jnp.concatenate([lo, zeros], axis=0))
        cross = both[:RANK, 128:] + both[128:128 + RANK, :128]
        inner = both[:RANK, :128] + (cross + (small + both[128:128 + RANK, 128:]))

        def beside(t):
            if t < len(PIECES):
                p, q, half = PIECES[t]
                lanes = slice(256 * half, 256 * half + 256)
                piece = dot_p(now[p], parts[q, :, lanes])
                ahead[:, lanes] = piece if p + q == 0 else ahead[:, lanes] + piece
            elif t == len(PIECES):
                for p, part in enumerate(split3(ahead[...])):
                    ahead_parts[p, :RANK] = part

        w = inverse_factor(inner, work, beside)
        inverse[...] = w[:, :RANK]
        hi, mid, lo = split3(w)
        y_hi, y_mid, y_lo = ahead_parts[0], ahead_parts[1], ahead_parts[2]
        image[...] = dot_p(
            jnp.concatenate([hi, mid, hi, lo, hi, mid], axis=1),
            jnp.concatenate([y_hi, y_hi, y_mid, y_hi, y_lo, y_mid], axis=0),
        )
        return carry

    lax.fori_loop(0, ITERS, turn, 0)
    basis = full(split3(inverse[...]), split3(last[...]), dot_p)
    st_ref[...] = basis
    basis_hi, basis_lo = split(basis)
    for slot in range(SLOTS):
        field_hi, field_lo = split(xt_ref[slot])
        part = dot_p(basis_hi, field_hi) + (dot_p(basis_hi, field_lo) + dot_p(basis_lo, field_hi))
        for d in range(Z):
            core_ref[d, slot] = part[7 * d:7 * d + 7, :]

    first = first_group(z, core)
    is_short = short(z, core)
    pl.semaphore_wait(barrier, 15)

    def push(n):
        def one(step, carry):
            d = partner(z, step)
            pltpu.make_async_remote_copy(
                src_ref=core_ref.at[d, pl.ds(0, n)], dst_ref=got.at[pl.ds(first, n)],
                send_sem=ssem, recv_sem=rsem, device_id={"gx": d}, device_id_type=MESH).start()
            return carry

        lax.fori_loop(0, 15, one, 0)
        got[pl.ds(first, n)] = core_ref[z, pl.ds(0, n)]
        wait_bytes(got.at[pl.ds(0, GROUPS - n)], rsem)
        wait_bytes(core_ref.at[pl.ds(0, 15), pl.ds(0, n)], ssem)

    @pl.when(is_short)
    def _():
        push(2)

    @pl.when(jnp.logical_not(is_short))
    def _():
        push(3)


def turns(g, s, xt):
    vm = pl.BlockSpec(memory_space=pltpu.VMEM)
    return pl.pallas_call(
        turns_kernel,
        out_shape=(jax.ShapeDtypeStruct((RANK, 512), F32), jax.ShapeDtypeStruct((GROUPS, 7, 128), F32)),
        in_specs=[vm, vm, vm],
        out_specs=(vm, vm),
        scratch_shapes=[
            pltpu.VMEM((RANK, 512), F32),
            pltpu.VMEM((RANK, 512), F32),
            pltpu.VMEM((RANK, 512), F32),
            pltpu.VMEM((3, 128, 512), BF16),
            pltpu.VMEM((RANK, RANK), F32),
            pltpu.VMEM((3, 512, 512), BF16),
            pltpu.VMEM((36, 8, 128), F32),
            pltpu.VMEM((Z, SLOTS, 7, 128), F32),
            pltpu.SemaphoreType.DMA,
            pltpu.SemaphoreType.DMA,
        ],
        compiler_params=pltpu.CompilerParams(
            collective_id=1, has_side_effects=True, vmem_limit_bytes=32 * 1024 * 1024),
    )(g, s, xt)


def unpack_kernel(st_ref, got_ref, st_out, core_out):
    st_out[...] = st_ref[...]
    for e in range(7):
        for s in range(11):
            core_out[e, s] = got_ref[4 * s:4 * s + 4, e, :]


def unpack(st, got):
    vm = pl.BlockSpec(memory_space=pltpu.VMEM)
    return pl.pallas_call(
        unpack_kernel,
        out_shape=(jax.ShapeDtypeStruct((RANK, 512), F32), jax.ShapeDtypeStruct((7, 11, 4, 128), F32)),
        in_specs=[vm, vm],
        out_specs=(vm, vm),
        compiler_params=pltpu.CompilerParams(vmem_limit_bytes=4 * 1024 * 1024),
    )(st, got)


def per_device(species_field, start_basis):
    total = float(11 * 16 * 1024)
    xt, gram_matrix = gram(species_field.reshape(11, 128, 128), total)
    st, core = unpack(*turns(gram_matrix, start_basis.T, xt))
    return (st.T, core)


def solution(mesh):
    placed = (P(None, "gx", "gy", "gz"), P())
    return jax.shard_map(
        per_device,
        mesh=mesh,
        in_specs=placed,
        out_specs=(P(), P("gx", None, "gy", "gz")),
        check_vma=False,
    )
```

```python
import functools

import jax
import jax.numpy as jnp
from jax import lax
from jax.experimental import pallas as pl
from jax.experimental.pallas import tpu as pltpu
from jax.sharding import PartitionSpec as P

ITERS = 8
MESH = pl.DeviceIdType.MESH
F32 = jnp.float32
BF16 = jnp.bfloat16

Z = 16
GROUPS = 44
SLOTS = 3
CHIPS = 16


def place():
    z = lax.axis_index("gx")
    x = lax.axis_index("gy")
    w = lax.axis_index("gz")
    core = lax.rem(w, 2)
    return z, x, lax.div(w, 2), core


def first_group(dest, core):
    return 3 * dest - lax.div(dest + 3 - 2 * core, 4)


def short(dest, core):
    return lax.rem(dest, 4) == 2 * core


def partner(me, step):
    half = lax.div(step + 1, 2)
    k = 8 + half * (2 * lax.rem(step, 2) - 1)
    return lax.rem(me + k, Z)


def wait_bytes(ref, sem):
    pltpu.make_async_copy(ref, ref, sem).wait()


def split(v):
    hi = v.astype(BF16)
    return hi, (v - hi.astype(F32)).astype(BF16)


def dot_t(a, b):
    return lax.dot_general(a, b, (((1,), (1,)), ((), ())), preferred_element_type=F32)


UNITS = 5


def gram_part(total, x_hbm, x_ref, g_ref, send, recv, hi_ref, lo_ref, part, sib, half, spread,
              chunk, chunks, mine, fin, ssem, rsem, lsem, token2, token3):
    z, x, y, core = place()
    q = x * 4 + y
    load = pltpu.make_async_copy(x_hbm, x_ref, lsem)
    load.start()

    def along_z(k):
        return {"gx": lax.rem(z + k + Z, Z)}

    def chip(p):
        return {"gy": lax.div(p, 4), "gz": lax.rem(p, 4) * 2 + core}

    sibling = {"gz": y * 2 + 1 - core}
    close = [along_z(k) for k in (1, -1, 2, -2)] + [sibling]
    close += [{"gy": lax.rem(x + k, 4)} for k in (1, 2, 3)]
    close += [{"gz": lax.rem(y + k, 4) * 2 + core} for k in (1, 2, 3)]
    barrier = pltpu.get_barrier_semaphore()
    for device in close:
        pl.semaphore_signal(barrier, inc=1, device_id=device, device_id_type=MESH)
    load.wait()
    for g in range(GROUPS):
        s, yy = divmod(g, 4)
        send[g] = x_ref[s, pl.ds(yy, 32, stride=4), :]
    pl.semaphore_wait(barrier, len(close))
    for device in close:
        pl.semaphore_signal(token2, inc=1, device_id=device, device_id_type=MESH)

    rows = pl.ds(pl.multiple_of(z * 32, 32), 32)

    def copy_to(slot, d):
        return pltpu.make_async_remote_copy(
            src_ref=send.at[first_group(d, core) + slot],
            dst_ref=recv.at[slot, rows],
            send_sem=ssem.at[slot],
            recv_sem=rsem.at[slot],
            device_id={"gx": d},
            device_id_type=MESH,
        )

    def push(slot, k):
        d = lax.rem(z + k + Z, Z)
        if slot < 2:
            copy_to(slot, d).start()
        else:
            @pl.when(jnp.logical_not(short(d, core)))
            def _():
                copy_to(slot, d).start()

    for slot in range(SLOTS):
        for k in (2, -2, 1, -1):
            push(slot, k)
    pl.semaphore_wait(token2, len(close))
    for k in range(1, 5):
        for sign in (1, -1):
            pl.semaphore_signal(token3, inc=1, device_id=along_z(sign * k), device_id_type=MESH)
    for slot in range(SLOTS):
        for k in (4, -4, 3, -3):
            push(slot, k)
    pl.semaphore_wait(token3, 8)
    for slot in range(SLOTS):
        for k in (8, 7, -7, 6, -6, 5, -5):
            push(slot, k)

    mine_first = first_group(z, core)
    recv[0, rows] = send[mine_first]
    recv[1, rows] = send[mine_first + 1]
    is_short = short(z, core)

    @pl.when(is_short)
    def _():
        recv[2] = jnp.zeros((512, 128), F32)

    @pl.when(jnp.logical_not(is_short))
    def _():
        recv[2, rows] = send[mine_first + 2]

    others = pl.ds(0, 480)

    halves = (((0, 0, 1), (1, 0, 2), (2, 0, 2)), ((2, 2, 3), (3, 0, 4)))

    def accumulate(lanes, first, which):
        for i, j0, j1 in halves[which]:
            ri = slice(128 * i, 128 * i + 128)
            rj = slice(128 * j0, 128 * j1)
            hi_i, lo_i = hi_ref[ri, lanes], lo_ref[ri, lanes]
            hi_j = hi_ref[rj, lanes]
            block = dot_t(hi_i, hi_j) + dot_t(hi_i, lo_ref[rj, lanes]) + dot_t(lo_i, hi_j)
            for j in range(j0, j1):
                b = i * (i + 1) // 2 + j
                rb = slice(128 * b, 128 * b + 128)
                piece = block[:, 128 * (j - j0):128 * (j - j0) + 128]
                part[rb] = piece if first else part[rb] + piece

    def take(slot):
        hi, lo = split(recv[slot])
        hi_ref[:, 128 * slot:128 * slot + 128] = hi
        lo_ref[:, 128 * slot:128 * slot + 128] = lo

    wait_bytes(recv.at[0, others], rsem.at[0])
    take(0)
    wait_bytes(recv.at[1, others], rsem.at[1])
    take(1)
    accumulate(slice(0, 256), True, 0)
    accumulate(slice(0, 256), True, 1)

    @pl.when(jnp.logical_not(is_short))
    def _():
        wait_bytes(recv.at[2, others], rsem.at[2])

    take(2)

    own_half = pl.ds(pl.multiple_of(core * 640, 8), 640)
    other_half = pl.ds(pl.multiple_of((1 - core) * 640, 8), 640)
    swap = pltpu.make_async_remote_copy(
        src_ref=part.at[other_half], dst_ref=sib, send_sem=ssem.at[3], recv_sem=rsem.at[3],
        device_id=sibling, device_id_type=MESH)
    for c in range(2):
        @pl.when(core == c)
        def _(c=c):
            accumulate(slice(256, 384), False, 1 - c)
            swap.start()
            accumulate(slice(256, 384), False, c)

    swap.wait_recv()
    half[...] = (part[own_half] + sib[...]).reshape(CHIPS, UNITS, 8, 128)

    odd = lax.rem(z, 2)
    even_z, odd_z = {"gx": z - odd}, {"gx": z - odd + 1}
    source = q * 2 + odd

    def for_even(p):
        return pltpu.make_async_remote_copy(
            src_ref=half.at[p, pl.ds(0, 3)], dst_ref=spread.at[source], send_sem=ssem.at[4], recv_sem=rsem.at[4],
            device_id=even_z | chip(p), device_id_type=MESH)

    def for_odd(p):
        return pltpu.make_async_remote_copy(
            src_ref=half.at[p, pl.ds(3, 2)], dst_ref=spread.at[source, pl.ds(0, 2)],
            send_sem=ssem.at[5], recv_sem=rsem.at[5],
            device_id=odd_z | chip(p), device_id_type=MESH)

    def spread_to(step, carry):
        p = lax.rem(q + step + 1, CHIPS)
        for_even(p).start()
        for_odd(p).start()
        return carry

    lax.fori_loop(0, 15, spread_to, 0)

    def along(k):
        return {"gx": lax.rem(z + k + Z, Z)}

    def rest(n, first, cross, sum_sem):
        own = pl.ds(0, n)
        spread[source, 0:n] = half[q, first:first + n]
        cross(q).start()
        wait_bytes(spread.at[pl.ds(0, 31), own], sum_sem)
        chunk[0:n] = jnp.sum(spread[:, 0:n], axis=0)

        for k in (8, 6, -6, 4, -4, 2, -2):
            pltpu.make_async_remote_copy(
                src_ref=chunk.at[own], dst_ref=chunks.at[lax.div(z, 2), own],
                send_sem=ssem.at[6], recv_sem=rsem.at[6], device_id=along(k), device_id_type=MESH).start()
        chunks[lax.div(z, 2), 0:n] = chunk[0:n]
        wait_bytes(chunks.at[pl.ds(0, 7), own], rsem.at[6])
        mine[0:n] = jnp.sum(chunks[:, 0:n], axis=0) * (1.0 / total)

        def back(p, z_too, sem):
            return pltpu.make_async_remote_copy(
                src_ref=mine.at[own], dst_ref=fin.at[core, q, pl.ds(first, n)],
                send_sem=ssem.at[sem], recv_sem=rsem.at[sem], device_id=z_too | chip(p), device_id_type=MESH)

        other_z = odd_z if first == 0 else even_z

        def back_to(step, carry):
            p = lax.rem(q + step + 1, CHIPS)
            back(p, other_z, 8).start()
            back(p, {}, 7).start()
            return carry

        lax.fori_loop(0, 15, back_to, 0)
        back(q, other_z, 8).start()
        fin[core, q, first:first + n] = mine[0:n]

        def to_sibling(units):
            return pltpu.make_async_remote_copy(
                src_ref=fin.at[core, :, units], dst_ref=fin.at[core, :, units],
                send_sem=ssem.at[9], recv_sem=rsem.at[9], device_id=sibling, device_id_type=MESH)

        same, other = pl.ds(first, n), pl.ds(3 - first, 5 - n)
        wait_bytes(fin.at[core, pl.ds(0, 15), same], rsem.at[7])
        to_sibling(same).start()
        wait_bytes(fin.at[core, :, other], rsem.at[8])
        to_sibling(other).start()
        wait_bytes(fin.at[1 - core], rsem.at[9])

        wait_bytes(chunks.at[pl.ds(0, 7), own], ssem.at[6])
        wait_bytes(fin.at[core, pl.ds(0, 15), same], ssem.at[7])
        wait_bytes(fin.at[core, :, same], ssem.at[8])

    @pl.when(odd == 0)
    def _():
        rest(3, 0, for_odd, rsem.at[4])
        wait_bytes(half.at[pl.ds(0, 15), pl.ds(0, 3)], ssem.at[4])
        wait_bytes(half.at[:, pl.ds(0, 2)], ssem.at[5])

    @pl.when(odd == 1)
    def _():
        rest(2, 3, for_even, rsem.at[5])
        wait_bytes(half.at[:, pl.ds(0, 3)], ssem.at[4])
        wait_bytes(half.at[pl.ds(0, 15), pl.ds(0, 2)], ssem.at[5])

    for i in range(4):
        for j in range(i + 1):
            b = i * (i + 1) // 2 + j
            tiles = []
            for r in range(16 * b, 16 * b + 16):
                h, rest = divmod(r, 80)
                tiles.append(fin[h, rest // UNITS, rest % UNITS])
            block = jnp.concatenate(tiles, axis=0)
            g_ref[128 * i:128 * i + 128, 128 * j:128 * j + 128] = block
            if j < i:
                g_ref[128 * j:128 * j + 128, 128 * i:128 * i + 128] = block.T

    wait_bytes(send.at[pl.ds(0, 15)], ssem.at[0])
    wait_bytes(send.at[pl.ds(0, 15)], ssem.at[1])

    @pl.when(is_short)
    def _():
        wait_bytes(send.at[pl.ds(0, 12)], ssem.at[2])

    @pl.when(jnp.logical_not(is_short))
    def _():
        wait_bytes(send.at[pl.ds(0, 11)], ssem.at[2])

    swap.wait_send()
    wait_bytes(fin.at[core], ssem.at[9])


RANK = 112
TILES = RANK // 8
PIECES = [(p, q, half) for p, q in ((0, 0), (0, 1), (1, 0), (0, 2), (2, 0), (1, 1)) for half in range(2)]


def spread_out(v):
    return jnp.broadcast_to(v, (8, 128))


def column(tile, k):
    return spread_out(tile[:, k:k + 1])


def row_of(ref, index, i):
    return spread_out(ref[index, i:i + 1, :])


NEAR = 3


def inverse_factor(a, work, beside):
    sub = lax.broadcasted_iota(jnp.int32, (8, 128), 0)
    lane = lax.broadcasted_iota(jnp.int32, (8, 128), 1)
    tiles = [a[8 * t:8 * t + 8, :] for t in range(TILES)]
    result = []
    ahead = None
    for t0 in range(TILES):
        k0 = 8 * t0
        base = (t0 % 2) * 18
        in_block = (lane >= k0) & (lane < k0 + 8)
        work[base] = jnp.where(in_block, (lane == sub + k0).astype(F32), tiles[t0])
        row = [row_of(work, base, i) for i in range(8)]
        for j in range(8):
            work[base + 2 + j] = column(tiles[t0], k0 + j) if ahead is None else ahead[j]
        s = [[row_of(work, base + 2 + j, i) for j in range(i + 1)] for i in range(8)]
        near = range(t0 + 1, min(TILES, t0 + 1 + NEAR))
        far = range(min(TILES, t0 + 1 + NEAR), TILES)
        col = {t: [column(tiles[t], k0 + j) for j in range(8)] for t in near}
        ahead = [column(tiles[t0 + 1], k0 + 8 + j) for j in range(8)] if near else None
        for t in near:
            tiles[t] = jnp.where(in_block, 0.0, tiles[t])
        beside(t0)
        factors, inverses = [], []
        for j in range(8):
            inv = 1.0 / s[j][j]
            m = [None] * 8
            for i in range(j + 1, 8):
                m[i] = s[i][j] * inv
            factors.append(m)
            inverses.append(inv)
            for i in range(j + 1, 8):
                for n in range(j + 1, i + 1):
                    s[i][n] = s[i][n] - m[i] * s[n][j]
            for i in range(j + 1, 8):
                row[i] = row[i] - m[i] * row[j]
            if near:
                work[base + 10 + j] = col[t0 + 1][j]
                next_row = [row_of(work, base + 10 + j, i) for i in range(8)]
            for t in near:
                x = col[t][j] * inv
                for n in range(j + 1, 8):
                    col[t][n] = col[t][n] - x * s[n][j]
                if t == t0 + 1:
                    ahead = [ahead[n] - x * next_row[n] for n in range(8)]
                tiles[t] = tiles[t] - x * row[j]
        tile, pivots = row[7], s[7][7]
        for i in range(7):
            tile = jnp.where(sub == i, row[i], tile)
            pivots = jnp.where(sub == i, s[i][i], pivots)
        result.append(jnp.where(lane < k0 + 8, tile * lax.rsqrt(pivots), 0.0))
        if far:
            back = [None] * 8
            for j in reversed(range(8)):
                u = row[j] * inverses[j]
                for i in range(j + 1, 8):
                    u = u - factors[j][i] * back[i]
                back[j] = u
            for t in far:
                u = jnp.where(in_block, 0.0, tiles[t])
                for j in range(8):
                    u = u - column(tiles[t], k0 + j) * back[j]
                tiles[t] = u
    return jnp.concatenate(result, axis=0)


def split3(v):
    hi = v.astype(BF16)
    rest = v - hi.astype(F32)
    mid = rest.astype(BF16)
    return hi, mid, (rest - mid.astype(F32)).astype(BF16)


def dot_p(a, b):
    return lax.dot_general(a, b, (((1,), (0,)), ((), ())), preferred_element_type=F32)


def full(a, b, mul):
    small = (mul(a[0], b[2]) + mul(a[2], b[0])) + mul(a[1], b[1])
    return mul(a[0], b[0]) + ((mul(a[0], b[1]) + mul(a[1], b[0])) + small)


def turns_part(g_ref, s_ref, xt_ref, st_ref, got, image, last, ahead, ahead_parts, inverse, parts, work, core_ref,
               ssem, rsem):
    z, x, y, core = place()

    for p, part in enumerate(split3(g_ref[...])):
        parts[p] = part
    image[...] = full(split3(s_ref[...]), (parts[0], parts[1], parts[2]), dot_p)
    zeros = jnp.zeros((16, 512), BF16)
    for p in range(3):
        ahead_parts[p, RANK:] = zeros

    def turn(index, carry):
        now = image[...]
        last[...] = now
        hi, mid, lo = now = split3(now)
        pair = jnp.concatenate([hi, zeros, mid, zeros], axis=0)
        both = dot_t(pair, pair)
        small = dot_t(lo, jnp.concatenate([hi, zeros], axis=0)) + dot_t(hi, jnp.concatenate([lo, zeros], axis=0))
        cross = both[:RANK, 128:] + both[128:128 + RANK, :128]
        inner = both[:RANK, :128] + (cross + (small + both[128:128 + RANK, 128:]))

        def beside(t):
            if t < len(PIECES):
                p, q, half = PIECES[t]
                lanes = slice(256 * half, 256 * half + 256)
                piece = dot_p(now[p], parts[q, :, lanes])
                ahead[:, lanes] = piece if p + q == 0 else ahead[:, lanes] + piece
            elif t == len(PIECES):
                for p, part in enumerate(split3(ahead[...])):
                    ahead_parts[p, :RANK] = part

        w = inverse_factor(inner, work, beside)
        inverse[...] = w[:, :RANK]
        hi, mid, lo = split3(w)
        y_hi, y_mid, y_lo = ahead_parts[0], ahead_parts[1], ahead_parts[2]
        image[...] = dot_p(
            jnp.concatenate([hi, mid, hi, lo, hi, mid], axis=1),
            jnp.concatenate([y_hi, y_hi, y_mid, y_hi, y_lo, y_mid], axis=0),
        )
        return carry

    lax.fori_loop(0, ITERS, turn, 0)
    basis = full(split3(inverse[...]), split3(last[...]), dot_p)
    basis_hi, basis_lo = split(basis)

    def project(slot):
        field_hi, field_lo = split(xt_ref[slot])
        part = dot_p(basis_hi, field_hi) + (dot_p(basis_hi, field_lo) + dot_p(basis_lo, field_hi))
        for d in range(Z):
            core_ref[d, slot] = part[7 * d:7 * d + 7, :]

    first = first_group(z, core)
    is_short = short(z, core)

    def push(slot, n):
        def one(step, carry):
            d = partner(z, step)
            pltpu.make_async_remote_copy(
                src_ref=core_ref.at[d, pl.ds(slot, n)], dst_ref=got.at[pl.ds(first + slot, n)],
                send_sem=ssem, recv_sem=rsem, device_id={"gx": d}, device_id_type=MESH).start()
            return carry

        lax.fori_loop(0, 15, one, 0)

    def finish(n):
        push(1, n - 1)
        got[pl.ds(first, n)] = core_ref[z, pl.ds(0, n)]
        st_ref[...] = basis
        wait_bytes(got.at[pl.ds(0, GROUPS - n)], rsem)
        wait_bytes(core_ref.at[pl.ds(0, 15), pl.ds(0, n)], ssem)

    project(0)
    push(0, 1)
    project(1)
    project(2)

    @pl.when(is_short)
    def _():
        finish(2)

    @pl.when(jnp.logical_not(is_short))
    def _():
        finish(3)


def step_kernel(total, x_hbm, s_hbm, st_ref, got, s_ref, s_sem, *scratch):
    recv, g_ref = scratch[3], scratch[1]
    load = pltpu.make_async_copy(s_hbm, s_ref, s_sem)
    load.start()
    gram_part(total, x_hbm, *scratch[:19])
    load.wait()
    turns_part(g_ref, s_ref, recv, st_ref, got, *scratch[19:])


def step(x, s, total):
    vm = pl.BlockSpec(memory_space=pltpu.VMEM)
    return pl.pallas_call(
        functools.partial(step_kernel, total),
        out_shape=(jax.ShapeDtypeStruct((RANK, 512), F32), jax.ShapeDtypeStruct((GROUPS, 7, 128), F32)),
        in_specs=[pl.BlockSpec(memory_space=pl.ANY)] * 2,
        out_specs=(vm, vm),
        scratch_shapes=[
            pltpu.VMEM((RANK, 512), F32),
            pltpu.SemaphoreType.DMA,
            pltpu.VMEM((11, 128, 128), F32),
            pltpu.VMEM((512, 512), F32),
            pltpu.VMEM((GROUPS, 32, 128), F32),
            pltpu.VMEM((SLOTS, 512, 128), F32),
            pltpu.VMEM((512, 384), BF16),
            pltpu.VMEM((512, 384), BF16),
            pltpu.VMEM((1280, 128), F32),
            pltpu.VMEM((640, 128), F32),
            pltpu.VMEM((CHIPS, UNITS, 8, 128), F32),
            pltpu.VMEM((2 * CHIPS, 3, 8, 128), F32),
            pltpu.VMEM((3, 8, 128), F32),
            pltpu.VMEM((Z // 2, 3, 8, 128), F32),
            pltpu.VMEM((3, 8, 128), F32),
            pltpu.VMEM((2, CHIPS, UNITS, 8, 128), F32),
            pltpu.SemaphoreType.DMA((10,)),
            pltpu.SemaphoreType.DMA((10,)),
            pltpu.SemaphoreType.DMA,
            pltpu.SemaphoreType.REGULAR,
            pltpu.SemaphoreType.REGULAR,
            pltpu.VMEM((RANK, 512), F32),
            pltpu.VMEM((RANK, 512), F32),
            pltpu.VMEM((RANK, 512), F32),
            pltpu.VMEM((3, 128, 512), BF16),
            pltpu.VMEM((RANK, RANK), F32),
            pltpu.VMEM((3, 512, 512), BF16),
            pltpu.VMEM((36, 8, 128), F32),
            pltpu.VMEM((Z, SLOTS, 7, 128), F32),
            pltpu.SemaphoreType.DMA,
            pltpu.SemaphoreType.DMA,
        ],
        compiler_params=pltpu.CompilerParams(
            collective_id=0, has_side_effects=True, vmem_limit_bytes=(64 * 1024 - 10816) * 1024),
    )(x, s)


def unpack_kernel(st_ref, got_ref, st_out, core_out):
    st_out[...] = st_ref[...]
    for e in range(7):
        for s in range(11):
            core_out[e, s] = got_ref[4 * s:4 * s + 4, e, :]


def unpack(st, got):
    vm = pl.BlockSpec(memory_space=pltpu.VMEM)
    return pl.pallas_call(
        unpack_kernel,
        out_shape=(jax.ShapeDtypeStruct((RANK, 512), F32), jax.ShapeDtypeStruct((7, 11, 4, 128), F32)),
        in_specs=[vm, vm],
        out_specs=(vm, vm),
        compiler_params=pltpu.CompilerParams(vmem_limit_bytes=4 * 1024 * 1024),
    )(st, got)


def per_device(species_field, start_basis):
    total = float(11 * 16 * 1024)
    st, core = unpack(*step(species_field.reshape(11, 128, 128), start_basis.T, total))
    return (st.T, core)


def solution(mesh):
    placed = (P(None, "gx", "gy", "gz"), P())
    return jax.shard_map(
        per_device,
        mesh=mesh,
        in_specs=placed,
        out_specs=(P(), P("gx", None, "gy", "gz")),
        check_vma=False,
    )
```

```python
import functools

import jax
import jax.numpy as jnp
from jax import lax
from jax.experimental import pallas as pl
from jax.experimental.pallas import tpu as pltpu
from jax.sharding import PartitionSpec as P

ITERS = 8
MESH = pl.DeviceIdType.MESH
F32 = jnp.float32
BF16 = jnp.bfloat16

Z = 16
GROUPS = 44
SLOTS = 3
CHIPS = 16


def place():
    z = lax.axis_index("gx")
    x = lax.axis_index("gy")
    w = lax.axis_index("gz")
    core = lax.rem(w, 2)
    return z, x, lax.div(w, 2), core


def first_group(dest, core):
    return 3 * dest - lax.div(dest + 3 - 2 * core, 4)


def short(dest, core):
    return lax.rem(dest, 4) == 2 * core


def partner(me, step):
    half = lax.div(step + 1, 2)
    k = 8 + half * (2 * lax.rem(step, 2) - 1)
    return lax.rem(me + k, Z)


def wait_bytes(ref, sem):
    pltpu.make_async_copy(ref, ref, sem).wait()


def split(v):
    hi = v.astype(BF16)
    return hi, (v - hi.astype(F32)).astype(BF16)


def dot_t(a, b):
    return lax.dot_general(a, b, (((1,), (1,)), ((), ())), preferred_element_type=F32)


OFFSETS = [(2, 2), (2, 1), (2, 3), (1, 2), (3, 2), (2, 0), (0, 2), (1, 1), (1, 3), (3, 1), (3, 3), (1, 0), (3, 0), (0, 1), (0, 3)]
UNITS = 5


def gram_part(total, x_hbm, x_ref, g_ref, send, recv, hi_ref, lo_ref, part, sib, half, spread,
              chunk, chunks, mine, fin, ssem, rsem, lsem, token2, token3):
    z, x, y, core = place()
    q = x * 4 + y
    load = pltpu.make_async_copy(x_hbm, x_ref, lsem)
    load.start()

    def along_z(k):
        return {"gx": lax.rem(z + k + Z, Z)}

    def chip(p):
        return {"gy": lax.div(p, 4), "gz": lax.rem(p, 4) * 2 + core}

    sibling = {"gz": y * 2 + 1 - core}
    close = [along_z(k) for k in (1, -1, 2, -2)] + [sibling]
    close += [{"gy": lax.rem(x + k, 4)} for k in (1, 2, 3)]
    close += [{"gz": lax.rem(y + k, 4) * 2 + core} for k in (1, 2, 3)]
    barrier = pltpu.get_barrier_semaphore()
    for device in close:
        pl.semaphore_signal(barrier, inc=1, device_id=device, device_id_type=MESH)
    load.wait()
    for g in range(GROUPS):
        s, yy = divmod(g, 4)
        send[g] = x_ref[s, pl.ds(yy, 32, stride=4), :]
    pl.semaphore_wait(barrier, len(close))
    for device in close:
        pl.semaphore_signal(token2, inc=1, device_id=device, device_id_type=MESH)

    rows = pl.ds(pl.multiple_of(z * 32, 32), 32)

    def copy_to(slot, d):
        return pltpu.make_async_remote_copy(
            src_ref=send.at[first_group(d, core) + slot],
            dst_ref=recv.at[slot, rows],
            send_sem=ssem.at[slot],
            recv_sem=rsem.at[slot],
            device_id={"gx": d},
            device_id_type=MESH,
        )

    def push(slot, k):
        d = lax.rem(z + k + Z, Z)
        if slot < 2:
            copy_to(slot, d).start()
        else:
            @pl.when(jnp.logical_not(short(d, core)))
            def _():
                copy_to(slot, d).start()

    for slot in range(SLOTS):
        for k in (2, -2, 1, -1):
            push(slot, k)
    pl.semaphore_wait(token2, len(close))
    for k in range(1, 5):
        for sign in (1, -1):
            pl.semaphore_signal(token3, inc=1, device_id=along_z(sign * k), device_id_type=MESH)
    for slot in range(SLOTS):
        for k in (4, -4, 3, -3):
            push(slot, k)
    pl.semaphore_wait(token3, 8)
    for slot in range(SLOTS):
        for k in (8, 7, -7, 6, -6, 5, -5):
            push(slot, k)

    mine_first = first_group(z, core)
    recv[0, rows] = send[mine_first]
    recv[1, rows] = send[mine_first + 1]
    is_short = short(z, core)

    @pl.when(is_short)
    def _():
        recv[2] = jnp.zeros((512, 128), F32)

    @pl.when(jnp.logical_not(is_short))
    def _():
        recv[2, rows] = send[mine_first + 2]

    others = pl.ds(0, 480)

    halves = (((0, 0, 1), (1, 0, 2), (2, 0, 2)), ((2, 2, 3), (3, 0, 4)))

    def accumulate(lanes, first, which):
        for i, j0, j1 in halves[which]:
            ri = slice(128 * i, 128 * i + 128)
            rj = slice(128 * j0, 128 * j1)
            hi_i, lo_i = hi_ref[ri, lanes], lo_ref[ri, lanes]
            hi_j = hi_ref[rj, lanes]
            block = dot_t(hi_i, hi_j) + dot_t(hi_i, lo_ref[rj, lanes]) + dot_t(lo_i, hi_j)
            for j in range(j0, j1):
                b = i * (i + 1) // 2 + j
                rb = slice(128 * b, 128 * b + 128)
                piece = block[:, 128 * (j - j0):128 * (j - j0) + 128]
                part[rb] = piece if first else part[rb] + piece

    def take(slot):
        hi, lo = split(recv[slot])
        hi_ref[:, 128 * slot:128 * slot + 128] = hi
        lo_ref[:, 128 * slot:128 * slot + 128] = lo

    wait_bytes(recv.at[0, others], rsem.at[0])
    take(0)
    wait_bytes(recv.at[1, others], rsem.at[1])
    take(1)
    accumulate(slice(0, 256), True, 0)
    accumulate(slice(0, 256), True, 1)

    @pl.when(jnp.logical_not(is_short))
    def _():
        wait_bytes(recv.at[2, others], rsem.at[2])

    take(2)

    own_half = pl.ds(pl.multiple_of(core * 640, 8), 640)
    other_half = pl.ds(pl.multiple_of((1 - core) * 640, 8), 640)
    swap = pltpu.make_async_remote_copy(
        src_ref=part.at[other_half], dst_ref=sib, send_sem=ssem.at[3], recv_sem=rsem.at[3],
        device_id=sibling, device_id_type=MESH)
    for c in range(2):
        @pl.when(core == c)
        def _(c=c):
            accumulate(slice(256, 384), False, 1 - c)
            swap.start()
            accumulate(slice(256, 384), False, c)

    swap.wait_recv()
    half[...] = (part[own_half] + sib[...]).reshape(CHIPS, UNITS, 8, 128)

    odd = lax.rem(z, 2)
    even_z, odd_z = {"gx": z - odd}, {"gx": z - odd + 1}
    source = q * 2 + odd

    def for_even(p):
        return pltpu.make_async_remote_copy(
            src_ref=half.at[p, pl.ds(0, 3)], dst_ref=spread.at[source], send_sem=ssem.at[4], recv_sem=rsem.at[4],
            device_id=even_z | chip(p), device_id_type=MESH)

    def for_odd(p):
        return pltpu.make_async_remote_copy(
            src_ref=half.at[p, pl.ds(3, 2)], dst_ref=spread.at[source, pl.ds(0, 2)],
            send_sem=ssem.at[5], recv_sem=rsem.at[5],
            device_id=odd_z | chip(p), device_id_type=MESH)

    def others_of_layer():
        return [lax.rem(x + ox, 4) * 4 + lax.rem(y + oy, 4) for ox, oy in OFFSETS]

    for p in others_of_layer():
        for_even(p).start()
        for_odd(p).start()

    def along(k):
        return {"gx": lax.rem(z + k + Z, Z)}

    def rest(n, first, cross, sum_sem):
        own = pl.ds(0, n)
        spread[source, 0:n] = half[q, first:first + n]
        cross(q).start()
        wait_bytes(spread.at[pl.ds(0, 31), own], sum_sem)
        chunk[0:n] = jnp.sum(spread[:, 0:n], axis=0)

        for k in (8, 6, -6, 4, -4, 2, -2):
            pltpu.make_async_remote_copy(
                src_ref=chunk.at[own], dst_ref=chunks.at[lax.div(z, 2), own],
                send_sem=ssem.at[6], recv_sem=rsem.at[6], device_id=along(k), device_id_type=MESH).start()
        chunks[lax.div(z, 2), 0:n] = chunk[0:n]
        wait_bytes(chunks.at[pl.ds(0, 7), own], rsem.at[6])
        mine[0:n] = jnp.sum(chunks[:, 0:n], axis=0) * (1.0 / total)

        def back(p, z_too, sem):
            return pltpu.make_async_remote_copy(
                src_ref=mine.at[own], dst_ref=fin.at[core, q, pl.ds(first, n)],
                send_sem=ssem.at[sem], recv_sem=rsem.at[sem], device_id=z_too | chip(p), device_id_type=MESH)

        other_z = odd_z if first == 0 else even_z

        for p in others_of_layer():
            back(p, other_z, 8).start()
            back(p, {}, 7).start()
        back(q, other_z, 8).start()
        fin[core, q, first:first + n] = mine[0:n]

        def to_sibling(units):
            return pltpu.make_async_remote_copy(
                src_ref=fin.at[core, :, units], dst_ref=fin.at[core, :, units],
                send_sem=ssem.at[9], recv_sem=rsem.at[9], device_id=sibling, device_id_type=MESH)

        same, other = pl.ds(first, n), pl.ds(3 - first, 5 - n)
        wait_bytes(fin.at[core, pl.ds(0, 15), same], rsem.at[7])
        to_sibling(same).start()
        wait_bytes(fin.at[core, :, other], rsem.at[8])
        to_sibling(other).start()
        wait_bytes(fin.at[1 - core], rsem.at[9])

        wait_bytes(chunks.at[pl.ds(0, 7), own], ssem.at[6])
        wait_bytes(fin.at[core, pl.ds(0, 15), same], ssem.at[7])
        wait_bytes(fin.at[core, :, same], ssem.at[8])

    @pl.when(odd == 0)
    def _():
        rest(3, 0, for_odd, rsem.at[4])
        wait_bytes(half.at[pl.ds(0, 15), pl.ds(0, 3)], ssem.at[4])
        wait_bytes(half.at[:, pl.ds(0, 2)], ssem.at[5])

    @pl.when(odd == 1)
    def _():
        rest(2, 3, for_even, rsem.at[5])
        wait_bytes(half.at[:, pl.ds(0, 3)], ssem.at[4])
        wait_bytes(half.at[pl.ds(0, 15), pl.ds(0, 2)], ssem.at[5])

    for i in range(4):
        for j in range(i + 1):
            b = i * (i + 1) // 2 + j
            tiles = []
            for r in range(16 * b, 16 * b + 16):
                h, rest = divmod(r, 80)
                tiles.append(fin[h, rest // UNITS, rest % UNITS])
            block = jnp.concatenate(tiles, axis=0)
            g_ref[128 * i:128 * i + 128, 128 * j:128 * j + 128] = block
            if j < i:
                g_ref[128 * j:128 * j + 128, 128 * i:128 * i + 128] = block.T

    wait_bytes(send.at[pl.ds(0, 15)], ssem.at[0])
    wait_bytes(send.at[pl.ds(0, 15)], ssem.at[1])

    @pl.when(is_short)
    def _():
        wait_bytes(send.at[pl.ds(0, 12)], ssem.at[2])

    @pl.when(jnp.logical_not(is_short))
    def _():
        wait_bytes(send.at[pl.ds(0, 11)], ssem.at[2])

    swap.wait_send()
    wait_bytes(fin.at[core], ssem.at[9])


RANK = 112
TILES = RANK // 8
PIECES = [(p, q, half) for p, q in ((0, 0), (0, 1), (1, 0), (0, 2), (2, 0), (1, 1)) for half in range(2)]


def spread_out(v):
    return jnp.broadcast_to(v, (8, 128))


def column(tile, k):
    return spread_out(tile[:, k:k + 1])


def row_of(ref, index, i):
    return spread_out(ref[index, i:i + 1, :])


NEAR = 3


def inverse_factor(a, work, beside):
    sub = lax.broadcasted_iota(jnp.int32, (8, 128), 0)
    lane = lax.broadcasted_iota(jnp.int32, (8, 128), 1)
    tiles = [a[8 * t:8 * t + 8, :] for t in range(TILES)]
    result = []
    ahead = None
    for t0 in range(TILES):
        k0 = 8 * t0
        base = (t0 % 2) * 18
        in_block = (lane >= k0) & (lane < k0 + 8)
        work[base] = jnp.where(in_block, (lane == sub + k0).astype(F32), tiles[t0])
        row = [row_of(work, base, i) for i in range(8)]
        for j in range(8):
            work[base + 2 + j] = column(tiles[t0], k0 + j) if ahead is None else ahead[j]
        s = [[row_of(work, base + 2 + j, i) for j in range(i + 1)] for i in range(8)]
        near = range(t0 + 1, min(TILES, t0 + 1 + NEAR))
        far = range(min(TILES, t0 + 1 + NEAR), TILES)
        col = {t: [column(tiles[t], k0 + j) for j in range(8)] for t in near}
        ahead = [column(tiles[t0 + 1], k0 + 8 + j) for j in range(8)] if near else None
        for t in near:
            tiles[t] = jnp.where(in_block, 0.0, tiles[t])
        beside(t0)
        factors, inverses = [], []
        for j in range(8):
            inv = 1.0 / s[j][j]
            m = [None] * 8
            for i in range(j + 1, 8):
                m[i] = s[i][j] * inv
            factors.append(m)
            inverses.append(inv)
            for i in range(j + 1, 8):
                for n in range(j + 1, i + 1):
                    s[i][n] = s[i][n] - m[i] * s[n][j]
            for i in range(j + 1, 8):
                row[i] = row[i] - m[i] * row[j]
            if near:
                work[base + 10 + j] = col[t0 + 1][j]
                next_row = [row_of(work, base + 10 + j, i) for i in range(8)]
            for t in near:
                x = col[t][j] * inv
                for n in range(j + 1, 8):
                    col[t][n] = col[t][n] - x * s[n][j]
                if t == t0 + 1:
                    ahead = [ahead[n] - x * next_row[n] for n in range(8)]
                tiles[t] = tiles[t] - x * row[j]
        tile, pivots = row[7], s[7][7]
        for i in range(7):
            tile = jnp.where(sub == i, row[i], tile)
            pivots = jnp.where(sub == i, s[i][i], pivots)
        result.append(jnp.where(lane < k0 + 8, tile * lax.rsqrt(pivots), 0.0))
        if far:
            back = [None] * 8
            for j in reversed(range(8)):
                u = row[j] * inverses[j]
                for i in range(j + 1, 8):
                    u = u - factors[j][i] * back[i]
                back[j] = u
            for t in far:
                u = jnp.where(in_block, 0.0, tiles[t])
                for j in range(8):
                    u = u - column(tiles[t], k0 + j) * back[j]
                tiles[t] = u
    return jnp.concatenate(result, axis=0)


def split3(v):
    hi = v.astype(BF16)
    rest = v - hi.astype(F32)
    mid = rest.astype(BF16)
    return hi, mid, (rest - mid.astype(F32)).astype(BF16)


def dot_p(a, b):
    return lax.dot_general(a, b, (((1,), (0,)), ((), ())), preferred_element_type=F32)


def long_product(a, b):
    hi, mid, lo = a
    b_hi, b_mid, b_lo = b
    return dot_p(
        jnp.concatenate([hi, mid, hi, lo, hi, mid], axis=1),
        jnp.concatenate([b_hi, b_hi, b_mid, b_hi, b_lo, b_mid], axis=0),
    )


def turns_part(g_ref, s_ref, hi_ref, lo_ref, st_ref, got, image, last, ahead, ahead_parts, inverse, parts, work, core_ref,
               ssem, rsem):
    z, x, y, core = place()

    for p, part in enumerate(split3(g_ref[...])):
        parts[p] = part
    image[...] = long_product(split3(s_ref[...]), (parts[0], parts[1], parts[2]))
    zeros = jnp.zeros((16, 512), BF16)
    for p in range(3):
        ahead_parts[p, RANK:] = zeros

    def turn(index, carry):
        now = image[...]
        last[...] = now
        hi, mid, lo = now = split3(now)
        pair = jnp.concatenate([hi, zeros, mid, zeros], axis=0)
        both = dot_t(pair, pair)
        small = dot_t(lo, jnp.concatenate([hi, zeros], axis=0)) + dot_t(hi, jnp.concatenate([lo, zeros], axis=0))
        cross = both[:RANK, 128:] + both[128:128 + RANK, :128]
        inner = both[:RANK, :128] + (cross + (small + both[128:128 + RANK, 128:]))

        def beside(t):
            if t < len(PIECES):
                p, q, half = PIECES[t]
                lanes = slice(256 * half, 256 * half + 256)
                piece = dot_p(now[p], parts[q, :, lanes])
                ahead[:, lanes] = piece if p + q == 0 else ahead[:, lanes] + piece
            elif t == len(PIECES):
                for p, part in enumerate(split3(ahead[...])):
                    ahead_parts[p, :RANK] = part

        w = inverse_factor(inner, work, beside)
        inverse[...] = w
        image[...] = long_product(split3(w), (ahead_parts[0], ahead_parts[1], ahead_parts[2]))
        return carry

    lax.fori_loop(0, ITERS, turn, 0)
    padded = tuple(jnp.concatenate([v, zeros], axis=0) for v in split3(last[...]))
    basis = long_product(split3(inverse[...]), padded)
    basis_hi, basis_lo = split(basis)

    def project(slot):
        lanes = slice(128 * slot, 128 * slot + 128)
        field_hi, field_lo = hi_ref[:, lanes], lo_ref[:, lanes]
        part = dot_p(
            jnp.concatenate([basis_hi, basis_hi, basis_lo], axis=1),
            jnp.concatenate([field_hi, field_lo, field_hi], axis=0),
        )
        for d in range(Z):
            core_ref[d, slot] = part[7 * d:7 * d + 7, :]

    first = first_group(z, core)
    is_short = short(z, core)

    def push(slot, n):
        def one(step, carry):
            d = partner(z, step)
            pltpu.make_async_remote_copy(
                src_ref=core_ref.at[d, pl.ds(slot, n)], dst_ref=got.at[pl.ds(first + slot, n)],
                send_sem=ssem, recv_sem=rsem, device_id={"gx": d}, device_id_type=MESH).start()
            return carry

        lax.fori_loop(0, 15, one, 0)

    def finish(n):
        push(1, n - 1)
        got[pl.ds(first, n)] = core_ref[z, pl.ds(0, n)]
        st_ref[...] = basis
        wait_bytes(got.at[pl.ds(0, GROUPS - n)], rsem)
        wait_bytes(core_ref.at[pl.ds(0, 15), pl.ds(0, n)], ssem)

    project(0)
    push(0, 1)
    project(1)
    project(2)

    @pl.when(is_short)
    def _():
        finish(2)

    @pl.when(jnp.logical_not(is_short))
    def _():
        finish(3)


def step_kernel(total, x_hbm, s_hbm, st_ref, got, s_ref, s_sem, *scratch):
    g_ref, hi_ref, lo_ref = scratch[1], scratch[4], scratch[5]
    load = pltpu.make_async_copy(s_hbm, s_ref, s_sem)
    load.start()
    gram_part(total, x_hbm, *scratch[:19])
    load.wait()
    turns_part(g_ref, s_ref, hi_ref, lo_ref, st_ref, got, *scratch[19:])


def step(x, s, total):
    vm = pl.BlockSpec(memory_space=pltpu.VMEM)
    return pl.pallas_call(
        functools.partial(step_kernel, total),
        out_shape=(jax.ShapeDtypeStruct((RANK, 512), F32), jax.ShapeDtypeStruct((GROUPS, 7, 128), F32)),
        in_specs=[pl.BlockSpec(memory_space=pl.ANY)] * 2,
        out_specs=(vm, vm),
        scratch_shapes=[
            pltpu.VMEM((RANK, 512), F32),
            pltpu.SemaphoreType.DMA,
            pltpu.VMEM((11, 128, 128), F32),
            pltpu.VMEM((512, 512), F32),
            pltpu.VMEM((GROUPS, 32, 128), F32),
            pltpu.VMEM((SLOTS, 512, 128), F32),
            pltpu.VMEM((512, 384), BF16),
            pltpu.VMEM((512, 384), BF16),
            pltpu.VMEM((1280, 128), F32),
            pltpu.VMEM((640, 128), F32),
            pltpu.VMEM((CHIPS, UNITS, 8, 128), F32),
            pltpu.VMEM((2 * CHIPS, 3, 8, 128), F32),
            pltpu.VMEM((3, 8, 128), F32),
            pltpu.VMEM((Z // 2, 3, 8, 128), F32),
            pltpu.VMEM((3, 8, 128), F32),
            pltpu.VMEM((2, CHIPS, UNITS, 8, 128), F32),
            pltpu.SemaphoreType.DMA((10,)),
            pltpu.SemaphoreType.DMA((10,)),
            pltpu.SemaphoreType.DMA,
            pltpu.SemaphoreType.REGULAR,
            pltpu.SemaphoreType.REGULAR,
            pltpu.VMEM((RANK, 512), F32),
            pltpu.VMEM((RANK, 512), F32),
            pltpu.VMEM((RANK, 512), F32),
            pltpu.VMEM((3, 128, 512), BF16),
            pltpu.VMEM((RANK, 128), F32),
            pltpu.VMEM((3, 512, 512), BF16),
            pltpu.VMEM((36, 8, 128), F32),
            pltpu.VMEM((Z, SLOTS, 7, 128), F32),
            pltpu.SemaphoreType.DMA,
            pltpu.SemaphoreType.DMA,
        ],
        compiler_params=pltpu.CompilerParams(
            collective_id=0, has_side_effects=True, vmem_limit_bytes=(64 * 1024 - 10816) * 1024),
    )(x, s)


def unpack_kernel(st_ref, got_ref, st_out, core_out):
    st_out[...] = st_ref[...]
    for e in range(7):
        for s in range(11):
            core_out[e, s] = got_ref[4 * s:4 * s + 4, e, :]


def unpack(st, got):
    vm = pl.BlockSpec(memory_space=pltpu.VMEM)
    return pl.pallas_call(
        unpack_kernel,
        out_shape=(jax.ShapeDtypeStruct((RANK, 512), F32), jax.ShapeDtypeStruct((7, 11, 4, 128), F32)),
        in_specs=[vm, vm],
        out_specs=(vm, vm),
        compiler_params=pltpu.CompilerParams(vmem_limit_bytes=4 * 1024 * 1024),
    )(st, got)


def per_device(species_field, start_basis):
    total = float(11 * 16 * 1024)
    st, core = unpack(*step(species_field.reshape(11, 128, 128), start_basis.T, total))
    return (st.T, core)


def solution(mesh):
    placed = (P(None, "gx", "gy", "gz"), P())
    return jax.shard_map(
        per_device,
        mesh=mesh,
        in_specs=placed,
        out_specs=(P(), P("gx", None, "gy", "gz")),
        check_vma=False,
    )
```

```python
import functools

import jax
import jax.numpy as jnp
from jax import lax
from jax.experimental import pallas as pl
from jax.experimental.pallas import tpu as pltpu
from jax.sharding import PartitionSpec as P

ITERS = 8
MESH = pl.DeviceIdType.MESH
F32 = jnp.float32
BF16 = jnp.bfloat16

Z = 16
GROUPS = 44
SLOTS = 3
CHIPS = 16


def place():
    z = lax.axis_index("gx")
    x = lax.axis_index("gy")
    w = lax.axis_index("gz")
    core = lax.rem(w, 2)
    return z, x, lax.div(w, 2), core


def first_group(dest, core):
    return 3 * dest - lax.div(dest + 3 - 2 * core, 4)


def short(dest, core):
    return lax.rem(dest, 4) == 2 * core


def partner(me, step):
    half = lax.div(step + 1, 2)
    k = 8 + half * (2 * lax.rem(step, 2) - 1)
    return lax.rem(me + k, Z)


def wait_bytes(ref, sem):
    pltpu.make_async_copy(ref, ref, sem).wait()


def split(v):
    hi = v.astype(BF16)
    return hi, (v - hi.astype(F32)).astype(BF16)


def dot_t(a, b):
    return lax.dot_general(a, b, (((1,), (1,)), ((), ())), preferred_element_type=F32)


OFFSETS = [(2, 2), (2, 1), (2, 3), (1, 2), (3, 2), (2, 0), (0, 2), (1, 1), (1, 3), (3, 1), (3, 3), (1, 0), (3, 0), (0, 1), (0, 3)]
UNITS = 5


def gram_part(total, x_hbm, x_ref, g_ref, send, recv, hi_ref, lo_ref, part, sib, half, spread,
              chunk, chunks, mine, fin, ssem, rsem, lsem, token2, token3):
    z, x, y, core = place()
    q = x * 4 + y
    load = pltpu.make_async_copy(x_hbm, x_ref, lsem)
    load.start()

    def along_z(k):
        return {"gx": lax.rem(z + k + Z, Z)}

    def chip(p):
        return {"gy": lax.div(p, 4), "gz": lax.rem(p, 4) * 2 + core}

    sibling = {"gz": y * 2 + 1 - core}
    close = [along_z(k) for k in (1, -1, 2, -2)] + [sibling]
    close += [{"gy": lax.rem(x + k, 4)} for k in (1, 2, 3)]
    close += [{"gz": lax.rem(y + k, 4) * 2 + core} for k in (1, 2, 3)]
    barrier = pltpu.get_barrier_semaphore()
    for device in close:
        pl.semaphore_signal(barrier, inc=1, device_id=device, device_id_type=MESH)
    load.wait()
    for g in range(GROUPS):
        s, yy = divmod(g, 4)
        send[g] = x_ref[s, pl.ds(yy, 32, stride=4), :]
    pl.semaphore_wait(barrier, len(close))
    for device in close:
        pl.semaphore_signal(token2, inc=1, device_id=device, device_id_type=MESH)

    rows = pl.ds(pl.multiple_of(z * 32, 32), 32)

    def copy_to(slot, d):
        return pltpu.make_async_remote_copy(
            src_ref=send.at[first_group(d, core) + slot],
            dst_ref=recv.at[slot, rows],
            send_sem=ssem.at[slot],
            recv_sem=rsem.at[slot],
            device_id={"gx": d},
            device_id_type=MESH,
        )

    def push(slot, k):
        d = lax.rem(z + k + Z, Z)
        if slot < 2:
            copy_to(slot, d).start()
        else:
            @pl.when(jnp.logical_not(short(d, core)))
            def _():
                copy_to(slot, d).start()

    for slot in range(SLOTS):
        for k in (2, -2, 1, -1):
            push(slot, k)
    pl.semaphore_wait(token2, len(close))
    for k in range(1, 5):
        for sign in (1, -1):
            pl.semaphore_signal(token3, inc=1, device_id=along_z(sign * k), device_id_type=MESH)
    for slot in range(SLOTS):
        for k in (4, -4, 3, -3):
            push(slot, k)
    pl.semaphore_wait(token3, 8)
    for slot in range(SLOTS):
        for k in (8, 7, -7, 6, -6, 5, -5):
            push(slot, k)

    mine_first = first_group(z, core)
    recv[0, rows] = send[mine_first]
    recv[1, rows] = send[mine_first + 1]
    is_short = short(z, core)

    @pl.when(is_short)
    def _():
        recv[2] = jnp.zeros((512, 128), F32)

    @pl.when(jnp.logical_not(is_short))
    def _():
        recv[2, rows] = send[mine_first + 2]

    others = pl.ds(0, 480)

    halves = (((0, 0, 1), (1, 0, 2), (2, 0, 2)), ((2, 2, 3), (3, 0, 4)))

    def accumulate(lanes, first, which):
        for i, j0, j1 in halves[which]:
            ri = slice(128 * i, 128 * i + 128)
            rj = slice(128 * j0, 128 * j1)
            hi_i, lo_i = hi_ref[ri, lanes], lo_ref[ri, lanes]
            hi_j = hi_ref[rj, lanes]
            lo_j = lo_ref[rj, lanes]
            block = dot_t(hi_i, hi_j) + (dot_t(hi_i, lo_j) + dot_t(lo_i, hi_j) + dot_t(lo_i, lo_j))
            for j in range(j0, j1):
                b = i * (i + 1) // 2 + j
                rb = slice(128 * b, 128 * b + 128)
                piece = block[:, 128 * (j - j0):128 * (j - j0) + 128]
                part[rb] = piece if first else part[rb] + piece

    def take(slot):
        hi, lo = split(recv[slot])
        hi_ref[:, 128 * slot:128 * slot + 128] = hi
        lo_ref[:, 128 * slot:128 * slot + 128] = lo

    wait_bytes(recv.at[0, others], rsem.at[0])
    take(0)
    wait_bytes(recv.at[1, others], rsem.at[1])
    take(1)
    accumulate(slice(0, 256), True, 0)
    accumulate(slice(0, 256), True, 1)

    @pl.when(jnp.logical_not(is_short))
    def _():
        wait_bytes(recv.at[2, others], rsem.at[2])

    take(2)

    own_half = pl.ds(pl.multiple_of(core * 640, 8), 640)
    other_half = pl.ds(pl.multiple_of((1 - core) * 640, 8), 640)
    swap = pltpu.make_async_remote_copy(
        src_ref=part.at[other_half], dst_ref=sib, send_sem=ssem.at[3], recv_sem=rsem.at[3],
        device_id=sibling, device_id_type=MESH)
    for c in range(2):
        @pl.when(core == c)
        def _(c=c):
            accumulate(slice(256, 384), False, 1 - c)
            swap.start()
            accumulate(slice(256, 384), False, c)

    swap.wait_recv()
    half[...] = (part[own_half] + sib[...]).reshape(CHIPS, UNITS, 8, 128)

    odd = lax.rem(z, 2)
    even_z, odd_z = {"gx": z - odd}, {"gx": z - odd + 1}
    source = q * 2 + odd

    def for_even(p):
        return pltpu.make_async_remote_copy(
            src_ref=half.at[p, pl.ds(0, 3)], dst_ref=spread.at[source], send_sem=ssem.at[4], recv_sem=rsem.at[4],
            device_id=even_z | chip(p), device_id_type=MESH)

    def for_odd(p):
        return pltpu.make_async_remote_copy(
            src_ref=half.at[p, pl.ds(3, 2)], dst_ref=spread.at[source, pl.ds(0, 2)],
            send_sem=ssem.at[5], recv_sem=rsem.at[5],
            device_id=odd_z | chip(p), device_id_type=MESH)

    def others_of_layer():
        return [lax.rem(x + ox, 4) * 4 + lax.rem(y + oy, 4) for ox, oy in OFFSETS]

    for p in others_of_layer():
        for_even(p).start()
        for_odd(p).start()

    def along(k):
        return {"gx": lax.rem(z + k + Z, Z)}

    def rest(n, first, cross, sum_sem):
        own = pl.ds(0, n)
        spread[source, 0:n] = half[q, first:first + n]
        cross(q).start()
        wait_bytes(spread.at[pl.ds(0, 31), own], sum_sem)
        chunk[0:n] = jnp.sum(spread[:, 0:n], axis=0)

        for k in (8, 6, -6, 4, -4, 2, -2):
            pltpu.make_async_remote_copy(
                src_ref=chunk.at[own], dst_ref=chunks.at[lax.div(z, 2), own],
                send_sem=ssem.at[6], recv_sem=rsem.at[6], device_id=along(k), device_id_type=MESH).start()
        chunks[lax.div(z, 2), 0:n] = chunk[0:n]
        wait_bytes(chunks.at[pl.ds(0, 7), own], rsem.at[6])
        mine[0:n] = jnp.sum(chunks[:, 0:n], axis=0) * (1.0 / total)

        def back(p, z_too, sem):
            return pltpu.make_async_remote_copy(
                src_ref=mine.at[own], dst_ref=fin.at[core, q, pl.ds(first, n)],
                send_sem=ssem.at[sem], recv_sem=rsem.at[sem], device_id=z_too | chip(p), device_id_type=MESH)

        other_z = odd_z if first == 0 else even_z

        for p in others_of_layer():
            back(p, other_z, 8).start()
            back(p, {}, 7).start()
        back(q, other_z, 8).start()
        fin[core, q, first:first + n] = mine[0:n]

        def to_sibling(units):
            return pltpu.make_async_remote_copy(
                src_ref=fin.at[core, :, units], dst_ref=fin.at[core, :, units],
                send_sem=ssem.at[9], recv_sem=rsem.at[9], device_id=sibling, device_id_type=MESH)

        same, other = pl.ds(first, n), pl.ds(3 - first, 5 - n)
        wait_bytes(fin.at[core, pl.ds(0, 15), same], rsem.at[7])
        to_sibling(same).start()
        wait_bytes(fin.at[core, :, other], rsem.at[8])
        to_sibling(other).start()
        wait_bytes(fin.at[1 - core], rsem.at[9])

        wait_bytes(chunks.at[pl.ds(0, 7), own], ssem.at[6])
        wait_bytes(fin.at[core, pl.ds(0, 15), same], ssem.at[7])
        wait_bytes(fin.at[core, :, same], ssem.at[8])

    @pl.when(odd == 0)
    def _():
        rest(3, 0, for_odd, rsem.at[4])
        wait_bytes(half.at[pl.ds(0, 15), pl.ds(0, 3)], ssem.at[4])
        wait_bytes(half.at[:, pl.ds(0, 2)], ssem.at[5])

    @pl.when(odd == 1)
    def _():
        rest(2, 3, for_even, rsem.at[5])
        wait_bytes(half.at[:, pl.ds(0, 3)], ssem.at[4])
        wait_bytes(half.at[pl.ds(0, 15), pl.ds(0, 2)], ssem.at[5])

    for i in range(4):
        for j in range(i + 1):
            b = i * (i + 1) // 2 + j
            tiles = []
            for r in range(16 * b, 16 * b + 16):
                h, rest = divmod(r, 80)
                tiles.append(fin[h, rest // UNITS, rest % UNITS])
            block = jnp.concatenate(tiles, axis=0)
            g_ref[128 * i:128 * i + 128, 128 * j:128 * j + 128] = block
            if j < i:
                g_ref[128 * j:128 * j + 128, 128 * i:128 * i + 128] = block.T

    wait_bytes(send.at[pl.ds(0, 15)], ssem.at[0])
    wait_bytes(send.at[pl.ds(0, 15)], ssem.at[1])

    @pl.when(is_short)
    def _():
        wait_bytes(send.at[pl.ds(0, 12)], ssem.at[2])

    @pl.when(jnp.logical_not(is_short))
    def _():
        wait_bytes(send.at[pl.ds(0, 11)], ssem.at[2])

    swap.wait_send()
    wait_bytes(fin.at[core], ssem.at[9])


RANK = 112
TILES = RANK // 8
PIECES = [(p, q, half) for p, q in ((0, 0), (0, 1), (1, 0), (0, 2), (2, 0), (1, 1)) for half in range(2)]


def spread_out(v):
    return jnp.broadcast_to(v, (8, 128))


def column(tile, k):
    return spread_out(tile[:, k:k + 1])


def row_of(ref, index, i):
    return spread_out(ref[index, i:i + 1, :])


NEAR = 3


def inverse_factor(a, work, beside):
    sub = lax.broadcasted_iota(jnp.int32, (8, 128), 0)
    lane = lax.broadcasted_iota(jnp.int32, (8, 128), 1)
    tiles = [a[8 * t:8 * t + 8, :] for t in range(TILES)]
    result = []
    ahead = None
    for t0 in range(TILES):
        k0 = 8 * t0
        base = (t0 % 2) * 18
        in_block = (lane >= k0) & (lane < k0 + 8)
        work[base] = jnp.where(in_block, (lane == sub + k0).astype(F32), tiles[t0])
        row = [row_of(work, base, i) for i in range(8)]
        for j in range(8):
            work[base + 2 + j] = column(tiles[t0], k0 + j) if ahead is None else ahead[j]
        s = [[row_of(work, base + 2 + j, i) for j in range(i + 1)] for i in range(8)]
        near = range(t0 + 1, min(TILES, t0 + 1 + NEAR))
        far = range(min(TILES, t0 + 1 + NEAR), TILES)
        col = {t: [column(tiles[t], k0 + j) for j in range(8)] for t in near}
        ahead = [column(tiles[t0 + 1], k0 + 8 + j) for j in range(8)] if near else None
        for t in near:
            tiles[t] = jnp.where(in_block, 0.0, tiles[t])
        beside(t0)
        factors, inverses = [], []
        for j in range(8):
            inv = 1.0 / s[j][j]
            m = [None] * 8
            for i in range(j + 1, 8):
                m[i] = s[i][j] * inv
            factors.append(m)
            inverses.append(inv)
            for i in range(j + 1, 8):
                for n in range(j + 1, i + 1):
                    s[i][n] = s[i][n] - m[i] * s[n][j]
            for i in range(j + 1, 8):
                row[i] = row[i] - m[i] * row[j]
            if near:
                work[base + 10 + j] = col[t0 + 1][j]
                next_row = [row_of(work, base + 10 + j, i) for i in range(8)]
            for t in near:
                x = col[t][j] * inv
                for n in range(j + 1, 8):
                    col[t][n] = col[t][n] - x * s[n][j]
                if t == t0 + 1:
                    ahead = [ahead[n] - x * next_row[n] for n in range(8)]
                tiles[t] = tiles[t] - x * row[j]
        tile, pivots = row[7], s[7][7]
        for i in range(7):
            tile = jnp.where(sub == i, row[i], tile)
            pivots = jnp.where(sub == i, s[i][i], pivots)
        result.append(jnp.where(lane < k0 + 8, tile * lax.rsqrt(pivots), 0.0))
        if far:
            back = [None] * 8
            for j in reversed(range(8)):
                u = row[j] * inverses[j]
                for i in range(j + 1, 8):
                    u = u - factors[j][i] * back[i]
                back[j] = u
            for t in far:
                u = jnp.where(in_block, 0.0, tiles[t])
                for j in range(8):
                    u = u - column(tiles[t], k0 + j) * back[j]
                tiles[t] = u
    return jnp.concatenate(result, axis=0)


def split3(v):
    hi = v.astype(BF16)
    rest = v - hi.astype(F32)
    mid = rest.astype(BF16)
    return hi, mid, (rest - mid.astype(F32)).astype(BF16)


def dot_p(a, b):
    return lax.dot_general(a, b, (((1,), (0,)), ((), ())), preferred_element_type=F32)


def long_product(a, b):
    hi, mid, lo = a
    b_hi, b_mid, b_lo = b
    return dot_p(
        jnp.concatenate([hi, mid, hi, lo, hi, mid], axis=1),
        jnp.concatenate([b_hi, b_hi, b_mid, b_hi, b_lo, b_mid], axis=0),
    )


def turns_part(g_ref, s_ref, hi_ref, lo_ref, st_ref, got, image, last, ahead, ahead_parts, inverse, parts, work, core_ref,
               ssem, rsem):
    z, x, y, core = place()

    for p, part in enumerate(split3(g_ref[...])):
        parts[p] = part
    image[...] = long_product(split3(s_ref[...]), (parts[0], parts[1], parts[2]))
    zeros = jnp.zeros((16, 512), BF16)
    for p in range(3):
        ahead_parts[p, RANK:] = zeros

    def turn(index, carry):
        now = image[...]
        last[...] = now
        hi, mid, lo = now = split3(now)
        pair = jnp.concatenate([hi, zeros, mid, zeros], axis=0)
        both = dot_t(pair, pair)
        small = dot_t(lo, jnp.concatenate([hi, zeros], axis=0)) + dot_t(hi, jnp.concatenate([lo, zeros], axis=0))
        cross = both[:RANK, 128:] + both[128:128 + RANK, :128]
        inner = both[:RANK, :128] + (cross + (small + both[128:128 + RANK, 128:]))

        def beside(t):
            if t < len(PIECES):
                p, q, half = PIECES[t]
                lanes = slice(256 * half, 256 * half + 256)
                piece = dot_p(now[p], parts[q, :, lanes])
                ahead[:, lanes] = piece if p + q == 0 else ahead[:, lanes] + piece
            elif t == len(PIECES):
                for p, part in enumerate(split3(ahead[...])):
                    ahead_parts[p, :RANK] = part

        w = inverse_factor(inner, work, beside)
        inverse[...] = w
        image[...] = long_product(split3(w), (ahead_parts[0], ahead_parts[1], ahead_parts[2]))
        return carry

    lax.fori_loop(0, ITERS, turn, 0)
    padded = tuple(jnp.concatenate([v, zeros], axis=0) for v in split3(last[...]))
    basis = long_product(split3(inverse[...]), padded)
    basis_hi, basis_lo = split(basis)

    def project(slot):
        lanes = slice(128 * slot, 128 * slot + 128)
        field_hi, field_lo = hi_ref[:, lanes], lo_ref[:, lanes]
        part = dot_p(
            jnp.concatenate([basis_hi, basis_hi, basis_lo], axis=1),
            jnp.concatenate([field_hi, field_lo, field_hi], axis=0),
        )
        for d in range(Z):
            core_ref[d, slot] = part[7 * d:7 * d + 7, :]

    first = first_group(z, core)
    is_short = short(z, core)

    def push(slot, n):
        def one(step, carry):
            d = partner(z, step)
            pltpu.make_async_remote_copy(
                src_ref=core_ref.at[d, pl.ds(slot, n)], dst_ref=got.at[pl.ds(first + slot, n)],
                send_sem=ssem, recv_sem=rsem, device_id={"gx": d}, device_id_type=MESH).start()
            return carry

        lax.fori_loop(0, 15, one, 0)

    def finish(n):
        push(1, n - 1)
        got[pl.ds(first, n)] = core_ref[z, pl.ds(0, n)]
        st_ref[...] = basis
        wait_bytes(got.at[pl.ds(0, GROUPS - n)], rsem)
        wait_bytes(core_ref.at[pl.ds(0, 15), pl.ds(0, n)], ssem)

    project(0)
    push(0, 1)
    project(1)
    project(2)

    @pl.when(is_short)
    def _():
        finish(2)

    @pl.when(jnp.logical_not(is_short))
    def _():
        finish(3)


def step_kernel(total, x_hbm, s_hbm, st_ref, got, s_ref, s_sem, *scratch):
    g_ref, hi_ref, lo_ref = scratch[1], scratch[4], scratch[5]
    load = pltpu.make_async_copy(s_hbm, s_ref, s_sem)
    load.start()
    gram_part(total, x_hbm, *scratch[:19])
    load.wait()
    turns_part(g_ref, s_ref, hi_ref, lo_ref, st_ref, got, *scratch[19:])


def step(x, s, total):
    vm = pl.BlockSpec(memory_space=pltpu.VMEM)
    return pl.pallas_call(
        functools.partial(step_kernel, total),
        out_shape=(jax.ShapeDtypeStruct((RANK, 512), F32), jax.ShapeDtypeStruct((GROUPS, 7, 128), F32)),
        in_specs=[pl.BlockSpec(memory_space=pl.ANY)] * 2,
        out_specs=(vm, vm),
        scratch_shapes=[
            pltpu.VMEM((RANK, 512), F32),
            pltpu.SemaphoreType.DMA,
            pltpu.VMEM((11, 128, 128), F32),
            pltpu.VMEM((512, 512), F32),
            pltpu.VMEM((GROUPS, 32, 128), F32),
            pltpu.VMEM((SLOTS, 512, 128), F32),
            pltpu.VMEM((512, 384), BF16),
            pltpu.VMEM((512, 384), BF16),
            pltpu.VMEM((1280, 128), F32),
            pltpu.VMEM((640, 128), F32),
            pltpu.VMEM((CHIPS, UNITS, 8, 128), F32),
            pltpu.VMEM((2 * CHIPS, 3, 8, 128), F32),
            pltpu.VMEM((3, 8, 128), F32),
            pltpu.VMEM((Z // 2, 3, 8, 128), F32),
            pltpu.VMEM((3, 8, 128), F32),
            pltpu.VMEM((2, CHIPS, UNITS, 8, 128), F32),
            pltpu.SemaphoreType.DMA((10,)),
            pltpu.SemaphoreType.DMA((10,)),
            pltpu.SemaphoreType.DMA,
            pltpu.SemaphoreType.REGULAR,
            pltpu.SemaphoreType.REGULAR,
            pltpu.VMEM((RANK, 512), F32),
            pltpu.VMEM((RANK, 512), F32),
            pltpu.VMEM((RANK, 512), F32),
            pltpu.VMEM((3, 128, 512), BF16),
            pltpu.VMEM((RANK, 128), F32),
            pltpu.VMEM((3, 512, 512), BF16),
            pltpu.VMEM((36, 8, 128), F32),
            pltpu.VMEM((Z, SLOTS, 7, 128), F32),
            pltpu.SemaphoreType.DMA,
            pltpu.SemaphoreType.DMA,
        ],
        compiler_params=pltpu.CompilerParams(
            collective_id=0, has_side_effects=True, vmem_limit_bytes=(64 * 1024 - 10816) * 1024),
    )(x, s)


def unpack_kernel(st_ref, got_ref, st_out, core_out):
    st_out[...] = st_ref[...]
    for e in range(7):
        for s in range(11):
            core_out[e, s] = got_ref[4 * s:4 * s + 4, e, :]


def unpack(st, got):
    vm = pl.BlockSpec(memory_space=pltpu.VMEM)
    return pl.pallas_call(
        unpack_kernel,
        out_shape=(jax.ShapeDtypeStruct((RANK, 512), F32), jax.ShapeDtypeStruct((7, 11, 4, 128), F32)),
        in_specs=[vm, vm],
        out_specs=(vm, vm),
        compiler_params=pltpu.CompilerParams(vmem_limit_bytes=4 * 1024 * 1024),
    )(st, got)


def per_device(species_field, start_basis):
    total = float(11 * 16 * 1024)
    st, core = unpack(*step(species_field.reshape(11, 128, 128), start_basis.T, total))
    return (st.T, core)


def solution(mesh):
    placed = (P(None, "gx", "gy", "gz"), P())
    return jax.shard_map(
        per_device,
        mesh=mesh,
        in_specs=placed,
        out_specs=(P(), P("gx", None, "gy", "gz")),
        check_vma=False,
    )
```

```python
import functools

import jax
import jax.numpy as jnp
from jax import lax
from jax.experimental import pallas as pl
from jax.experimental.pallas import tpu as pltpu
from jax.sharding import PartitionSpec as P

ITERS = 8
MESH = pl.DeviceIdType.MESH
F32 = jnp.float32
BF16 = jnp.bfloat16

Z = 16
GROUPS = 44
SLOTS = 3
CHIPS = 16


def place():
    z = lax.axis_index("gx")
    x = lax.axis_index("gy")
    w = lax.axis_index("gz")
    core = lax.rem(w, 2)
    return z, x, lax.div(w, 2), core


def first_group(dest, core):
    return 3 * dest - lax.div(dest + 3 - 2 * core, 4)


def short(dest, core):
    return lax.rem(dest, 4) == 2 * core


def partner(me, step):
    half = lax.div(step + 1, 2)
    k = 8 + half * (2 * lax.rem(step, 2) - 1)
    return lax.rem(me + k, Z)


def wait_bytes(ref, sem):
    pltpu.make_async_copy(ref, ref, sem).wait()


def split(v):
    hi = v.astype(BF16)
    return hi, (v - hi.astype(F32)).astype(BF16)


def dot_t(a, b):
    return lax.dot_general(a, b, (((1,), (1,)), ((), ())), preferred_element_type=F32)


OFFSETS = [(2, 2), (2, 1), (2, 3), (1, 2), (3, 2), (2, 0), (0, 2), (1, 1), (1, 3), (3, 1), (3, 3), (1, 0), (3, 0), (0, 1), (0, 3)]
UNITS = 5


def gram_part(total, x_hbm, x_ref, g_ref, send, recv, hi_ref, lo_ref, part, sib, half, spread,
              chunk, chunks, mine, fin, ssem, rsem, lsem, token2, token3):
    z, x, y, core = place()
    q = x * 4 + y
    load = pltpu.make_async_copy(x_hbm, x_ref, lsem)
    load.start()

    def along_z(k):
        return {"gx": lax.rem(z + k + Z, Z)}

    def chip(p):
        return {"gy": lax.div(p, 4), "gz": lax.rem(p, 4) * 2 + core}

    sibling = {"gz": y * 2 + 1 - core}
    close = [along_z(k) for k in (1, -1, 2, -2)] + [sibling]
    close += [{"gy": lax.rem(x + k, 4)} for k in (1, 2, 3)]
    close += [{"gz": lax.rem(y + k, 4) * 2 + core} for k in (1, 2, 3)]
    barrier = pltpu.get_barrier_semaphore()
    for device in close:
        pl.semaphore_signal(barrier, inc=1, device_id=device, device_id_type=MESH)
    load.wait()
    for g in range(GROUPS):
        s, yy = divmod(g, 4)
        send[g] = x_ref[s, pl.ds(yy, 32, stride=4), :]
    pl.semaphore_wait(barrier, len(close))
    for device in close:
        pl.semaphore_signal(token2, inc=1, device_id=device, device_id_type=MESH)

    rows = pl.ds(pl.multiple_of(z * 32, 32), 32)

    def copy_to(slot, d):
        return pltpu.make_async_remote_copy(
            src_ref=send.at[first_group(d, core) + slot],
            dst_ref=recv.at[slot, rows],
            send_sem=ssem.at[slot],
            recv_sem=rsem.at[slot],
            device_id={"gx": d},
            device_id_type=MESH,
        )

    def push(slot, k):
        d = lax.rem(z + k + Z, Z)
        if slot < 2:
            copy_to(slot, d).start()
        else:
            @pl.when(jnp.logical_not(short(d, core)))
            def _():
                copy_to(slot, d).start()

    for slot in range(SLOTS):
        for k in (2, -2, 1, -1):
            push(slot, k)
    pl.semaphore_wait(token2, len(close))
    for k in range(1, 5):
        for sign in (1, -1):
            pl.semaphore_signal(token3, inc=1, device_id=along_z(sign * k), device_id_type=MESH)
    for slot in range(SLOTS):
        for k in (4, -4, 3, -3):
            push(slot, k)
    pl.semaphore_wait(token3, 8)
    for slot in range(SLOTS):
        for k in (8, 7, -7, 6, -6, 5, -5):
            push(slot, k)

    mine_first = first_group(z, core)
    recv[0, rows] = send[mine_first]
    recv[1, rows] = send[mine_first + 1]
    is_short = short(z, core)

    @pl.when(is_short)
    def _():
        recv[2] = jnp.zeros((512, 128), F32)

    @pl.when(jnp.logical_not(is_short))
    def _():
        recv[2, rows] = send[mine_first + 2]

    others = pl.ds(0, 480)

    halves = (((0, 0, 1), (1, 0, 2), (2, 0, 2)), ((2, 2, 3), (3, 0, 4)))

    def accumulate(lanes, first, which):
        for i, j0, j1 in halves[which]:
            ri = slice(128 * i, 128 * i + 128)
            rj = slice(128 * j0, 128 * j1)
            hi_i, lo_i = hi_ref[ri, lanes], lo_ref[ri, lanes]
            hi_j = hi_ref[rj, lanes]
            lo_j = lo_ref[rj, lanes]
            block = dot_t(hi_i, hi_j) + (dot_t(hi_i, lo_j) + dot_t(lo_i, hi_j) + dot_t(lo_i, lo_j))
            for j in range(j0, j1):
                b = i * (i + 1) // 2 + j
                rb = slice(128 * b, 128 * b + 128)
                piece = block[:, 128 * (j - j0):128 * (j - j0) + 128]
                part[rb] = piece if first else part[rb] + piece

    def take(slot):
        hi, lo = split(recv[slot])
        hi_ref[:, 128 * slot:128 * slot + 128] = hi
        lo_ref[:, 128 * slot:128 * slot + 128] = lo

    wait_bytes(recv.at[0, others], rsem.at[0])
    take(0)
    wait_bytes(recv.at[1, others], rsem.at[1])
    take(1)
    accumulate(slice(0, 256), True, 0)
    accumulate(slice(0, 256), True, 1)

    @pl.when(jnp.logical_not(is_short))
    def _():
        wait_bytes(recv.at[2, others], rsem.at[2])

    take(2)

    own_half = pl.ds(pl.multiple_of(core * 640, 8), 640)
    other_half = pl.ds(pl.multiple_of((1 - core) * 640, 8), 640)
    swap = pltpu.make_async_remote_copy(
        src_ref=part.at[other_half], dst_ref=sib, send_sem=ssem.at[3], recv_sem=rsem.at[3],
        device_id=sibling, device_id_type=MESH)
    for c in range(2):
        @pl.when(core == c)
        def _(c=c):
            accumulate(slice(256, 384), False, 1 - c)
            swap.start()
            accumulate(slice(256, 384), False, c)

    swap.wait_recv()
    half[...] = (part[own_half] + sib[...]).reshape(CHIPS, UNITS, 8, 128)

    odd = lax.rem(z, 2)
    even_z, odd_z = {"gx": z - odd}, {"gx": z - odd + 1}
    source = q * 2 + odd

    def for_even(p):
        return pltpu.make_async_remote_copy(
            src_ref=half.at[p, pl.ds(0, 3)], dst_ref=spread.at[source], send_sem=ssem.at[4], recv_sem=rsem.at[4],
            device_id=even_z | chip(p), device_id_type=MESH)

    def for_odd(p):
        return pltpu.make_async_remote_copy(
            src_ref=half.at[p, pl.ds(3, 2)], dst_ref=spread.at[source, pl.ds(0, 2)],
            send_sem=ssem.at[5], recv_sem=rsem.at[5],
            device_id=odd_z | chip(p), device_id_type=MESH)

    def others_of_layer():
        return [lax.rem(x + ox, 4) * 4 + lax.rem(y + oy, 4) for ox, oy in OFFSETS]

    for p in others_of_layer():
        for_even(p).start()
        for_odd(p).start()

    def along(k):
        return {"gx": lax.rem(z + k + Z, Z)}

    def rest(n, first, cross, sum_sem):
        own = pl.ds(0, n)
        spread[source, 0:n] = half[q, first:first + n]
        cross(q).start()
        wait_bytes(spread.at[pl.ds(0, 31), own], sum_sem)
        chunk[0:n] = jnp.sum(spread[:, 0:n], axis=0)

        for k in (8, 6, -6, 4, -4, 2, -2):
            pltpu.make_async_remote_copy(
                src_ref=chunk.at[own], dst_ref=chunks.at[lax.div(z, 2), own],
                send_sem=ssem.at[6], recv_sem=rsem.at[6], device_id=along(k), device_id_type=MESH).start()
        chunks[lax.div(z, 2), 0:n] = chunk[0:n]
        wait_bytes(chunks.at[pl.ds(0, 7), own], rsem.at[6])
        mine[0:n] = jnp.sum(chunks[:, 0:n], axis=0) * (1.0 / total)

        def back(p, z_too, sem):
            return pltpu.make_async_remote_copy(
                src_ref=mine.at[own], dst_ref=fin.at[core, q, pl.ds(first, n)],
                send_sem=ssem.at[sem], recv_sem=rsem.at[sem], device_id=z_too | chip(p), device_id_type=MESH)

        other_z = odd_z if first == 0 else even_z

        for p in others_of_layer():
            back(p, other_z, 8).start()
            back(p, {}, 7).start()
        back(q, other_z, 8).start()
        fin[core, q, first:first + n] = mine[0:n]

        def to_sibling(units):
            return pltpu.make_async_remote_copy(
                src_ref=fin.at[core, :, units], dst_ref=fin.at[core, :, units],
                send_sem=ssem.at[9], recv_sem=rsem.at[9], device_id=sibling, device_id_type=MESH)

        same, other = pl.ds(first, n), pl.ds(3 - first, 5 - n)
        wait_bytes(fin.at[core, pl.ds(0, 15), same], rsem.at[7])
        to_sibling(same).start()
        wait_bytes(fin.at[core, :, other], rsem.at[8])
        to_sibling(other).start()

        wait_bytes(chunks.at[pl.ds(0, 7), own], ssem.at[6])
        wait_bytes(fin.at[core, pl.ds(0, 15), same], ssem.at[7])
        wait_bytes(fin.at[core, :, same], ssem.at[8])

    @pl.when(odd == 0)
    def _():
        rest(3, 0, for_odd, rsem.at[4])
        wait_bytes(half.at[pl.ds(0, 15), pl.ds(0, 3)], ssem.at[4])
        wait_bytes(half.at[:, pl.ds(0, 2)], ssem.at[5])

    @pl.when(odd == 1)
    def _():
        rest(2, 3, for_even, rsem.at[5])
        wait_bytes(half.at[:, pl.ds(0, 3)], ssem.at[4])
        wait_bytes(half.at[pl.ds(0, 15), pl.ds(0, 2)], ssem.at[5])

    def assemble(which):
        for i, j0, j1 in halves[which]:
            for j in range(j0, j1):
                b = i * (i + 1) // 2 + j - 5 * which
                tiles = [fin[which, r // UNITS, r % UNITS] for r in range(16 * b, 16 * b + 16)]
                block = jnp.concatenate(tiles, axis=0)
                g_ref[128 * i:128 * i + 128, 128 * j:128 * j + 128] = block
                if j < i:
                    g_ref[128 * j:128 * j + 128, 128 * i:128 * i + 128] = block.T

    for c in range(2):
        @pl.when(core == c)
        def _(c=c):
            assemble(c)
            wait_bytes(fin.at[1 - c], rsem.at[9])
            assemble(1 - c)

    wait_bytes(send.at[pl.ds(0, 15)], ssem.at[0])
    wait_bytes(send.at[pl.ds(0, 15)], ssem.at[1])

    @pl.when(is_short)
    def _():
        wait_bytes(send.at[pl.ds(0, 12)], ssem.at[2])

    @pl.when(jnp.logical_not(is_short))
    def _():
        wait_bytes(send.at[pl.ds(0, 11)], ssem.at[2])

    swap.wait_send()
    wait_bytes(fin.at[core], ssem.at[9])


RANK = 112
TILES = RANK // 8
PIECES = [(p, q, half) for p, q in ((0, 0), (0, 1), (1, 0), (0, 2), (2, 0), (1, 1)) for half in range(2)]


def spread_out(v):
    return jnp.broadcast_to(v, (8, 128))


def column(tile, k):
    return spread_out(tile[:, k:k + 1])


def row_of(ref, index, i):
    return spread_out(ref[index, i:i + 1, :])


NEAR = 3


def inverse_factor(a, work, beside):
    sub = lax.broadcasted_iota(jnp.int32, (8, 128), 0)
    lane = lax.broadcasted_iota(jnp.int32, (8, 128), 1)
    tiles = [a[8 * t:8 * t + 8, :] for t in range(TILES)]
    result = []
    ahead = None
    for t0 in range(TILES):
        k0 = 8 * t0
        base = (t0 % 2) * 18
        in_block = (lane >= k0) & (lane < k0 + 8)
        work[base] = jnp.where(in_block, (lane == sub + k0).astype(F32), tiles[t0])
        row = [row_of(work, base, i) for i in range(8)]
        for j in range(8):
            work[base + 2 + j] = column(tiles[t0], k0 + j) if ahead is None else ahead[j]
        s = [[row_of(work, base + 2 + j, i) for j in range(i + 1)] for i in range(8)]
        near = range(t0 + 1, min(TILES, t0 + 1 + NEAR))
        far = range(min(TILES, t0 + 1 + NEAR), TILES)
        col = {t: [column(tiles[t], k0 + j) for j in range(8)] for t in near}
        ahead = [column(tiles[t0 + 1], k0 + 8 + j) for j in range(8)] if near else None
        for t in near:
            tiles[t] = jnp.where(in_block, 0.0, tiles[t])
        beside(t0)
        factors, inverses = [], []
        for j in range(8):
            inv = 1.0 / s[j][j]
            m = [None] * 8
            for i in range(j + 1, 8):
                m[i] = s[i][j] * inv
            factors.append(m)
            inverses.append(inv)
            for i in range(j + 1, 8):
                for n in range(j + 1, i + 1):
                    s[i][n] = s[i][n] - m[i] * s[n][j]
            for i in range(j + 1, 8):
                row[i] = row[i] - m[i] * row[j]
            if near:
                work[base + 10 + j] = col[t0 + 1][j]
                next_row = [row_of(work, base + 10 + j, i) for i in range(8)]
            for t in near:
                x = col[t][j] * inv
                for n in range(j + 1, 8):
                    col[t][n] = col[t][n] - x * s[n][j]
                if t == t0 + 1:
                    ahead = [ahead[n] - x * next_row[n] for n in range(8)]
                tiles[t] = tiles[t] - x * row[j]
        tile, pivots = row[7], s[7][7]
        for i in range(7):
            tile = jnp.where(sub == i, row[i], tile)
            pivots = jnp.where(sub == i, s[i][i], pivots)
        result.append(jnp.where(lane < k0 + 8, tile * lax.rsqrt(pivots), 0.0))
        if far:
            back = [None] * 8
            for j in reversed(range(8)):
                u = row[j] * inverses[j]
                for i in range(j + 1, 8):
                    u = u - factors[j][i] * back[i]
                back[j] = u
            for t in far:
                u = jnp.where(in_block, 0.0, tiles[t])
                for j in range(8):
                    u = u - column(tiles[t], k0 + j) * back[j]
                tiles[t] = u
    return jnp.concatenate(result, axis=0)


def split3(v):
    hi = v.astype(BF16)
    rest = v - hi.astype(F32)
    mid = rest.astype(BF16)
    return hi, mid, (rest - mid.astype(F32)).astype(BF16)


def dot_p(a, b):
    return lax.dot_general(a, b, (((1,), (0,)), ((), ())), preferred_element_type=F32)


def long_product(a, b):
    hi, mid, lo = a
    b_hi, b_mid, b_lo = b
    return dot_p(
        jnp.concatenate([hi, mid, hi, lo, hi, mid], axis=1),
        jnp.concatenate([b_hi, b_hi, b_mid, b_hi, b_lo, b_mid], axis=0),
    )


def turns_part(g_ref, s_ref, hi_ref, lo_ref, st_ref, got, image, last, ahead, ahead_parts, inverse, parts, work, core_ref,
               ssem, rsem):
    z, x, y, core = place()

    for p, part in enumerate(split3(g_ref[...])):
        parts[p] = part
    image[...] = long_product(split3(s_ref[...]), (parts[0], parts[1], parts[2]))
    zeros = jnp.zeros((16, 512), BF16)
    for p in range(3):
        ahead_parts[p, RANK:] = zeros

    def turn(index, carry):
        now = image[...]
        last[...] = now
        hi, mid, lo = now = split3(now)
        pair = jnp.concatenate([hi, zeros, mid, zeros], axis=0)
        both = dot_t(pair, pair)
        small = dot_t(lo, jnp.concatenate([hi, zeros], axis=0)) + dot_t(hi, jnp.concatenate([lo, zeros], axis=0))
        cross = both[:RANK, 128:] + both[128:128 + RANK, :128]
        inner = both[:RANK, :128] + (cross + (small + both[128:128 + RANK, 128:]))

        def beside(t):
            if t < len(PIECES):
                p, q, half = PIECES[t]
                lanes = slice(256 * half, 256 * half + 256)
                piece = dot_p(now[p], parts[q, :, lanes])
                ahead[:, lanes] = piece if p + q == 0 else ahead[:, lanes] + piece
            elif t == len(PIECES):
                for p, part in enumerate(split3(ahead[...])):
                    ahead_parts[p, :RANK] = part

        w = inverse_factor(inner, work, beside)
        inverse[...] = w
        image[...] = long_product(split3(w), (ahead_parts[0], ahead_parts[1], ahead_parts[2]))
        return carry

    lax.fori_loop(0, ITERS, turn, 0)
    padded = tuple(jnp.concatenate([v, zeros], axis=0) for v in split3(last[...]))
    basis = long_product(split3(inverse[...]), padded)
    basis_hi, basis_lo = split(basis)

    def project(slot):
        lanes = slice(128 * slot, 128 * slot + 128)
        field_hi, field_lo = hi_ref[:, lanes], lo_ref[:, lanes]
        part = dot_p(
            jnp.concatenate([basis_hi, basis_hi, basis_lo], axis=1),
            jnp.concatenate([field_hi, field_lo, field_hi], axis=0),
        )
        for d in range(Z):
            core_ref[d, slot] = part[7 * d:7 * d + 7, :]

    first = first_group(z, core)
    is_short = short(z, core)

    def push(slot, n):
        def one(step, carry):
            d = partner(z, step)
            pltpu.make_async_remote_copy(
                src_ref=core_ref.at[d, pl.ds(slot, n)], dst_ref=got.at[pl.ds(first + slot, n)],
                send_sem=ssem, recv_sem=rsem, device_id={"gx": d}, device_id_type=MESH).start()
            return carry

        lax.fori_loop(0, 15, one, 0)

    def finish(n):
        push(1, n - 1)
        got[pl.ds(first, n)] = core_ref[z, pl.ds(0, n)]
        st_ref[...] = basis
        wait_bytes(got.at[pl.ds(0, GROUPS - n)], rsem)
        wait_bytes(core_ref.at[pl.ds(0, 15), pl.ds(0, n)], ssem)

    project(0)
    push(0, 1)
    project(1)
    project(2)

    @pl.when(is_short)
    def _():
        finish(2)

    @pl.when(jnp.logical_not(is_short))
    def _():
        finish(3)


def step_kernel(total, x_hbm, s_hbm, st_ref, got, s_ref, s_sem, *scratch):
    g_ref, hi_ref, lo_ref = scratch[1], scratch[4], scratch[5]
    load = pltpu.make_async_copy(s_hbm, s_ref, s_sem)
    load.start()
    gram_part(total, x_hbm, *scratch[:19])
    load.wait()
    turns_part(g_ref, s_ref, hi_ref, lo_ref, st_ref, got, *scratch[19:])


def step(x, s, total):
    vm = pl.BlockSpec(memory_space=pltpu.VMEM)
    return pl.pallas_call(
        functools.partial(step_kernel, total),
        out_shape=(jax.ShapeDtypeStruct((RANK, 512), F32), jax.ShapeDtypeStruct((GROUPS, 7, 128), F32)),
        in_specs=[pl.BlockSpec(memory_space=pl.ANY)] * 2,
        out_specs=(vm, vm),
        scratch_shapes=[
            pltpu.VMEM((RANK, 512), F32),
            pltpu.SemaphoreType.DMA,
            pltpu.VMEM((11, 128, 128), F32),
            pltpu.VMEM((512, 512), F32),
            pltpu.VMEM((GROUPS, 32, 128), F32),
            pltpu.VMEM((SLOTS, 512, 128), F32),
            pltpu.VMEM((512, 384), BF16),
            pltpu.VMEM((512, 384), BF16),
            pltpu.VMEM((1280, 128), F32),
            pltpu.VMEM((640, 128), F32),
            pltpu.VMEM((CHIPS, UNITS, 8, 128), F32),
            pltpu.VMEM((2 * CHIPS, 3, 8, 128), F32),
            pltpu.VMEM((3, 8, 128), F32),
            pltpu.VMEM((Z // 2, 3, 8, 128), F32),
            pltpu.VMEM((3, 8, 128), F32),
            pltpu.VMEM((2, CHIPS, UNITS, 8, 128), F32),
            pltpu.SemaphoreType.DMA((10,)),
            pltpu.SemaphoreType.DMA((10,)),
            pltpu.SemaphoreType.DMA,
            pltpu.SemaphoreType.REGULAR,
            pltpu.SemaphoreType.REGULAR,
            pltpu.VMEM((RANK, 512), F32),
            pltpu.VMEM((RANK, 512), F32),
            pltpu.VMEM((RANK, 512), F32),
            pltpu.VMEM((3, 128, 512), BF16),
            pltpu.VMEM((RANK, 128), F32),
            pltpu.VMEM((3, 512, 512), BF16),
            pltpu.VMEM((36, 8, 128), F32),
            pltpu.VMEM((Z, SLOTS, 7, 128), F32),
            pltpu.SemaphoreType.DMA,
            pltpu.SemaphoreType.DMA,
        ],
        compiler_params=pltpu.CompilerParams(
            collective_id=0, has_side_effects=True, vmem_limit_bytes=(64 * 1024 - 10816) * 1024),
    )(x, s)


def unpack_kernel(st_ref, got_ref, st_out, core_out):
    st_out[...] = st_ref[...]
    for e in range(7):
        for s in range(11):
            core_out[e, s] = got_ref[4 * s:4 * s + 4, e, :]


def unpack(st, got):
    vm = pl.BlockSpec(memory_space=pltpu.VMEM)
    return pl.pallas_call(
        unpack_kernel,
        out_shape=(jax.ShapeDtypeStruct((RANK, 512), F32), jax.ShapeDtypeStruct((7, 11, 4, 128), F32)),
        in_specs=[vm, vm],
        out_specs=(vm, vm),
        compiler_params=pltpu.CompilerParams(vmem_limit_bytes=4 * 1024 * 1024),
    )(st, got)


def per_device(species_field, start_basis):
    total = float(11 * 16 * 1024)
    st, core = unpack(*step(species_field.reshape(11, 128, 128), start_basis.T, total))
    return (st.T, core)


def solution(mesh):
    placed = (P(None, "gx", "gy", "gz"), P())
    return jax.shard_map(
        per_device,
        mesh=mesh,
        in_specs=placed,
        out_specs=(P(), P("gx", None, "gy", "gz")),
        check_vma=False,
    )
```
